32 devices in a mesh: dp: 4 (over y, core), ctx: 8 (over z, x).
Axes of the slice: x: 2, y: 2, z: 4, core: 2. Of those that a mesh axis runs over, the one named last changes fastest.
Arguments:
- tokens: bfloat16 [16, 2048, 1024], P('dp', 'ctx'), may hold values from -6 to 6
- cotangent: bfloat16 [16, 2048, 1024], P('dp', 'ctx'), may hold values from -6 to 6
- segments: int32 [16, 2048], P('dp', 'ctx'), may hold values from 0 to 3, as said below
- w_in: float32 [1024, 4384], P(('dp', 'ctx')), may hold values from -0.1875 to 0.1875
- w_out: float32 [2048, 1024], P(('dp', 'ctx')), may hold values from -0.125 to 0.125
- conv: float32 [2304, 5], P(('dp', 'ctx')), may hold values from -3 to 3
- gains: float32 [3072], P(('dp', 'ctx')), may hold values from 0.25 to 1.75
- heads: float32 [3, 32], replicated, may hold values from -9 to 3, as said below
- in_first: float32 [1024, 4384], P(('dp', 'ctx'))
- in_second: float32 [1024, 4384], P(('dp', 'ctx')), may hold values from 147 to 595
- out_first: float32 [2048, 1024], P(('dp', 'ctx'))
- out_second: float32 [2048, 1024], P(('dp', 'ctx')), may hold values from 1638 to 6553
- conv_first: float32 [2304, 5], P(('dp', 'ctx'))
- conv_second: float32 [2304, 5], P(('dp', 'ctx')), may hold values from 147 to 595
- gain_first: float32 [3072], P(('dp', 'ctx'))
- gain_second: float32 [3072], P(('dp', 'ctx')), may hold values from 595 to 2340
- head_first: float32 [3, 32], replicated
- head_second: float32 [3, 32], replicated, may hold values from 9362 to 37449
Outputs:
- output: bfloat16 [16, 2048, 1024], P('dp', 'ctx')
- grad_tokens: float32 [16, 2048, 1024], P('dp', 'ctx')
- in_first_new: float32 [1024, 4384], P(('dp', 'ctx'))
- in_second_new: float32 [1024, 4384], P(('dp', 'ctx'))
- in_weight_new: float32 [1024, 4384], P(('dp', 'ctx'))
- out_first_new: float32 [2048, 1024], P(('dp', 'ctx'))
- out_second_new: float32 [2048, 1024], P(('dp', 'ctx'))
- out_weight_new: float32 [2048, 1024], P(('dp', 'ctx'))
- conv_first_new: float32 [2304, 5], P(('dp', 'ctx'))
- conv_second_new: float32 [2304, 5], P(('dp', 'ctx'))
- conv_weight_new: float32 [2304, 5], P(('dp', 'ctx'))
- gain_first_new: float32 [3072], P(('dp', 'ctx'))
- gain_second_new: float32 [3072], P(('dp', 'ctx'))
- gain_vector_new: float32 [3072], P(('dp', 'ctx'))
- head_first_new: float32 [3, 32], replicated
- head_second_new: float32 [3, 32], replicated
- head_params_new: float32 [3, 32], replicated
The draws below stay inside these ranges and needn't reach their ends.
Inputs may be any that keep to these rules, and one draw needn't show every extreme that they name: `segments`: each row starts at 0, never falls and rises by one at exactly three tokens or never; among the 4 rows of one index of dp, one holds a single document. `heads`: row 0 holds the logarithms of the decay rates, row 1 the skip gains, row 2 the step biases.
All inputs are finite; a program needn't handle non-finite values.
Results may differ from the reference program's by a relative error of at most 0.004.
The reference program's roundings to bfloat16 on the way count: a program that leaves them out, or rounds other values in their place, can miss the bound.
Values may be sent and summed in bfloat16 or wider, within the bound.
No kernel may reach another device: no remote copies, remote signals or barrier semaphores. Data moves between devices by JAX's collectives and lax.ppermute only.
A program may use at most 256 MiB of HBM per device.

```python
import math
import jax
import jax.numpy as jnp
from jax import lax

D = 1024
INNER = 2048
HEADS = 32
HEAD_DIM = 64
STATE = 128
KERNEL = 4
BLOCK = 256
SEQ_DEV = 4
STEP = 10
LENGTH = 2048
BATCH = 16
TOKENS = 32768
PROJ = 4384
CHAN = 2304
GAINS = 3072


def moment_like(key, shape, size_factor):
    return size_factor * math.sqrt(TOKENS) * jax.random.normal(key, shape, jnp.float32)


def draw_segments(key, part):
    key = jax.random.fold_in(key, 7)
    place_key, whole_key = jax.random.split(key)
    row_keys = jax.random.split(place_key, BATCH)
    cut_points = jax.vmap(lambda row_key: jax.random.permutation(row_key, LENGTH - 1)[:3] + 1)(row_keys).astype(jnp.int32)
    positions = jnp.arange(LENGTH, dtype=jnp.int32)
    starts = jnp.sum((positions[None, :, None] == cut_points[:, None, :]).astype(jnp.int32), axis=2)
    whole_row = jax.random.randint(whole_key, (BATCH // SEQ_DEV,), 0, SEQ_DEV)
    row_index = jnp.arange(BATCH, dtype=jnp.int32)
    keep_rows = (row_index % SEQ_DEV != jnp.repeat(whole_row, SEQ_DEV)).astype(jnp.int32)
    starts = starts * keep_rows[:, None]
    return jnp.cumsum(starts, axis=1).astype(jnp.int32)


def draw_heads(key, part):
    key = jax.random.fold_in(key, 5)
    pick_key, jitter_key, bias_key, skip_key = jax.random.split(key, 4)
    fast_share = 0.5
    fast_mask = (jax.random.uniform(pick_key, (HEADS,), jnp.float32) < fast_share).astype(jnp.float32)
    jitter = jax.random.uniform(jitter_key, (HEADS,), jnp.float32, 0.5, 2.0)
    bias_shift = jax.random.uniform(bias_key, (HEADS,), jnp.float32, -0.5, 0.5)
    fast_rate = jitter / 40.0
    slow_rate = 0.8 * jitter / LENGTH
    step_bias = fast_mask * -1.0 + (1.0 - fast_mask) * -4.0 + bias_shift
    mean_step = fast_mask * 0.55 + (1.0 - fast_mask) * 0.03
    log_rate = jnp.log((fast_mask * fast_rate + (1.0 - fast_mask) * slow_rate) / mean_step)
    skip_gain = jax.random.uniform(skip_key, (HEADS,), jnp.float32, 1.0, 3.0)
    return jnp.stack([log_rate, skip_gain, step_bias])


def draw_in_first(key, part):
    key = jax.random.fold_in(key, 21)
    return moment_like(key, (D, PROJ), 0.033)


def draw_out_first(key, part):
    key = jax.random.fold_in(key, 22)
    return moment_like(key, (INNER, D), 0.11)


def draw_conv_first(key, part):
    key = jax.random.fold_in(key, 23)
    return moment_like(key, (CHAN, KERNEL + 1), 0.033)


def draw_gain_first(key, part):
    key = jax.random.fold_in(key, 24)
    return moment_like(key, (GAINS,), 0.066)


def draw_head_first(key, part):
    key = jax.random.fold_in(key, 25)
    return moment_like(key, (3, HEADS), 0.26)


def levels(key, extent, cuts, smallest, high):
    factor_of = 1.0
    for dim, parts in cuts:
        heights = jax.random.uniform(jax.random.fold_in(jax.random.fold_in(key, 6), dim), (parts,), jnp.float32, smallest / len(cuts), high / len(cuts))
        factor_of = factor_of * jnp.repeat(jnp.exp(heights), extent[dim] // parts).reshape((-1,) + (1,) * (len(extent) - 1 - dim))
    return factor_of


def centred(own_key, dims, deviation, bound, cuts=(), held_as=jnp.bfloat16):
    factor_of = levels(own_key, dims, cuts, -0.22, 0.18) if cuts else 1.0
    drawn = jax.random.normal(own_key, dims, jnp.float32) * deviation * factor_of
    return jnp.minimum(jnp.maximum(drawn, -bound), bound).astype(held_as)


def setup_inputs(seed: int = 0) -> dict:
    seeds = jax.random.split(jax.random.key(seed), 19)
    return {
        "tokens": centred(seeds[0], (BATCH, LENGTH, D), 1.0, 6.0, ((0, 4), (1, 8))),
        "cotangent": centred(seeds[1], (BATCH, LENGTH, D), 1.0, 6.0, ((0, 4), (1, 8))),
        "segments": draw_segments(jax.random.fold_in(seeds[18], 71), 0),
        "w_in": centred(seeds[3], (D, PROJ), D ** -0.5, 0.1875, ((0, 32),), jnp.float32),
        "w_out": centred(seeds[4], (INNER, D), INNER ** -0.5, 0.125, ((0, 32),), jnp.float32),
        "conv": centred(seeds[5], (CHAN, KERNEL + 1), KERNEL ** -0.5, 3.0, ((0, 32),), jnp.float32),
        "gains": jnp.clip(1.0 + 0.15 * jax.random.normal(seeds[6], (GAINS,), jnp.float32), 0.25, 1.75),
        "heads": draw_heads(jax.random.fold_in(seeds[18], 71), 0),
        "in_first": draw_in_first(jax.random.fold_in(seeds[18], 71), 0),
        "in_second": jnp.clip(jnp.exp(math.log(595.0) - 1.39812882 * jax.random.uniform(seeds[9], (D, PROJ), jnp.float32) ** levels(seeds[9], (D, PROJ), ((0, 32),), -0.2, 0.2)), 147.0, 595.0),
        "out_first": draw_out_first(jax.random.fold_in(seeds[18], 71), 0),
        "out_second": jnp.clip(jnp.exp(math.log(6553.0) - 1.386447 * jax.random.uniform(seeds[11], (INNER, D), jnp.float32) ** levels(seeds[11], (INNER, D), ((0, 32),), -0.2, 0.2)), 1638.0, 6553.0),
        "conv_first": draw_conv_first(jax.random.fold_in(seeds[18], 71), 0),
        "conv_second": jnp.clip(jnp.exp(math.log(595.0) - 1.39812882 * jax.random.uniform(seeds[13], (CHAN, KERNEL + 1), jnp.float32) ** levels(seeds[13], (CHAN, KERNEL + 1), ((0, 32),), -0.2, 0.2)), 147.0, 595.0),
        "gain_first": draw_gain_first(jax.random.fold_in(seeds[18], 71), 0),
        "gain_second": jnp.clip(jnp.exp(math.log(2340.0) - 1.3693448 * jax.random.uniform(seeds[15], (GAINS,), jnp.float32) ** levels(seeds[15], (GAINS,), ((0, 32),), -0.2, 0.2)), 595.0, 2340.0),
        "head_first": draw_head_first(jax.random.fold_in(seeds[18], 71), 0),
        "head_second": jnp.clip(jnp.exp(jax.random.uniform(seeds[17], (3, HEADS), jnp.float32, math.log(9362.0), math.log(37449.0))), 9362.0, 37449.0),
    }


EPSILON = 1e-05
BETA_ONE = 0.9
BETA_TWO = 0.95
ADAM_EPS = 1e-08
DECAY_RATE = 0.1
RATE_IN = 0.03
RATE_OUT = 0.02
RATE_CONV = 0.3
RATE_GAIN = 0.2
RATE_HEAD = 0.5
HIGHEST = lax.Precision.HIGHEST

@jax.custom_vjp
def low(v):
    return lax.optimization_barrier(v.astype(jnp.bfloat16)).astype(jnp.float32)

@jax.custom_vjp
def low_back(v):
    return v

def low_keep(v):
    return (low(v), None)

def low_pass(kept, grad):
    return (grad,)

def back_keep(v):
    return (v, None)

def back_low(kept, grad):
    return (low(grad),)
low.defvjp(low_keep, low_pass)
low_back.defvjp(back_keep, back_low)

def matmul(left, right):
    return jnp.dot(left, right, precision=HIGHEST)

def inverse_rms(values):
    return lax.rsqrt(lax.optimization_barrier(jnp.mean(values * values, axis=-1, keepdims=True)) + EPSILON)

def convolve(conv_in, segment, conv_weight):
    length = conv_in.shape[0]
    padded = jnp.concatenate([jnp.zeros((KERNEL - 1, conv_in.shape[1]), jnp.float32), conv_in], 0)
    seg_pad = jnp.concatenate([jnp.full((KERNEL - 1,), -1, jnp.int32), segment.astype(jnp.int32)], 0)
    summed = jnp.broadcast_to(conv_weight[:, KERNEL], conv_in.shape)
    for offset in range(KERNEL):
        same_doc = (seg_pad[offset:offset + length] == segment).astype(jnp.float32)
        summed = summed + conv_weight[:, offset] * padded[offset:offset + length] * same_doc[:, None]
    return summed

def block_parts(x_heads, b_state, c_state, step_size, segment, seg_before, head_rate, skip_gain):
    decay_sum = jnp.cumsum(step_size * head_rate, axis=0)
    positions = jnp.arange(BLOCK)
    causal = (positions[:, None] >= positions[None, :]) & (segment[:, None] == segment[None, :])
    span_sums = decay_sum.T[:, :, None] - decay_sum.T[:, None, :]
    decay_mat = jnp.where(causal[None], jnp.exp(jnp.where(causal[None], span_sums, 0.0)), 0.0)
    scores = low_back(matmul(c_state, b_state.T))
    mixing = low(scores[None] * decay_mat * step_size.T[:, None, :])
    y_local = jnp.einsum('hts,shp->thp', mixing, x_heads, precision=HIGHEST) + skip_gain[:, None] * x_heads
    tail_doc = (segment == segment[BLOCK - 1]).astype(jnp.float32)
    end_weight = jnp.exp(decay_sum[BLOCK - 1][None, :] - decay_sum) * tail_doc[:, None] * step_size
    scaled = low(end_weight[:, :, None] * x_heads)
    local_state = low_back(jnp.einsum('shp,sn->hpn', scaled, b_state, precision=HIGHEST))
    link_doc = (segment == seg_before).astype(jnp.float32)
    entry_decay = jnp.exp(decay_sum) * link_doc[:, None]
    return (y_local, local_state, entry_decay)

def sequence_ssd(x_heads, b_state, c_state, step_size, segment, head_rate, skip_gain):
    blocks = x_heads.shape[0] // BLOCK
    x_blocks = x_heads.reshape(blocks, BLOCK, HEADS, HEAD_DIM)
    b_blocks = b_state.reshape(blocks, BLOCK, STATE)
    c_blocks = c_state.reshape(blocks, BLOCK, STATE)
    step_blocks = step_size.reshape(blocks, BLOCK, HEADS)
    seg_blocks = segment.reshape(blocks, BLOCK)
    seg_before = jnp.concatenate([jnp.full((1,), -1, jnp.int32), seg_blocks[:-1, BLOCK - 1].astype(jnp.int32)])
    local_fn = jax.checkpoint(lambda block_item: block_parts(*block_item, head_rate, skip_gain))
    y_local, local_state, entry_decay = lax.map(local_fn, (x_blocks, b_blocks, c_blocks, step_blocks, seg_blocks, seg_before))

    def carry_state(carried, block_item):
        local_piece, passing = block_item
        return (passing[:, None, None] * carried + local_piece, carried)
    start_state = jnp.zeros((HEADS, HEAD_DIM, STATE), jnp.float32)
    last_state, incoming = lax.scan(carry_state, start_state, (local_state, entry_decay[:, BLOCK - 1, :]))
    incoming_low = low(incoming)
    from_before = low_back(jnp.einsum('ktn,khpn->kthp', c_blocks, incoming_low, precision=HIGHEST))
    y_all = y_local + entry_decay[:, :, :, None] * from_before
    return y_all.reshape(-1, HEADS * HEAD_DIM)

def layer_row(row_x, row_seg, input_weight, output_weight, conv_weight, gain_vector, head_params):
    gain_in = gain_vector[:D]
    gain_out = gain_vector[D:]
    normalized_rows = low(row_x * inverse_rms(row_x) * gain_in)
    projected_rows = low_back(matmul(normalized_rows, input_weight))
    gate_raw = projected_rows[:, :INNER]
    conv_in = low(projected_rows[:, INNER:INNER + CHAN])
    step_raw = projected_rows[:, INNER + CHAN:]
    activated = low(jax.nn.silu(convolve(conv_in, row_seg, conv_weight)))
    x_heads = activated[:, :INNER].reshape(-1, HEADS, HEAD_DIM)
    b_state = activated[:, INNER:INNER + STATE]
    c_state = activated[:, INNER + STATE:]
    step_size = jax.nn.softplus(step_raw + head_params[2])
    head_rate = -jnp.exp(head_params[0])
    ssd_out = low_back(sequence_ssd(x_heads, b_state, c_state, step_size, row_seg, head_rate, head_params[1]))
    gated = ssd_out * jax.nn.silu(gate_raw)
    mixer_output = low(gated * inverse_rms(gated) * gain_out)
    return row_x + matmul(mixer_output, output_weight)

def adamw(weight, gradient, first_moment, second_moment, step_rate):
    first_new = BETA_ONE * first_moment + (1.0 - BETA_ONE) * gradient
    second_new = BETA_TWO * second_moment + (1.0 - BETA_TWO) * gradient * gradient
    corrected = first_new / (1.0 - BETA_ONE ** STEP)
    spread = jnp.sqrt(second_new / (1.0 - BETA_TWO ** STEP))
    weight_new = weight - step_rate * (corrected / (spread + ADAM_EPS) + DECAY_RATE * weight)
    return (first_new, second_new, weight_new)

def reference(tokens, cotangent, segments, w_in, w_out, conv, gains, heads, in_first, in_second, out_first, out_second, conv_first, conv_second, gain_first, gain_second, head_first, head_second):
    in_work = w_in.astype(jnp.bfloat16).astype(jnp.float32)
    out_work = w_out.astype(jnp.bfloat16).astype(jnp.float32)
    conv_work = conv.astype(jnp.bfloat16).astype(jnp.float32)
    gain_work = gains.astype(jnp.bfloat16).astype(jnp.float32)

    def forward(x_all, input_weight, output_weight, conv_weight, gain_vector, head_params):
        row_fn = jax.checkpoint(lambda row_item: layer_row(row_item[0], row_item[1], input_weight, output_weight, conv_weight, gain_vector, head_params))
        return lax.map(row_fn, (x_all, segments))
    output, pullback = jax.vjp(forward, tokens.astype(jnp.float32), in_work, out_work, conv_work, gain_work, heads)
    gradients = pullback(cotangent.astype(jnp.float32))
    in_new = adamw(w_in, gradients[1], in_first, in_second, RATE_IN)
    out_new = adamw(w_out, gradients[2], out_first, out_second, RATE_OUT)
    conv_new = adamw(conv, gradients[3], conv_first, conv_second, RATE_CONV)
    gain_new = adamw(gains, gradients[4], gain_first, gain_second, RATE_GAIN)
    head_new = adamw(heads, gradients[5], head_first, head_second, RATE_HEAD)
    return (output.astype(jnp.bfloat16), gradients[0], in_new[0], in_new[1], in_new[2], out_new[0], out_new[1], out_new[2], conv_new[0], conv_new[1], conv_new[2], gain_new[0], gain_new[1], gain_new[2], head_new[0], head_new[1], head_new[2])
```

```python
import jax
import jax.numpy as jnp
from jax import lax
from jax.sharding import PartitionSpec as P

STEP = 10


EPSILON = 1e-05
BETA_ONE = 0.9
BETA_TWO = 0.95
ADAM_EPS = 1e-08
DECAY_RATE = 0.1
RATE_IN = 0.03
RATE_OUT = 0.02
RATE_CONV = 0.3
RATE_GAIN = 0.2
RATE_HEAD = 0.5


def shifted(value, axis, steps):
    count = lax.axis_size(axis)
    first, last = (max(0, -steps), min(count, count - steps))
    return lax.ppermute(value, axis, [(source, source + steps) for source in range(first, last)])


def split_parts(values):
    high = values.astype(jnp.bfloat16)
    rest = values - high.astype(jnp.float32)
    middle = rest.astype(jnp.bfloat16)
    low = (rest - middle.astype(jnp.float32)).astype(jnp.bfloat16)
    return high, middle, low


def bit_count(axis):
    return lax.axis_size(axis).bit_length() - 1


def halve(values, axis, bit, dim, sent_type):
    mine = (lax.axis_index(axis) >> bit) & 1
    kept = lax.dynamic_index_in_dim(values, mine, dim, keepdims=False)
    away = lax.dynamic_index_in_dim(values, 1 - mine, dim, keepdims=False).astype(sent_type)
    count = lax.axis_size(axis)
    away = lax.ppermute(away, axis, [(place, place ^ (1 << bit)) for place in range(count)])
    return kept + away.astype(jnp.float32)


def sum_to_owner(values, y_first):
    dp_bits, ctx_bits = bit_count("dp"), bit_count("ctx")
    x_bits = dp_bits - 1
    names = [("dp", bit) for bit in reversed(range(dp_bits))]
    names += [("ctx", bit) for bit in reversed(range(ctx_bits))]
    rows = values.shape[0] >> len(names)
    values = values.reshape((2,) * len(names) + (rows, values.shape[1]))
    y_part = [("dp", bit) for bit in reversed(range(1, dp_bits))]
    x_part = [("ctx", bit) for bit in reversed(range(x_bits))]
    z_part = [("ctx", bit) for bit in reversed(range(x_bits, ctx_bits))]
    order = [("dp", 0)] + (y_part + x_part if y_first else x_part + y_part) + z_part
    for item in order:
        sent_type = jnp.float32 if item == ("dp", 0) else jnp.bfloat16
        values = halve(values, item[0], item[1], names.index(item), sent_type)
        names.remove(item)
    return values


def sum_small(values, shared):
    dp_bits, ctx_bits = bit_count("dp"), bit_count("ctx")
    names = [("dp", bit) for bit in reversed(range(dp_bits))]
    names += [("ctx", bit) for bit in reversed(range(ctx_bits))]
    values = values.reshape((2,) * len(names) + (values.shape[1],))
    for axis, bit in list(names):
        dim = names.index((axis, bit))
        mine = (lax.axis_index(axis) >> bit) & 1
        kept = lax.dynamic_index_in_dim(values, mine, dim, keepdims=False)
        away = lax.dynamic_index_in_dim(values, 1 - mine, dim, keepdims=False)
        count = lax.axis_size(axis)
        away = lax.ppermute(
            jnp.concatenate([away.reshape(-1), shared]),
            axis,
            [(place, place ^ (1 << bit)) for place in range(count)],
        )
        values = kept + away[: kept.size].reshape(kept.shape)
        shared = shared + away[kept.size :]
        names.remove((axis, bit))
    return values, shared


def inverse_rms(values):
    return lax.rsqrt(jnp.mean(values * values, axis=-1, keepdims=True) + EPSILON)


def silu_slope(values):
    sigmoid_val = jax.nn.sigmoid(values)
    return sigmoid_val * (1.0 + values * (1.0 - sigmoid_val))


def block_mixing(b_state, c_state, step_size, decay_sum, segment):
    length = segment.shape[0]
    positions = lax.iota(jnp.int32, length)
    causal = (positions[:, None] >= positions[None, :]) & (segment[:, None] == segment[None, :])
    span_sums = decay_sum.T[:, :, None] - decay_sum.T[:, None, :]
    decay_mat = jnp.where(causal[None], jnp.exp(jnp.where(causal[None], span_sums, 0.0)), 0.0)
    scores = jnp.dot(c_state, b_state.T, preferred_element_type=jnp.float32)
    mixing = scores[None] * decay_mat * step_size.T[:, None, :]
    return (scores, decay_mat, mixing)


def block_forward(block_item):
    x_heads, b_state, c_state, step_size, decay_sum, segment = block_item
    scores, decay_mat, mixing = block_mixing(b_state, c_state, step_size, decay_sum, segment)
    return jnp.einsum(
        "hts,shp->thp", mixing.astype(jnp.bfloat16), x_heads, preferred_element_type=jnp.float32
    )


def block_backward(block_item):
    x_heads, b_state, c_state, step_size, decay_sum, segment, grad_ssd = block_item
    scores, decay_mat, mixing = block_mixing(b_state, c_state, step_size, decay_sum, segment)
    grad_mixing = jnp.einsum("thp,shp->hts", grad_ssd, x_heads, preferred_element_type=jnp.float32)
    grad_x = jnp.einsum(
        "hts,thp->shp", mixing.astype(jnp.bfloat16), grad_ssd, preferred_element_type=jnp.float32
    )
    grad_scores = jnp.sum(grad_mixing * decay_mat * step_size.T[:, None, :], axis=0).astype(
        jnp.bfloat16
    )
    grad_step = jnp.sum(grad_mixing * scores[None] * decay_mat, axis=1).T
    spread_grad = grad_mixing * mixing
    grad_decay = (jnp.sum(spread_grad, axis=2) - jnp.sum(spread_grad, axis=1)).T
    grad_c = jnp.dot(grad_scores, b_state, preferred_element_type=jnp.float32)
    grad_b = jnp.dot(grad_scores.T, c_state, preferred_element_type=jnp.float32)
    return (grad_x, grad_b, grad_c, grad_step, grad_decay)


def adamw(weight, gradient, first_moment, second_moment, step_rate):
    first_new = BETA_ONE * first_moment + (1.0 - BETA_ONE) * gradient
    second_new = BETA_TWO * second_moment + (1.0 - BETA_TWO) * gradient * gradient
    corrected = first_new / (1.0 - BETA_ONE**STEP)
    spread = jnp.sqrt(second_new / (1.0 - BETA_TWO**STEP))
    weight_new = weight - step_rate * (corrected / (spread + ADAM_EPS) + DECAY_RATE * weight)
    return (first_new, second_new, weight_new)


def local(
    tokens,
    cotangent,
    segments,
    w_in,
    w_out,
    conv,
    gains,
    heads,
    in_first,
    in_second,
    out_first,
    out_second,
    conv_first,
    conv_second,
    gain_first,
    gain_second,
    head_first,
    head_second,
):
    inner_width = w_out.shape[0] * lax.axis_size(("dp", "ctx"))
    own_rows = w_in.shape[0]
    small = jnp.concatenate([conv.reshape(-1), gains])
    spare = -(w_in.shape[1] - inner_width) % 128
    small = jnp.pad(small, (0, own_rows * spare - small.shape[0])).reshape(own_rows, spare)
    first_send = jnp.concatenate([w_in[:, inner_width:], small], axis=1).astype(jnp.bfloat16)
    first_weights = lax.all_gather(first_send, ("dp", "ctx"), axis=0, tiled=True)
    second_send = jnp.concatenate(
        [w_in[:, :inner_width], w_out.reshape(own_rows, -1)], axis=1
    ).astype(jnp.bfloat16)
    first_weights, second_send = lax.optimization_barrier((first_weights, second_send))
    second_weights = lax.all_gather(second_send, ("dp", "ctx"), axis=0, tiled=True)
    gate_weight = second_weights[:, :inner_width]
    output_weight = second_weights[:, inner_width:].reshape(inner_width, -1)
    mixer_weight = first_weights[:, : w_in.shape[1] - inner_width]
    small = first_weights[:, w_in.shape[1] - inner_width :].reshape(-1, own_rows * spare)
    conv_weight = small[:, : conv.size].reshape(-1, conv.shape[1])
    gain_vector = small[:, conv.size : conv.size + gains.size].reshape(-1)
    seq_count, length, model_width = tokens.shape
    channels = conv_weight.shape[0]
    kernel_taps = conv_weight.shape[1] - 1
    state_dim = (channels - inner_width) // 2
    heads_count = heads.shape[1]
    head_dim = inner_width // heads_count
    input_float = tokens.astype(jnp.float32)
    gain_float = gain_vector.astype(jnp.float32)
    gain_in = gain_float[:model_width]
    gain_out = gain_float[model_width:]
    scale_in = inverse_rms(input_float)
    unit_in = input_float * scale_in
    normalized_rows = (unit_in * gain_in).astype(jnp.bfloat16)
    projected_rows = jnp.einsum(
        "aok,ku->aou", normalized_rows, mixer_weight, preferred_element_type=jnp.float32
    )
    conv_in = projected_rows[:, :, :channels].astype(jnp.bfloat16)
    step_raw = projected_rows[:, :, channels:]
    gate_raw = jnp.einsum(
        "aok,ku->aou", normalized_rows, gate_weight, preferred_element_type=jnp.float32
    )
    rim_x, rim_seg = shifted(
        (conv_in[:, length - kernel_taps + 1 :], segments[:, length - kernel_taps + 1 :]), "ctx", 1
    )
    wide_x = jnp.concatenate([rim_x, conv_in], axis=1)
    wide_seg = jnp.concatenate([rim_seg, segments], axis=1)
    conv_float = conv_weight.astype(jnp.float32)
    same_doc = [
        (wide_seg[:, offset : offset + length] == segments).astype(jnp.float32)[:, :, None]
        for offset in range(kernel_taps)
    ]
    pre_act = jnp.broadcast_to(conv_float[:, kernel_taps], (seq_count, length, channels))
    for offset in range(kernel_taps):
        pre_act = (
            pre_act + conv_float[:, offset] * wide_x[:, offset : offset + length] * same_doc[offset]
        )
    activated = jax.nn.silu(pre_act).astype(jnp.bfloat16)
    x_heads = activated[:, :, :inner_width].reshape(seq_count, length, heads_count, head_dim)
    b_state = activated[:, :, inner_width : inner_width + state_dim]
    c_state = activated[:, :, inner_width + state_dim :]
    step_size = jax.nn.softplus(step_raw + heads[2])
    head_rate = -jnp.exp(heads[0])
    decay_sum = jnp.cumsum(step_size * head_rate, axis=1)
    within_block = lax.map(
        block_forward, (x_heads, b_state, c_state, step_size, decay_sum, segments)
    )
    tail_doc = (segments == segments[:, length - 1 :]).astype(jnp.float32)[:, :, None]
    fall_off = jnp.exp(decay_sum[:, length - 1 :] - decay_sum) * tail_doc
    end_weight = fall_off * step_size
    scaled = (end_weight[..., None] * x_heads).astype(jnp.bfloat16)
    scaled = scaled.reshape(seq_count, length, inner_width)
    local_state = jnp.einsum("sln,slc->snc", b_state, scaled, preferred_element_type=jnp.float32)
    link_doc = (segments == rim_seg[:, kernel_taps - 2 :]).astype(jnp.float32)[:, :, None]
    entry_decay = jnp.exp(decay_sum) * link_doc
    passing = entry_decay[:, length - 1]

    ctx_count = lax.axis_size("ctx")
    groups = ctx_count // seq_count
    lanes = inner_width // groups

    def to_owners(states, extra):
        parts = list(split_parts(extra)) + [jnp.zeros_like(extra, jnp.bfloat16)] * 13
        packed = jnp.concatenate([states.astype(jnp.bfloat16), jnp.stack(parts, axis=1)], axis=1)
        packed = packed.reshape(seq_count, -1, groups, lanes).transpose(0, 2, 1, 3)
        packed = packed.reshape(ctx_count, -1, lanes)
        return lax.all_to_all(packed, "ctx", 0, 0, tiled=True)

    def to_blocks(states, extra):
        parts = list(split_parts(extra)) + [jnp.zeros_like(extra, jnp.bfloat16)] * 13
        packed = jnp.concatenate([states.astype(jnp.bfloat16), jnp.stack(parts, axis=1)], axis=1)
        packed = lax.all_to_all(packed, "ctx", 0, 0, tiled=True)
        packed = packed.reshape(seq_count, groups, -1, lanes).transpose(0, 2, 1, 3)
        return packed.reshape(seq_count, -1, inner_width)

    received = to_owners(local_state, jnp.repeat(passing, head_dim, axis=1))
    received = received.astype(jnp.float32)
    owner_passing = jnp.sum(received[:, state_dim : state_dim + 3], axis=1)
    carried = jnp.zeros_like(received[0, :state_dim])
    owner_incoming = []
    for block in range(ctx_count):
        owner_incoming.append(carried)
        carried = owner_passing[block] * carried + received[block, :state_dim]
    owner_incoming = jnp.stack(owner_incoming)
    incoming_low = to_blocks(owner_incoming, jnp.zeros_like(owner_passing))[:, :state_dim]
    from_before = jnp.einsum(
        "sln,snc->slc", c_state, incoming_low, preferred_element_type=jnp.float32
    ).reshape(seq_count, length, heads_count, head_dim)
    ssd_out = within_block + heads[1][:, None] * x_heads + entry_decay[..., None] * from_before
    ssd_flat = ssd_out.reshape(seq_count, length, inner_width)
    gate_silu = jax.nn.silu(gate_raw)
    gated = ssd_flat * gate_silu
    scale_out = inverse_rms(gated)
    unit_out = gated * scale_out
    mixer_output = (unit_out * gain_out).astype(jnp.bfloat16)
    output = (
        input_float
        + jnp.einsum("exp,pk->exk", mixer_output, output_weight, preferred_element_type=jnp.float32)
    ).astype(jnp.bfloat16)
    grad_out_weight = jnp.einsum(
        "gva,gvk->ak", mixer_output, cotangent, preferred_element_type=jnp.float32
    )
    grad_mixed = jnp.einsum(
        "pjy,hy->pjh", cotangent, output_weight, preferred_element_type=jnp.float32
    )
    grad_gain_out = jnp.sum(grad_mixed * unit_out, axis=(0, 1))
    grad_unit = grad_mixed * gain_out
    grad_gated = scale_out * (
        grad_unit - unit_out * jnp.mean(grad_unit * unit_out, axis=-1, keepdims=True)
    )
    grad_ssd = (
        (grad_gated * gate_silu)
        .astype(jnp.bfloat16)
        .reshape(seq_count, length, heads_count, head_dim)
    )
    grad_gate = grad_gated * ssd_flat * silu_slope(gate_raw)
    grad_skip = jnp.einsum("slhp,slhp->h", grad_ssd, x_heads, preferred_element_type=jnp.float32)
    grad_entry = jnp.sum(grad_ssd * from_before, axis=3)
    grad_before = (grad_ssd * entry_decay[..., None]).astype(jnp.bfloat16)
    grad_before = grad_before.reshape(seq_count, length, inner_width)
    grad_c_outer = jnp.einsum(
        "slc,snc->sln", grad_before, incoming_low, preferred_element_type=jnp.float32
    )
    grad_incoming = jnp.einsum(
        "sln,slc->snc", c_state, grad_before, preferred_element_type=jnp.float32
    )
    received = to_owners(grad_incoming, jnp.zeros((seq_count, inner_width), jnp.float32))
    received = received[:, :state_dim].astype(jnp.float32)
    carried = jnp.zeros_like(received[0])
    owner_leaving = []
    for block in reversed(range(ctx_count)):
        owner_leaving.append(carried)
        carried = owner_passing[block] * carried + received[block]
    owner_leaving = jnp.stack(owner_leaving[::-1])
    returned = to_blocks(owner_leaving, jnp.sum(owner_leaving * owner_incoming, axis=1))
    grad_local = returned[:, :state_dim]
    grad_passing = jnp.sum(
        returned[:, state_dim : state_dim + 3]
        .astype(jnp.float32)
        .reshape(seq_count, 3, heads_count, head_dim),
        axis=(1, 3),
    )
    grad_scaled = jnp.einsum(
        "snc,sln->slc", grad_local, b_state, preferred_element_type=jnp.float32
    ).reshape(seq_count, length, heads_count, head_dim)
    grad_b_state = jnp.einsum(
        "slc,snc->sln", scaled, grad_local, preferred_element_type=jnp.float32
    )
    grad_end = jnp.sum(grad_scaled * x_heads, axis=3)
    inner_x, inner_b, inner_c, inner_step, inner_decay = lax.map(
        block_backward, (x_heads, b_state, c_state, step_size, decay_sum, segments, grad_ssd)
    )
    spread_end = grad_end * end_weight
    grad_decay = inner_decay + grad_entry * entry_decay - spread_end
    grad_decay = grad_decay.at[:, length - 1].add(
        jnp.sum(spread_end, axis=1) + grad_passing * passing
    )
    grad_later = jnp.flip(jnp.cumsum(jnp.flip(grad_decay, 1), axis=1), 1)
    grad_step = inner_step + grad_end * fall_off + grad_later * head_rate
    grad_log_rate = jnp.sum(grad_later * step_size, axis=(0, 1)) * head_rate
    grad_step_raw = grad_step * jax.nn.sigmoid(step_raw + heads[2])
    grad_step_bias = jnp.sum(grad_step_raw, axis=(0, 1))
    grad_x = inner_x + heads[1][:, None] * grad_ssd + end_weight[..., None] * grad_scaled
    grad_act = jnp.concatenate(
        [
            grad_x.reshape(seq_count, length, inner_width),
            inner_b + grad_b_state,
            inner_c + grad_c_outer,
        ],
        axis=2,
    )
    grad_pre = grad_act * silu_slope(pre_act)
    grad_bias = jnp.sum(grad_pre, axis=(0, 1))
    grad_taps = []
    grad_wide = jnp.zeros((seq_count, length + kernel_taps - 1, channels), jnp.float32)
    for offset in range(kernel_taps):
        masked = grad_pre * same_doc[offset]
        grad_taps.append(jnp.sum(masked * wide_x[:, offset : offset + length], axis=(0, 1)))
        grad_wide = grad_wide + jnp.pad(
            masked * conv_float[:, offset], ((0, 0), (offset, kernel_taps - 1 - offset), (0, 0))
        )
    rim_back = shifted(grad_wide[:, : kernel_taps - 1].astype(jnp.bfloat16), "ctx", -1).astype(
        jnp.float32
    )
    grad_conv_in = grad_wide[:, kernel_taps - 1 :].at[:, length - kernel_taps + 1 :].add(rim_back)
    grad_gate = grad_gate.astype(jnp.bfloat16)
    grad_mixer = jnp.concatenate([grad_conv_in, grad_step_raw], axis=2).astype(jnp.bfloat16)
    grad_gate_weight = jnp.einsum(
        "nay,nag->yg", normalized_rows, grad_gate, preferred_element_type=jnp.float32
    )
    grad_mixer_weight = jnp.einsum(
        "nay,nag->yg", normalized_rows, grad_mixer, preferred_element_type=jnp.float32
    )
    grad_normed = jnp.einsum(
        "hou,qu->hoq", grad_gate, gate_weight, preferred_element_type=jnp.float32
    ) + jnp.einsum(
        "hou,qu->hoq", grad_mixer, mixer_weight, preferred_element_type=jnp.float32
    )
    grad_gain_in = jnp.sum(grad_normed * unit_in, axis=(0, 1))
    grad_unit_in = grad_normed * gain_in
    grad_tokens = cotangent.astype(jnp.float32) + scale_in * (
        grad_unit_in - unit_in * jnp.mean(grad_unit_in * unit_in, axis=-1, keepdims=True)
    )
    grad_conv = jnp.stack(grad_taps + [grad_bias], axis=1)
    grad_gains = jnp.concatenate([grad_gain_in, grad_gain_out])
    grad_heads = jnp.stack([grad_log_rate, grad_skip, grad_step_bias])
    devices = lax.axis_size(("dp", "ctx"))
    small_sum, head_grad = sum_small(
        jnp.concatenate(
            [grad_conv.reshape(devices, -1), grad_gains.reshape(devices, -1)], axis=1
        ),
        grad_heads.reshape(-1),
    )
    middle = grad_mixer_weight.shape[1] // 256 * 128
    gate_sum = sum_to_owner(grad_gate_weight, True)
    out_sum = sum_to_owner(grad_out_weight.reshape(devices * own_rows, -1), False)
    left_sum = sum_to_owner(grad_mixer_weight[:, :middle], True)
    right_sum = sum_to_owner(grad_mixer_weight[:, middle:], False)
    owned_grads = (
        jnp.concatenate([gate_sum, left_sum, right_sum], axis=1),
        out_sum.reshape(w_out.shape),
        small_sum[: conv.size].reshape(conv.shape),
        small_sum[conv.size :],
    )
    head_grad = head_grad.reshape(heads.shape)
    in_new = adamw(w_in, owned_grads[0], in_first, in_second, RATE_IN)
    out_new = adamw(w_out, owned_grads[1], out_first, out_second, RATE_OUT)
    conv_new = adamw(conv, owned_grads[2], conv_first, conv_second, RATE_CONV)
    gain_new = adamw(gains, owned_grads[3], gain_first, gain_second, RATE_GAIN)
    head_new = adamw(heads, head_grad, head_first, head_second, RATE_HEAD)
    return (
        output,
        grad_tokens,
        in_new[0],
        in_new[1],
        in_new[2],
        out_new[0],
        out_new[1],
        out_new[2],
        conv_new[0],
        conv_new[1],
        conv_new[2],
        gain_new[0],
        gain_new[1],
        gain_new[2],
        head_new[0],
        head_new[1],
        head_new[2],
    )


def solution(mesh):
    placed = (
        P("dp", "ctx", None),
        P("dp", "ctx", None),
        P("dp", "ctx"),
        P(("dp", "ctx"), None),
        P(("dp", "ctx"), None),
        P(("dp", "ctx"), None),
        P(("dp", "ctx")),
        P(),
        P(("dp", "ctx"), None),
        P(("dp", "ctx"), None),
        P(("dp", "ctx"), None),
        P(("dp", "ctx"), None),
        P(("dp", "ctx"), None),
        P(("dp", "ctx"), None),
        P(("dp", "ctx")),
        P(("dp", "ctx")),
        P(),
        P(),
    )
    return jax.shard_map(
        local,
        mesh=mesh,
        in_specs=placed,
        out_specs=(
            P("dp", "ctx", None),
            P("dp", "ctx", None),
            P(("dp", "ctx"), None),
            P(("dp", "ctx"), None),
            P(("dp", "ctx"), None),
            P(("dp", "ctx"), None),
            P(("dp", "ctx"), None),
            P(("dp", "ctx"), None),
            P(("dp", "ctx"), None),
            P(("dp", "ctx"), None),
            P(("dp", "ctx"), None),
            P(("dp", "ctx")),
            P(("dp", "ctx")),
            P(("dp", "ctx")),
            P(),
            P(),
            P(),
        ),
        check_vma=False,
    )
```

```python
import functools

import jax
import jax.numpy as jnp
from jax import lax
from jax.experimental import pallas as pl
from jax.experimental.pallas import tpu as pltpu
from jax.sharding import PartitionSpec as P

STEP = 10


EPSILON = 1e-05
BETA_ONE = 0.9
BETA_TWO = 0.95
ADAM_EPS = 1e-08
DECAY_RATE = 0.1
RATE_IN = 0.03
RATE_OUT = 0.02
RATE_CONV = 0.3
RATE_GAIN = 0.2
RATE_HEAD = 0.5
LOG2E = 1.4426950408889634
BELOW = -1e30
LANES = 128
VMEM_BYTES = 58 << 20
NT = (((1,), (1,)), ((), ()))
TN = (((0,), (0,)), ((), ()))


def shifted(value, axis, steps):
    count = lax.axis_size(axis)
    first, last = (max(0, -steps), min(count, count - steps))
    return lax.ppermute(value, axis, [(source, source + steps) for source in range(first, last)])


def bit_count(axis):
    return lax.axis_size(axis).bit_length() - 1


def halve(values, axis, bit, dim, sent_type):
    mine = (lax.axis_index(axis) >> bit) & 1
    kept = lax.dynamic_index_in_dim(values, mine, dim, keepdims=False)
    away = lax.dynamic_index_in_dim(values, 1 - mine, dim, keepdims=False).astype(sent_type)
    count = lax.axis_size(axis)
    away = lax.ppermute(away, axis, [(place, place ^ (1 << bit)) for place in range(count)])
    return kept + away.astype(jnp.float32)


def sum_to_owner(values, y_first):
    dp_bits, ctx_bits = bit_count("dp"), bit_count("ctx")
    x_bits = dp_bits - 1
    names = [("dp", bit) for bit in reversed(range(dp_bits))]
    names += [("ctx", bit) for bit in reversed(range(ctx_bits))]
    rows = values.shape[0] >> len(names)
    values = values.reshape((2,) * len(names) + (rows, values.shape[1]))
    y_part = [("dp", bit) for bit in reversed(range(1, dp_bits))]
    x_part = [("ctx", bit) for bit in reversed(range(x_bits))]
    z_part = [("ctx", bit) for bit in reversed(range(x_bits, ctx_bits))]
    order = [("dp", 0)] + (y_part + x_part if y_first else x_part + y_part) + z_part
    for item in order:
        sent_type = jnp.float32
        values = halve(values, item[0], item[1], names.index(item), sent_type)
        names.remove(item)
    return values


def sum_small(values, shared):
    dp_bits, ctx_bits = bit_count("dp"), bit_count("ctx")
    names = [("dp", bit) for bit in reversed(range(dp_bits))]
    names += [("ctx", bit) for bit in reversed(range(ctx_bits))]
    values = values.reshape((2,) * len(names) + (values.shape[1],))
    for axis, bit in list(names):
        dim = names.index((axis, bit))
        mine = (lax.axis_index(axis) >> bit) & 1
        kept = lax.dynamic_index_in_dim(values, mine, dim, keepdims=False)
        away = lax.dynamic_index_in_dim(values, 1 - mine, dim, keepdims=False)
        count = lax.axis_size(axis)
        away = lax.ppermute(
            jnp.concatenate([away.reshape(-1), shared]),
            axis,
            [(place, place ^ (1 << bit)) for place in range(count)],
        )
        values = kept + away[: kept.size].reshape(kept.shape)
        shared = shared + away[kept.size :]
        names.remove((axis, bit))
    return values, shared


def inverse_rms(values):
    return lax.rsqrt(jnp.mean(values * values, axis=-1, keepdims=True) + EPSILON)


def dot(left, right, dims=(((1,), (0,)), ((), ())), precision=None):
    return lax.dot_general(
        left, right, dims, precision=precision, preferred_element_type=jnp.float32
    )


def split_parts(values):
    high = values.astype(jnp.bfloat16)
    rest = values - high.astype(jnp.float32)
    middle = rest.astype(jnp.bfloat16)
    low = (rest - middle.astype(jnp.float32)).astype(jnp.bfloat16)
    return high, middle, low


def spread_heads(values, spread):
    high, middle, low = split_parts(values)
    return dot(high, spread) + dot(middle, spread) + dot(low, spread)


def sum_heads(values, spread):
    high, middle, low = split_parts(values)
    return dot(high, spread, NT) + dot(middle, spread, NT) + dot(low, spread, NT)


def causal(rows, columns):
    at_row = lax.broadcasted_iota(jnp.int32, (rows, columns), 0)
    at_column = lax.broadcasted_iota(jnp.int32, (rows, columns), 1)
    return at_row, at_column


def kernel_call(body, grid, in_specs, out_specs, out_shape, scratch=()):
    return pl.pallas_call(
        body,
        grid=grid,
        in_specs=in_specs,
        out_specs=out_specs,
        out_shape=out_shape,
        scratch_shapes=list(scratch),
        compiler_params=pltpu.CompilerParams(
            dimension_semantics=("arbitrary",) * len(grid), vmem_limit_bytes=VMEM_BYTES
        ),
    )


def per_row(*shape):
    return pl.BlockSpec((1,) + shape, lambda row, *_: (row,) + (0,) * len(shape))


def whole(*shape):
    return pl.BlockSpec(shape, lambda *_: (0,) * len(shape))


def shape_of(shape, dtype):
    return jax.ShapeDtypeStruct(shape, dtype)


def entry_kernel(
    heads_count,
    x_ref,
    rim_ref,
    marks_ref,
    weight_ref,
    gain_ref,
    conv_ref,
    heads_ref,
    spread_ref,
    normed_ref,
    wide_out_ref,
    act_ref,
    raw_ref,
    step_ref,
    decay_ref,
    send_ref,
    wide_ref,
):
    length = x_ref.shape[1]
    inner, channels = spread_ref.shape[1], act_ref.shape[2]
    state = (channels - inner) // 2
    gain = gain_ref[0:1]

    def normalize(values):
        values = values.astype(jnp.float32)
        scale = lax.rsqrt(jnp.mean(values * values, axis=-1, keepdims=True) + EPSILON)
        return (values * scale * gain).astype(jnp.bfloat16)

    normed = normalize(x_ref[0])
    normed_ref[0] = normed
    rim = dot(normalize(rim_ref[0]), weight_ref[:, :channels])
    wide_ref[0:8] = rim[8:16].astype(jnp.bfloat16).astype(jnp.float32)
    part = 768 if channels % 768 == 0 else LANES
    for start in range(0, channels, part):
        piece = dot(normed, weight_ref[:, start : start + part]).astype(jnp.bfloat16)
        wide_ref[8:, start : start + part] = piece.astype(jnp.float32)
    raw = dot(normed, weight_ref[:, channels:])
    raw_ref[0] = raw

    def convolve(tile, carry):
        at = pl.ds(pl.multiple_of(tile * LANES, LANES), LANES)
        pre = jnp.broadcast_to(conv_ref[4:5, at], (length, LANES))
        for tap in range(3):
            taken = wide_ref[5 + tap : 5 + tap + length, at]
            pre = pre + conv_ref[tap : tap + 1, at] * taken * marks_ref[0, :, tap : tap + 1]
        pre = pre + conv_ref[3:4, at] * wide_ref[8:, at]
        act_ref[0, :, at] = (pre * jax.nn.sigmoid(pre)).astype(jnp.bfloat16)
        wide_out_ref[0, :, at] = jnp.concatenate(
            [jnp.zeros((8, LANES), jnp.float32), wide_ref[:, at]], axis=0
        ).astype(jnp.bfloat16)
        return carry

    lax.fori_loop(0, channels // LANES, convolve, 0)

    biased = raw + heads_ref[0:1]
    step = jnp.maximum(biased, 0.0) + jnp.log1p(jnp.exp(-jnp.abs(biased)))
    lane = lax.broadcasted_iota(jnp.int32, step.shape, 1)
    step = jnp.where(lane < heads_count, step, 0.0)
    step_ref[0] = step
    at_row, at_column = causal(length, length)
    lower = jnp.where(at_row >= at_column, 1.0, 0.0)
    decay = dot(lower, step * heads_ref[1:2], precision=lax.Precision.HIGHEST)
    decay_ref[0] = decay
    last = decay[length - 1 : length]
    end_weight = jnp.exp(last - decay) * marks_ref[0, :, 4:5] * step
    spread = spread_ref[...]
    scaled = (spread_heads(end_weight, spread) * act_ref[0, :, :inner].astype(jnp.float32)).astype(
        jnp.bfloat16
    )
    states = dot(act_ref[0, :, inner : inner + state], scaled, TN)
    passing = jnp.exp(last) * marks_ref[0, length - 1 : length, 3:4]
    passing = spread_heads(jnp.broadcast_to(passing, (8, LANES)), spread)
    groups, lanes = send_ref.shape[1], send_ref.shape[3]
    for group in range(groups):
        at = slice(group * lanes, (group + 1) * lanes)
        send_ref[0, group, :state] = states[:, at]
        send_ref[0, group, state:] = passing[:, at]


def pair_masks(pair_lanes, head_dim, rows):
    lane = lax.broadcasted_iota(jnp.int32, (rows, pair_lanes), 1)
    return [
        (lane >= member * head_dim) & (lane < (member + 1) * head_dim)
        for member in range(pair_lanes // head_dim)
    ]


def inner_forward_kernel(
    heads_count, act_ref, step_ref, decay_ref, marks_ref, segment_ref, y_ref
):
    length = act_ref.shape[1]
    inner = y_ref.shape[2]
    state = (act_ref.shape[2] - inner) // 2
    head_dim = inner // heads_count
    b_state = act_ref[0, :, inner : inner + state]
    c_state = act_ref[0, :, inner + state :]
    decay = decay_ref[0] * LOG2E
    lifted = (decay - jnp.log2(step_ref[0])).T
    at_row, at_column = causal(length, length)
    joined = (at_row >= at_column) & (marks_ref[0, :, 5:6] == segment_ref[0, 0:1])
    masked = jnp.where(joined, 0.0, BELOW)
    scores = dot(c_state, b_state, NT)
    chunk = max(length // 2, 16)
    masks = pair_masks(LANES, head_dim, length)
    for pair in range(inner // LANES):
        at = slice(pair * LANES, (pair + 1) * LANES)
        x_pair = act_ref[0, :, at]
        members = [jnp.where(mask, x_pair, jnp.zeros_like(x_pair)) for mask in masks]
        for start in range(0, length, chunk):
            rows, seen = slice(start, start + chunk), start + chunk
            total = jnp.zeros((chunk, LANES), jnp.float32)
            for member, x_member in enumerate(members):
                head = pair * len(masks) + member
                span = decay[rows, head : head + 1] - lifted[head : head + 1, :seen]
                mixing = scores[rows, :seen] * jnp.exp2(span + masked[rows, :seen])
                total = total + dot(mixing.astype(jnp.bfloat16), x_member[:seen])
            y_ref[0, rows, at] = total


def carry_forward_kernel(received_ref, low_ref, incoming_ref):
    blocks, state = low_ref.shape[0], low_ref.shape[1]
    carried = jnp.zeros(low_ref.shape[1:], jnp.float32)
    for block in range(blocks):
        incoming_ref[block] = carried
        low_ref[block] = carried.astype(jnp.bfloat16)
        passing = received_ref[block, state : state + 1]
        carried = passing * carried + received_ref[block, :state].astype(jnp.float32)


def carry_backward_kernel(received_ref, passing_ref, incoming_ref, send_ref):
    blocks, state = received_ref.shape[0], received_ref.shape[1]
    carried = jnp.zeros(received_ref.shape[1:], jnp.float32)
    for block in reversed(range(blocks)):
        send_ref[block, :state] = carried.astype(jnp.bfloat16)
        total = jnp.sum(carried * incoming_ref[block], axis=0, keepdims=True)
        parts = [part.astype(jnp.float32) for part in split_parts(total)]
        parts.append(jnp.zeros((13,) + total.shape[1:], jnp.float32))
        send_ref[block, state:] = jnp.concatenate(parts, axis=0).astype(jnp.bfloat16)
        carried = passing_ref[block, 0:1] * carried + received_ref[block].astype(jnp.float32)


def join_groups(ref, rows):
    return jnp.concatenate([ref[0, group, rows] for group in range(ref.shape[1])], axis=1)


def middle_kernel(
    groups,
    cotangent_ref,
    normed_ref,
    gate_weight_ref,
    out_weight_ref,
    gain_ref,
    skip_ref,
    act_ref,
    y_ref,
    incoming_ref,
    decay_ref,
    marks_ref,
    spread_ref,
    mixed_ref,
    grad_gate_ref,
    grad_ssd_ref,
    send_ref,
    grad_c_ref,
    row_term_ref,
    grad_gain_ref,
    grad_skip_ref,
    total_ref,
):
    row, piece = pl.program_id(0), pl.program_id(1)
    inner = spread_ref.shape[1]
    state = total_ref.shape[0]
    spread = spread_ref[...]
    gain, skip = gain_ref[0:1], skip_ref[0:1]
    x_part = act_ref[0, :, :inner].astype(jnp.float32)
    c_state = act_ref[0, :, inner + state :]
    incoming = join_groups(incoming_ref, slice(None))
    entry = spread_heads(jnp.exp(decay_ref[0]) * marks_ref[0, :, 3:4], spread)
    inner_part = y_ref[0] + entry * dot(c_state, incoming)
    ssd = inner_part + skip * x_part
    gate = dot(normed_ref[0], gate_weight_ref[...])
    sigmoid = jax.nn.sigmoid(gate)
    silu = gate * sigmoid
    gated = ssd * silu
    scale = lax.rsqrt(jnp.mean(gated * gated, axis=-1, keepdims=True) + EPSILON)
    unit = gated * scale
    mixed_ref[0] = (unit * gain).astype(jnp.bfloat16)
    grad_mixed = dot(cotangent_ref[0], out_weight_ref[...], NT)
    grad_unit = grad_mixed * gain
    mean = jnp.mean(grad_unit * unit, axis=-1, keepdims=True)
    grad_gated = scale * (grad_unit - unit * mean)
    slope = sigmoid * (1.0 + gate * (1.0 - sigmoid))
    grad_gate_ref[0] = (grad_gated * ssd * slope).astype(jnp.bfloat16)
    grad_ssd = (grad_gated * silu).astype(jnp.bfloat16)
    grad_ssd_ref[0] = grad_ssd
    grad_ssd = grad_ssd.astype(jnp.float32)
    row_term_ref[0] = sum_heads(grad_ssd * inner_part, spread)
    grad_before = (grad_ssd * entry).astype(jnp.bfloat16)
    grad_c_ref[0] = dot(grad_before, incoming, NT)
    grad_states = dot(c_state, grad_before, TN)
    gain_sum = jnp.sum(grad_mixed * unit, axis=0, keepdims=True)
    skip_sum = jnp.sum(grad_ssd * x_part, axis=0, keepdims=True)

    @pl.when(piece == 0)
    def _():
        total_ref[...] = grad_states

    @pl.when(piece > 0)
    def _():
        total_ref[...] += grad_states

    @pl.when((piece == 0) & (row == 0))
    def _():
        grad_gain_ref[...] = jnp.zeros_like(grad_gain_ref)
        grad_skip_ref[...] = jnp.zeros_like(grad_skip_ref)

    grad_gain_ref[0:1] += gain_sum
    grad_skip_ref[0:1] += skip_sum
    lanes = inner // groups

    @pl.when(piece == pl.num_programs(1) - 1)
    def _():
        for group in range(groups):
            at = slice(group * lanes, (group + 1) * lanes)
            send_ref[0, group] = total_ref[:, at].astype(jnp.bfloat16)


def inner_backward_kernel(
    heads_count,
    act_ref,
    grad_ssd_ref,
    step_ref,
    decay_ref,
    marks_ref,
    segment_ref,
    grad_x_ref,
    grad_b_ref,
    grad_c_ref,
    total_ref,
):
    length = act_ref.shape[1]
    inner = grad_ssd_ref.shape[2]
    state = (act_ref.shape[2] - inner) // 2
    head_dim = inner // heads_count
    b_state = act_ref[0, :, inner : inner + state]
    c_state = act_ref[0, :, inner + state :]
    decay = decay_ref[0] * LOG2E
    lowered = jnp.log2(step_ref[0]) - decay
    decay = decay.T
    at_row, at_column = causal(length, length)
    joined = (at_row <= at_column) & (marks_ref[0, :, 5:6] == segment_ref[0, 0:1])
    masked = jnp.where(joined, 0.0, BELOW)
    scores = dot(b_state, c_state, NT)
    chunk = max(length // 2, 16)
    masks = pair_masks(LANES, head_dim, length)
    total_ref[...] = jnp.zeros_like(total_ref)
    for pair in range(inner // LANES):
        at = slice(pair * LANES, (pair + 1) * LANES)
        x_pair = act_ref[0, :, at]
        grad_pair = grad_ssd_ref[0, :, at]
        members = [jnp.where(mask, grad_pair, jnp.zeros_like(grad_pair)) for mask in masks]
        for start in range(0, length, chunk):
            rows, later = slice(start, start + chunk), slice(start, length)
            grad_x = jnp.zeros((chunk, LANES), jnp.float32)
            for member, grad_member in enumerate(members):
                head = pair * len(masks) + member
                span = decay[head : head + 1, later] + lowered[rows, head : head + 1]
                weight = jnp.exp2(span + masked[rows, later])
                mixing = (scores[rows, later] * weight).astype(jnp.bfloat16)
                grad_x = grad_x + dot(mixing, grad_member[later])
                total_ref[rows, later] += dot(x_pair[rows], grad_member[later], NT) * weight
            grad_x_ref[0, rows, at] = grad_x
    grad_scores = total_ref[...].astype(jnp.bfloat16)
    grad_b_ref[0] = dot(grad_scores, c_state)
    grad_c_ref[0] = dot(grad_scores, b_state, TN)


def exit_kernel(
    act_ref,
    wide_ref,
    grad_ssd_ref,
    inner_x_ref,
    inner_b_ref,
    inner_c_ref,
    outer_c_ref,
    leaving_ref,
    row_term_ref,
    raw_ref,
    step_ref,
    decay_ref,
    marks_ref,
    conv_ref,
    heads_ref,
    skip_ref,
    spread_ref,
    grad_mixer_ref,
    tail_ref,
    rim_ref,
    grad_conv_ref,
    grad_heads_ref,
    grad_act_ref,
    shift_ref,
    taken_ref,
):
    row = pl.program_id(0)
    length, channels = act_ref.shape[1], act_ref.shape[2]
    inner = spread_ref.shape[1]
    state = (channels - inner) // 2
    spread = spread_ref[...]
    step, decay = step_ref[0], decay_ref[0]
    b_state = act_ref[0, :, inner : inner + state]
    leaving = join_groups(leaving_ref, slice(0, state))
    x_part = act_ref[0, :, :inner].astype(jnp.float32)
    last = decay[length - 1 : length]
    end_weight = spread_heads(jnp.exp(last - decay) * marks_ref[0, :, 4:5] * step, spread)
    scaled = (end_weight * x_part).astype(jnp.bfloat16)
    end_part = end_weight * dot(b_state, leaving)
    grad_x = inner_x_ref[0] + end_part
    grad_act_ref[:, :inner] = grad_x + skip_ref[0:1] * grad_ssd_ref[0].astype(jnp.float32)
    grad_act_ref[:, inner : inner + state] = inner_b_ref[0] + dot(scaled, leaving, NT)
    grad_act_ref[:, inner + state :] = inner_c_ref[0] + outer_c_ref[0]
    column_term = sum_heads(x_part * grad_x, spread)
    passed = join_groups(leaving_ref, slice(state, state + 16)).astype(jnp.float32)
    passed = jnp.sum(passed, axis=0, keepdims=True)
    ended = jnp.sum(x_part * end_part, axis=0, keepdims=True)
    ends = sum_heads(jnp.concatenate([passed, ended, jnp.zeros((6, inner), jnp.float32)], 0), spread)
    passing = jnp.exp(last) * marks_ref[0, length - 1 : length, 3:4]
    final = ends[1:2] + ends[0:1] * passing
    at_row, at_column = causal(length, length)
    token = lax.broadcasted_iota(jnp.int32, step.shape, 0)
    grad_decay = row_term_ref[0] - column_term + jnp.where(token == length - 1, final, 0.0)
    upper = jnp.where(at_row <= at_column, 1.0, 0.0)
    grad_later = dot(upper, grad_decay, precision=lax.Precision.HIGHEST)
    rate = heads_ref[1:2]
    grad_step = jnp.where(step > 0.0, column_term / jnp.where(step > 0.0, step, 1.0), 0.0)
    grad_step = grad_step + rate * grad_later
    grad_raw = grad_step * jax.nn.sigmoid(raw_ref[0] + heads_ref[0:1])
    grad_raw = jnp.where(step > 0.0, grad_raw, 0.0)
    grad_mixer_ref[0, :, channels:] = grad_raw.astype(jnp.bfloat16)

    @pl.when(row == 0)
    def _():
        grad_conv_ref[...] = jnp.zeros_like(grad_conv_ref)
        grad_heads_ref[...] = jnp.zeros_like(grad_heads_ref)

    grad_heads_ref[0:1] += jnp.sum(grad_later * step, axis=0, keepdims=True) * rate
    grad_heads_ref[1:2] += jnp.sum(grad_raw, axis=0, keepdims=True)

    def convolve(tile, carry):
        at = pl.ds(pl.multiple_of(tile * LANES, LANES), LANES)
        taken_ref[...] = wide_ref[0, :, at].astype(jnp.float32)
        pre = jnp.broadcast_to(conv_ref[4:5, at], (length, LANES))
        for tap in range(3):
            taken = taken_ref[13 + tap : 13 + tap + length]
            pre = pre + conv_ref[tap : tap + 1, at] * taken * marks_ref[0, :, tap : tap + 1]
        pre = pre + conv_ref[3:4, at] * taken_ref[16:]
        sigmoid = jax.nn.sigmoid(pre)
        grad_pre = grad_act_ref[:, at] * (sigmoid * (1.0 + pre * (1.0 - sigmoid)))
        grad_conv_ref[4:5, at] += jnp.sum(grad_pre, axis=0, keepdims=True)
        grad_conv_ref[3:4, at] += jnp.sum(grad_pre * taken_ref[16:], axis=0, keepdims=True)
        grad_in = grad_pre * conv_ref[3:4, at]
        rim = jnp.zeros((8, LANES), jnp.float32)
        shift_ref[0:8] = jnp.zeros((8, LANES), jnp.float32)
        shift_ref[length + 8 :] = jnp.zeros((8, LANES), jnp.float32)
        for tap in range(3):
            masked = grad_pre * marks_ref[0, :, tap : tap + 1]
            taken = taken_ref[13 + tap : 13 + tap + length]
            grad_conv_ref[tap : tap + 1, at] += jnp.sum(masked * taken, axis=0, keepdims=True)
            shift_ref[8 : length + 8] = masked * conv_ref[tap : tap + 1, at]
            grad_in = grad_in + shift_ref[11 - tap : 11 - tap + length]
            rim = rim + shift_ref[8 - tap : 16 - tap]
        grad_mixer_ref[0, :, at] = grad_in.astype(jnp.bfloat16)
        tail_ref[0, :, at] = grad_in[length - 8 :]
        rim_ref[0, :, at] = rim
        return carry

    lax.fori_loop(0, channels // LANES, convolve, 0)


def adamw(weight, gradient, first_moment, second_moment, step_rate):
    first_new = BETA_ONE * first_moment + (1.0 - BETA_ONE) * gradient
    second_new = BETA_TWO * second_moment + (1.0 - BETA_TWO) * gradient * gradient
    corrected = first_new / (1.0 - BETA_ONE**STEP)
    spread = jnp.sqrt(second_new / (1.0 - BETA_TWO**STEP))
    weight_new = weight - step_rate * (corrected / (spread + ADAM_EPS) + DECAY_RATE * weight)
    return (first_new, second_new, weight_new)


def local(
    tokens,
    cotangent,
    segments,
    w_in,
    w_out,
    conv,
    gains,
    heads,
    in_first,
    in_second,
    out_first,
    out_second,
    conv_first,
    conv_second,
    gain_first,
    gain_second,
    head_first,
    head_second,
):
    devices = lax.axis_size(("dp", "ctx"))
    ctx_count = lax.axis_size("ctx")
    inner_width = w_out.shape[0] * devices
    own_rows, projected_width = w_in.shape
    seq_count, length, model_width = tokens.shape
    channels, taps = conv.shape[0] * devices, conv.shape[1] - 1
    state_dim = (channels - inner_width) // 2
    heads_count = heads.shape[1]
    head_dim = inner_width // heads_count
    mixer_width = projected_width - inner_width
    spare = -mixer_width % LANES
    wide_width = mixer_width + spare
    groups = ctx_count // seq_count
    lanes = inner_width // groups
    f32, bf16 = jnp.float32, jnp.bfloat16

    small = jnp.concatenate([conv.reshape(-1), gains])
    small = jnp.pad(small, (0, own_rows * spare - small.shape[0])).reshape(own_rows, spare)
    first_send = jnp.concatenate([w_in[:, inner_width:], small], axis=1).astype(bf16)
    mixer_weight = lax.all_gather(first_send, ("dp", "ctx"), axis=0, tiled=True)
    second_send = jnp.concatenate([w_in[:, :inner_width], w_out.reshape(own_rows, -1)], axis=1)
    mixer_weight, second_send = lax.optimization_barrier(
        (mixer_weight, second_send.astype(bf16))
    )
    second_weights = lax.all_gather(second_send, ("dp", "ctx"), axis=0, tiled=True)
    gate_weight = second_weights[:, :inner_width]
    output_weight = second_weights[:, inner_width:].reshape(inner_width, model_width)
    small = mixer_weight[:, mixer_width:].reshape(devices, own_rows * spare)
    conv_rows = small[:, : conv.size].reshape(channels, taps + 1).astype(f32).T
    conv_rows = jnp.pad(conv_rows, ((0, 7 - taps), (0, 0)))
    gain_vector = small[:, conv.size : conv.size + gains.size].reshape(-1).astype(f32)
    gain_in, gain_out = gain_vector[:model_width], gain_vector[model_width:]

    rim_x, rim_segment = shifted((tokens[:, length - 16 :], segments[:, length - 16 :]), "ctx", 1)
    rim_segment = jnp.where(lax.axis_index("ctx") == 0, -1, rim_segment)
    wide_segment = jnp.concatenate([rim_segment, segments], axis=1)
    marks = [wide_segment[:, 13 + tap : 13 + tap + length] == segments for tap in range(3)]
    marks.append(segments == rim_segment[:, 15:])
    marks.append(segments == segments[:, length - 1 :])
    marks = [mark.astype(f32) for mark in marks] + [segments.astype(f32)]
    marks = jnp.stack(marks + [jnp.zeros_like(marks[0])] * 2, axis=2)
    segment_rows = jnp.broadcast_to(segments.astype(f32)[:, None], (seq_count, 8, length))
    head_rows = jnp.stack([heads[2], -jnp.exp(heads[0])])
    head_rows = jnp.pad(head_rows, ((0, 6), (0, LANES - heads_count)))
    skip_row = jnp.broadcast_to(jnp.repeat(heads[1], head_dim), (8, inner_width))
    lane_head = lax.broadcasted_iota(jnp.int32, (LANES, inner_width), 1) // head_dim
    spread = lane_head == lax.broadcasted_iota(jnp.int32, (LANES, inner_width), 0)
    spread = spread.astype(bf16)
    gain_rows = jnp.broadcast_to(gain_in, (8, model_width))
    gate_rows = jnp.broadcast_to(gain_out, (8, inner_width))

    normed, wide_in, activated, step_raw, step_size, decay_sum, sent = kernel_call(
        functools.partial(entry_kernel, heads_count),
        (seq_count,),
        [
            per_row(length, model_width),
            per_row(16, model_width),
            per_row(length, 8),
            whole(model_width, wide_width),
            whole(8, model_width),
            whole(8, channels),
            whole(8, LANES),
            whole(LANES, inner_width),
        ],
        [
            per_row(length, model_width),
            per_row(length + 16, channels),
            per_row(length, channels),
            per_row(length, LANES),
            per_row(length, LANES),
            per_row(length, LANES),
            per_row(groups, state_dim + 8, lanes),
        ],
        [
            shape_of((seq_count, length, model_width), bf16),
            shape_of((seq_count, length + 16, channels), bf16),
            shape_of((seq_count, length, channels), bf16),
            shape_of((seq_count, length, LANES), f32),
            shape_of((seq_count, length, LANES), f32),
            shape_of((seq_count, length, LANES), f32),
            shape_of((seq_count, groups, state_dim + 8, lanes), f32),
        ],
        [pltpu.VMEM((length + 8, channels), f32)],
    )(tokens, rim_x, marks, mixer_weight, gain_rows, conv_rows, head_rows, spread)

    received = lax.all_to_all(
        sent.reshape(ctx_count, state_dim + 8, lanes), "ctx", 0, 0, tiled=True
    )
    within = kernel_call(
        functools.partial(inner_forward_kernel, heads_count),
        (seq_count,),
        [
            per_row(length, channels),
            per_row(length, LANES),
            per_row(length, LANES),
            per_row(length, 8),
            per_row(8, length),
        ],
        per_row(length, inner_width),
        shape_of((seq_count, length, inner_width), f32),
    )(activated, step_size, decay_sum, marks, segment_rows)
    tile = min(lanes, 2 * LANES)
    by_lane = lambda rows: pl.BlockSpec((ctx_count, rows, tile), lambda place: (0, 0, place))
    incoming_low, incoming = kernel_call(
        carry_forward_kernel,
        (lanes // tile,),
        [by_lane(state_dim + 8)],
        [by_lane(state_dim), by_lane(state_dim)],
        [
            shape_of((ctx_count, state_dim, lanes), bf16),
            shape_of((ctx_count, state_dim, lanes), f32),
        ],
    )(received)
    incoming_low = lax.all_to_all(incoming_low, "ctx", 0, 0, tiled=True)
    incoming_low = incoming_low.reshape(seq_count, groups, state_dim, lanes)

    half = min(length, 128)
    by_piece = lambda columns: pl.BlockSpec((1, half, columns), lambda row, piece: (row, piece, 0))
    mixed, grad_gate, grad_ssd, sent, outer_c, row_term, grad_gain_out, grad_skip = kernel_call(
        functools.partial(middle_kernel, groups),
        (seq_count, length // half),
        [
            by_piece(model_width),
            by_piece(model_width),
            whole(model_width, inner_width),
            whole(inner_width, model_width),
            whole(8, inner_width),
            whole(8, inner_width),
            by_piece(channels),
            by_piece(inner_width),
            per_row(groups, state_dim, lanes),
            by_piece(LANES),
            by_piece(8),
            whole(LANES, inner_width),
        ],
        [
            by_piece(inner_width),
            by_piece(inner_width),
            by_piece(inner_width),
            per_row(groups, state_dim, lanes),
            by_piece(state_dim),
            by_piece(LANES),
            whole(8, inner_width),
            whole(8, inner_width),
        ],
        [
            shape_of((seq_count, length, inner_width), bf16),
            shape_of((seq_count, length, inner_width), bf16),
            shape_of((seq_count, length, inner_width), bf16),
            shape_of((seq_count, groups, state_dim, lanes), bf16),
            shape_of((seq_count, length, state_dim), f32),
            shape_of((seq_count, length, LANES), f32),
            shape_of((8, inner_width), f32),
            shape_of((8, inner_width), f32),
        ],
        [pltpu.VMEM((state_dim, inner_width), f32)],
    )(
        cotangent,
        normed,
        gate_weight,
        output_weight,
        gate_rows,
        skip_row,
        activated,
        within,
        incoming_low,
        decay_sum,
        marks,
        spread,
    )
    grad_received = lax.all_to_all(
        sent.reshape(ctx_count, state_dim, lanes), "ctx", 0, 0, tiled=True
    )
    inner_x, inner_b, inner_c = kernel_call(
        functools.partial(inner_backward_kernel, heads_count),
        (seq_count,),
        [
            per_row(length, channels),
            per_row(length, inner_width),
            per_row(length, LANES),
            per_row(length, LANES),
            per_row(length, 8),
            per_row(8, length),
        ],
        [per_row(length, inner_width), per_row(length, state_dim), per_row(length, state_dim)],
        [
            shape_of((seq_count, length, inner_width), f32),
            shape_of((seq_count, length, state_dim), f32),
            shape_of((seq_count, length, state_dim), f32),
        ],
        [pltpu.VMEM((length, length), f32)],
    )(activated, grad_ssd, step_size, decay_sum, marks, segment_rows)
    sent = kernel_call(
        carry_backward_kernel,
        (lanes // tile,),
        [
            by_lane(state_dim),
            pl.BlockSpec((ctx_count, 8, tile), lambda place: (0, state_dim // 8, place)),
            by_lane(state_dim),
        ],
        by_lane(state_dim + 16),
        shape_of((ctx_count, state_dim + 16, lanes), bf16),
    )(grad_received, received, incoming)
    leaving = lax.all_to_all(sent, "ctx", 0, 0, tiled=True)
    leaving = leaving.reshape(seq_count, groups, state_dim + 16, lanes)

    def join(left, right):
        return jnp.einsum("nay,nag->yg", left, right, preferred_element_type=f32)

    input_float = tokens.astype(f32)
    output = (
        input_float
        + jnp.einsum("exp,pk->exk", mixed, output_weight, preferred_element_type=f32)
    ).astype(bf16)
    out_sum = sum_to_owner(join(mixed, cotangent).reshape(devices * own_rows, -1), False)
    gate_sum = sum_to_owner(join(normed, grad_gate), True)
    gate_normed = jnp.einsum("hou,qu->hoq", grad_gate, gate_weight, preferred_element_type=f32)

    grad_mixer, tail, rim, grad_conv, grad_heads = kernel_call(
        exit_kernel,
        (seq_count,),
        [
            per_row(length, channels),
            per_row(length + 16, channels),
            per_row(length, inner_width),
            per_row(length, inner_width),
            per_row(length, state_dim),
            per_row(length, state_dim),
            per_row(length, state_dim),
            per_row(groups, state_dim + 16, lanes),
            per_row(length, LANES),
            per_row(length, LANES),
            per_row(length, LANES),
            per_row(length, LANES),
            per_row(length, 8),
            whole(8, channels),
            whole(8, LANES),
            whole(8, inner_width),
            whole(LANES, inner_width),
        ],
        [
            per_row(length, wide_width),
            per_row(8, channels),
            per_row(8, channels),
            whole(8, channels),
            whole(8, LANES),
        ],
        [
            shape_of((seq_count, length, wide_width), bf16),
            shape_of((seq_count, 8, channels), f32),
            shape_of((seq_count, 8, channels), f32),
            shape_of((8, channels), f32),
            shape_of((8, LANES), f32),
        ],
        [
            pltpu.VMEM((length, channels), f32),
            pltpu.VMEM((length + 16, LANES), f32),
            pltpu.VMEM((length + 16, LANES), f32),
        ],
    )(
        activated,
        wide_in,
        grad_ssd,
        inner_x,
        inner_b,
        inner_c,
        outer_c,
        leaving,
        row_term,
        step_raw,
        step_size,
        decay_sum,
        marks,
        conv_rows,
        head_rows,
        skip_row,
        spread,
    )
    rim_back = shifted(rim[:, : taps - 1].astype(bf16), "ctx", -1).astype(f32)
    tail = tail.at[:, 9 - taps :].add(rim_back).astype(bf16)
    grad_mixer = grad_mixer.at[:, length - 8 :, :channels].set(tail)
    grad_mixer_weight = join(normed, grad_mixer)
    middle = wide_width // 256 * 128
    left_sum = sum_to_owner(grad_mixer_weight[:, :middle], True)
    right_sum = sum_to_owner(grad_mixer_weight[:, middle:], False)
    grad_normed = gate_normed + jnp.einsum(
        "hou,qu->hoq", grad_mixer, mixer_weight, preferred_element_type=f32
    )
    scale_in = inverse_rms(input_float)
    unit_in = input_float * scale_in
    grad_gain_in = jnp.sum(grad_normed * unit_in, axis=(0, 1))
    grad_unit_in = grad_normed * gain_in
    grad_tokens = cotangent.astype(f32) + scale_in * (
        grad_unit_in - unit_in * jnp.mean(grad_unit_in * unit_in, axis=-1, keepdims=True)
    )
    grad_conv = grad_conv[: taps + 1].T
    grad_gains = jnp.concatenate([grad_gain_in, grad_gain_out[0]])
    grad_skip = jnp.sum(grad_skip[0].reshape(heads_count, head_dim), axis=1)
    grad_heads = jnp.concatenate(
        [grad_heads[0, :heads_count], grad_skip, grad_heads[1, :heads_count]]
    )
    small_sum, head_grad = sum_small(
        jnp.concatenate(
            [grad_conv.reshape(devices, -1), grad_gains.reshape(devices, -1)], axis=1
        ),
        grad_heads,
    )
    owned_grads = (
        jnp.concatenate([gate_sum, left_sum, right_sum], axis=1)[:, :projected_width],
        out_sum.reshape(w_out.shape),
        small_sum[: conv.size].reshape(conv.shape),
        small_sum[conv.size :],
    )
    head_grad = head_grad.reshape(heads.shape)
    in_new = adamw(w_in, owned_grads[0], in_first, in_second, RATE_IN)
    out_new = adamw(w_out, owned_grads[1], out_first, out_second, RATE_OUT)
    conv_new = adamw(conv, owned_grads[2], conv_first, conv_second, RATE_CONV)
    gain_new = adamw(gains, owned_grads[3], gain_first, gain_second, RATE_GAIN)
    head_new = adamw(heads, head_grad, head_first, head_second, RATE_HEAD)
    return (
        output,
        grad_tokens,
        in_new[0],
        in_new[1],
        in_new[2],
        out_new[0],
        out_new[1],
        out_new[2],
        conv_new[0],
        conv_new[1],
        conv_new[2],
        gain_new[0],
        gain_new[1],
        gain_new[2],
        head_new[0],
        head_new[1],
        head_new[2],
    )


def solution(mesh):
    placed = (
        P("dp", "ctx", None),
        P("dp", "ctx", None),
        P("dp", "ctx"),
        P(("dp", "ctx"), None),
        P(("dp", "ctx"), None),
        P(("dp", "ctx"), None),
        P(("dp", "ctx")),
        P(),
        P(("dp", "ctx"), None),
        P(("dp", "ctx"), None),
        P(("dp", "ctx"), None),
        P(("dp", "ctx"), None),
        P(("dp", "ctx"), None),
        P(("dp", "ctx"), None),
        P(("dp", "ctx")),
        P(("dp", "ctx")),
        P(),
        P(),
    )
    return jax.shard_map(
        local,
        mesh=mesh,
        in_specs=placed,
        out_specs=(
            P("dp", "ctx", None),
            P("dp", "ctx", None),
            P(("dp", "ctx"), None),
            P(("dp", "ctx"), None),
            P(("dp", "ctx"), None),
            P(("dp", "ctx"), None),
            P(("dp", "ctx"), None),
            P(("dp", "ctx"), None),
            P(("dp", "ctx"), None),
            P(("dp", "ctx"), None),
            P(("dp", "ctx"), None),
            P(("dp", "ctx")),
            P(("dp", "ctx")),
            P(("dp", "ctx")),
            P(),
            P(),
            P(),
        ),
        check_vma=False,
    )
```

```python
import functools

import jax
import jax.numpy as jnp
from jax import lax
from jax.experimental import pallas as pl
from jax.experimental.pallas import tpu as pltpu
from jax.sharding import PartitionSpec as P

STEP = 10


EPSILON = 1e-05
BETA_ONE = 0.9
BETA_TWO = 0.95
ADAM_EPS = 1e-08
DECAY_RATE = 0.1
RATE_IN = 0.03
RATE_OUT = 0.02
RATE_CONV = 0.3
RATE_GAIN = 0.2
RATE_HEAD = 0.5
LOG2E = 1.4426950408889634
BELOW = -1e30
LANES = 128
VMEM_BYTES = 58 << 20
NT = (((1,), (1,)), ((), ()))
TN = (((0,), (0,)), ((), ()))


def shifted(value, axis, steps):
    count = lax.axis_size(axis)
    first, last = (max(0, -steps), min(count, count - steps))
    return lax.ppermute(value, axis, [(source, source + steps) for source in range(first, last)])


def bit_count(axis):
    return lax.axis_size(axis).bit_length() - 1


def swap(values, axis, bit):
    count = lax.axis_size(axis)
    return lax.ppermute(values, axis, [(place, place ^ (1 << bit)) for place in range(count)])


def sum_small(values, shared):
    dp_bits, ctx_bits = bit_count("dp"), bit_count("ctx")
    names = [("dp", bit) for bit in reversed(range(dp_bits))]
    names += [("ctx", bit) for bit in reversed(range(ctx_bits))]
    values = values.reshape((2,) * len(names) + (values.shape[1],))
    for axis, bit in list(names):
        dim = names.index((axis, bit))
        mine = (lax.axis_index(axis) >> bit) & 1
        kept = lax.dynamic_index_in_dim(values, mine, dim, keepdims=False)
        away = lax.dynamic_index_in_dim(values, 1 - mine, dim, keepdims=False)
        count = lax.axis_size(axis)
        away = lax.ppermute(
            jnp.concatenate([away.reshape(-1), shared]),
            axis,
            [(place, place ^ (1 << bit)) for place in range(count)],
        )
        values = kept + away[: kept.size].reshape(kept.shape)
        shared = shared + away[kept.size :]
        names.remove((axis, bit))
    return values, shared


def inverse_rms(values):
    return lax.rsqrt(jnp.mean(values * values, axis=-1, keepdims=True) + EPSILON)


def dot(left, right, dims=(((1,), (0,)), ((), ())), precision=None):
    return lax.dot_general(
        left, right, dims, precision=precision, preferred_element_type=jnp.float32
    )


def split_parts(values):
    high = values.astype(jnp.bfloat16)
    rest = values - high.astype(jnp.float32)
    middle = rest.astype(jnp.bfloat16)
    low = (rest - middle.astype(jnp.float32)).astype(jnp.bfloat16)
    return high, middle, low


def spread_heads(values, spread):
    high, middle, low = split_parts(values)
    return dot(high, spread) + dot(middle, spread) + dot(low, spread)


def sum_heads(values, spread):
    high, middle, low = split_parts(values)
    return dot(high, spread, NT) + dot(middle, spread, NT) + dot(low, spread, NT)


def causal(rows, columns):
    at_row = lax.broadcasted_iota(jnp.int32, (rows, columns), 0)
    at_column = lax.broadcasted_iota(jnp.int32, (rows, columns), 1)
    return at_row, at_column


def kernel_call(body, grid, in_specs, out_specs, out_shape, scratch=(), aliases=None):
    return pl.pallas_call(
        body,
        grid=grid,
        in_specs=in_specs,
        out_specs=out_specs,
        out_shape=out_shape,
        scratch_shapes=list(scratch),
        input_output_aliases=aliases or {},
        compiler_params=pltpu.CompilerParams(
            dimension_semantics=("arbitrary",) * len(grid), vmem_limit_bytes=VMEM_BYTES
        ),
    )


def per_row(*shape, first=0):
    return pl.BlockSpec((1,) + shape, lambda row, *_: (row + first,) + (0,) * len(shape))


def whole(*shape):
    return pl.BlockSpec(shape, lambda *_: (0,) * len(shape))


def untouched():
    return pl.BlockSpec(memory_space=pl.ANY)


def shape_of(shape, dtype):
    return jax.ShapeDtypeStruct(shape, dtype)


def entry_kernel(
    heads_count,
    x_ref,
    rim_ref,
    marks_ref,
    weight_ref,
    gain_ref,
    conv_ref,
    heads_ref,
    spread_ref,
    normed_ref,
    wide_out_ref,
    act_ref,
    raw_ref,
    step_ref,
    decay_ref,
    send_ref,
    wide_ref,
):
    length = x_ref.shape[1]
    inner, channels = spread_ref.shape[1], act_ref.shape[2]
    state = (channels - inner) // 2
    gain = gain_ref[0:1]

    def normalize(values):
        values = values.astype(jnp.float32)
        scale = lax.rsqrt(jnp.mean(values * values, axis=-1, keepdims=True) + EPSILON)
        return (values * scale * gain).astype(jnp.bfloat16)

    normed = normalize(x_ref[0])
    normed_ref[0] = normed
    normed = jnp.concatenate([normalize(rim_ref[0]), normed], axis=0)
    part = 768 if channels % 768 == 0 else LANES
    for start in range(0, channels, part):
        piece = dot(normed, weight_ref[:, start : start + part]).astype(jnp.bfloat16)
        wide_ref[:, start : start + part] = piece[8:].astype(jnp.float32)
    raw = dot(normed, weight_ref[:, channels:])[16:]
    raw_ref[0] = raw

    same = [
        jnp.broadcast_to(marks_ref[0, :, tap : tap + 1], (length, LANES)) for tap in range(3)
    ]

    def convolve(tile, carry):
        at = pl.ds(pl.multiple_of(tile * LANES, LANES), LANES)
        pre = jnp.broadcast_to(conv_ref[4:5, at], (length, LANES))
        for tap in range(3):
            taken = wide_ref[5 + tap : 5 + tap + length, at]
            pre = pre + conv_ref[tap : tap + 1, at] * taken * same[tap]
        pre = pre + conv_ref[3:4, at] * wide_ref[8:, at]
        act_ref[0, :, at] = (pre * jax.nn.sigmoid(pre)).astype(jnp.bfloat16)
        wide_out_ref[0, :, at] = jnp.concatenate(
            [jnp.zeros((8, LANES), jnp.float32), wide_ref[:, at]], axis=0
        ).astype(jnp.bfloat16)
        return carry

    lax.fori_loop(0, channels // LANES, convolve, 0)

    biased = raw + heads_ref[0:1]
    step = jnp.maximum(biased, 0.0) + jnp.log1p(jnp.exp(-jnp.abs(biased)))
    lane = lax.broadcasted_iota(jnp.int32, step.shape, 1)
    step = jnp.where(lane < heads_count, step, 0.0)
    step_ref[0] = step
    at_row, at_column = causal(length, length)
    lower = jnp.where(at_row >= at_column, 1.0, 0.0)
    decay = dot(lower, step * heads_ref[1:2], precision=lax.Precision.HIGHEST)
    decay_ref[0] = decay
    last = decay[length - 1 : length]
    end_weight = jnp.exp(last - decay) * marks_ref[0, :, 4:5] * step
    spread = spread_ref[...]
    scaled = (spread_heads(end_weight, spread) * act_ref[0, :, :inner].astype(jnp.float32)).astype(
        jnp.bfloat16
    )
    states = dot(act_ref[0, :, inner : inner + state], scaled, TN)
    passing = jnp.exp(last) * marks_ref[0, length - 1 : length, 3:4]
    passing = spread_heads(jnp.broadcast_to(passing, (8, LANES)), spread)
    groups, lanes = send_ref.shape[1], send_ref.shape[3]
    for group in range(groups):
        at = slice(group * lanes, (group + 1) * lanes)
        send_ref[0, group, :state] = states[:, at]
        send_ref[0, group, state:] = passing[:, at]


def pair_masks(pair_lanes, head_dim, rows):
    lane = lax.broadcasted_iota(jnp.int32, (rows, pair_lanes), 1)
    return [
        (lane >= member * head_dim) & (lane < (member + 1) * head_dim)
        for member in range(pair_lanes // head_dim)
    ]


def inner_forward_kernel(
    heads_count, act_ref, step_ref, decay_ref, marks_ref, segment_ref, y_ref
):
    length = act_ref.shape[1]
    inner = y_ref.shape[2]
    state = (act_ref.shape[2] - inner) // 2
    head_dim = inner // heads_count
    b_state = act_ref[0, :, inner : inner + state]
    c_state = act_ref[0, :, inner + state :]
    decay = decay_ref[0] * LOG2E
    lifted = (decay - jnp.log2(step_ref[0])).T
    at_row, at_column = causal(length, length)
    joined = (at_row >= at_column) & (marks_ref[0, :, 5:6] == segment_ref[0, 0:1])
    masked = jnp.where(joined, 0.0, BELOW)
    scores = dot(c_state, b_state, NT)
    chunk = max(length // 2, 16)
    masks = pair_masks(LANES, head_dim, length)
    for pair in range(inner // LANES):
        at = slice(pair * LANES, (pair + 1) * LANES)
        x_pair = act_ref[0, :, at]
        members = [jnp.where(mask, x_pair, jnp.zeros_like(x_pair)) for mask in masks]
        for start in range(0, length, chunk):
            rows, seen = slice(start, start + chunk), start + chunk
            total = jnp.zeros((chunk, LANES), jnp.float32)
            for member, x_member in enumerate(members):
                head = pair * len(masks) + member
                span = decay[rows, head : head + 1] - lifted[head : head + 1, :seen]
                mixing = scores[rows, :seen] * jnp.exp2(span + masked[rows, :seen])
                total = total + dot(mixing.astype(jnp.bfloat16), x_member[:seen])
            y_ref[0, rows, at] = total


def carry_forward_kernel(received_ref, held_ref, low_ref, incoming_ref, kept_ref):
    blocks, state = low_ref.shape[0], low_ref.shape[1]
    carried = jnp.zeros(low_ref.shape[1:], jnp.float32)
    for block in range(blocks):
        incoming_ref[block] = carried
        low_ref[block] = carried.astype(jnp.bfloat16)
        passing = received_ref[block, state : state + 1]
        carried = passing * carried + received_ref[block, :state]


def carry_backward_kernel(
    received_ref, passing_ref, incoming_ref, inner_ref, mixed_ref, gate_ref, send_ref, *kept_refs
):
    blocks, state = received_ref.shape[0], received_ref.shape[1]
    carried = jnp.zeros(received_ref.shape[1:], jnp.float32)
    for block in reversed(range(blocks)):
        send_ref[block, :state] = carried.astype(jnp.bfloat16)
        total = jnp.sum(carried * incoming_ref[block], axis=0, keepdims=True)
        parts = [part.astype(jnp.float32) for part in split_parts(total)]
        parts.append(jnp.zeros((13,) + total.shape[1:], jnp.float32))
        send_ref[block, state:] = jnp.concatenate(parts, axis=0).astype(jnp.bfloat16)
        carried = passing_ref[block, 0:1] * carried + received_ref[block].astype(jnp.float32)


def join_groups(ref, rows):
    return jnp.concatenate([ref[0, group, rows] for group in range(ref.shape[1])], axis=1)


def middle_kernel(
    groups,
    cotangent_ref,
    normed_ref,
    gate_weight_ref,
    out_weight_ref,
    gain_ref,
    skip_ref,
    act_ref,
    y_ref,
    incoming_ref,
    decay_ref,
    marks_ref,
    spread_ref,
    mixed_ref,
    grad_gate_ref,
    grad_ssd_ref,
    send_ref,
    grad_c_ref,
    row_term_ref,
    grad_gain_ref,
    grad_skip_ref,
    total_ref,
):
    row, piece = pl.program_id(0), pl.program_id(1)
    inner = spread_ref.shape[1]
    state = total_ref.shape[0]
    spread = spread_ref[...]
    gain, skip = gain_ref[0:1], skip_ref[0:1]
    x_part = act_ref[0, :, :inner].astype(jnp.float32)
    c_state = act_ref[0, :, inner + state :]
    incoming = join_groups(incoming_ref, slice(None))
    entry = spread_heads(jnp.exp(decay_ref[0]) * marks_ref[0, :, 3:4], spread)
    inner_part = y_ref[0] + entry * dot(c_state, incoming)
    ssd = inner_part + skip * x_part
    gate = dot(normed_ref[0], gate_weight_ref[...])
    sigmoid = jax.nn.sigmoid(gate)
    silu = gate * sigmoid
    gated = ssd * silu
    scale = lax.rsqrt(jnp.mean(gated * gated, axis=-1, keepdims=True) + EPSILON)
    unit = gated * scale
    mixed_ref[0] = (unit * gain).astype(jnp.bfloat16)
    grad_mixed = dot(cotangent_ref[0], out_weight_ref[...], NT)
    grad_unit = grad_mixed * gain
    mean = jnp.mean(grad_unit * unit, axis=-1, keepdims=True)
    grad_gated = scale * (grad_unit - unit * mean)
    slope = sigmoid * (1.0 + gate * (1.0 - sigmoid))
    grad_gate_ref[0] = (grad_gated * ssd * slope).astype(jnp.bfloat16)
    grad_ssd = (grad_gated * silu).astype(jnp.bfloat16)
    grad_ssd_ref[0] = grad_ssd
    grad_ssd = grad_ssd.astype(jnp.float32)
    row_term_ref[0] = sum_heads(grad_ssd * inner_part, spread)
    grad_before = (grad_ssd * entry).astype(jnp.bfloat16)
    grad_c_ref[0] = dot(grad_before, incoming, NT)
    grad_states = dot(c_state, grad_before, TN)
    gain_sum = jnp.sum(grad_mixed * unit, axis=0, keepdims=True)
    skip_sum = jnp.sum(grad_ssd * x_part, axis=0, keepdims=True)

    @pl.when(piece == 0)
    def _():
        total_ref[...] = grad_states

    @pl.when(piece > 0)
    def _():
        total_ref[...] += grad_states

    @pl.when((piece == 0) & (row == 0))
    def _():
        grad_gain_ref[...] = jnp.zeros_like(grad_gain_ref)
        grad_skip_ref[...] = jnp.zeros_like(grad_skip_ref)

    grad_gain_ref[0:1] += gain_sum
    grad_skip_ref[0:1] += skip_sum
    lanes = inner // groups

    @pl.when(piece == pl.num_programs(1) - 1)
    def _():
        for group in range(groups):
            at = slice(group * lanes, (group + 1) * lanes)
            send_ref[0, group] = total_ref[:, at].astype(jnp.bfloat16)


def inner_backward_kernel(
    heads_count,
    act_ref,
    grad_ssd_ref,
    step_ref,
    decay_ref,
    marks_ref,
    segment_ref,
    grad_x_ref,
    grad_b_ref,
    grad_c_ref,
    total_ref,
):
    length = act_ref.shape[1]
    inner = grad_ssd_ref.shape[2]
    state = (act_ref.shape[2] - inner) // 2
    head_dim = inner // heads_count
    b_state = act_ref[0, :, inner : inner + state]
    c_state = act_ref[0, :, inner + state :]
    decay = decay_ref[0] * LOG2E
    lowered = jnp.log2(step_ref[0]) - decay
    decay = decay.T
    at_row, at_column = causal(length, length)
    joined = (at_row <= at_column) & (marks_ref[0, :, 5:6] == segment_ref[0, 0:1])
    masked = jnp.where(joined, 0.0, BELOW)
    scores = dot(b_state, c_state, NT)
    chunk = max(length // 2, 16)
    masks = pair_masks(LANES, head_dim, length)
    total_ref[...] = jnp.zeros_like(total_ref)
    for pair in range(inner // LANES):
        at = slice(pair * LANES, (pair + 1) * LANES)
        x_pair = act_ref[0, :, at]
        grad_pair = grad_ssd_ref[0, :, at]
        members = [jnp.where(mask, grad_pair, jnp.zeros_like(grad_pair)) for mask in masks]
        for start in range(0, length, chunk):
            rows, later = slice(start, start + chunk), slice(start, length)
            grad_x = jnp.zeros((chunk, LANES), jnp.float32)
            for member, grad_member in enumerate(members):
                head = pair * len(masks) + member
                span = decay[head : head + 1, later] + lowered[rows, head : head + 1]
                weight = jnp.exp2(span + masked[rows, later])
                mixing = (scores[rows, later] * weight).astype(jnp.bfloat16)
                grad_x = grad_x + dot(mixing, grad_member[later])
                total_ref[rows, later] += dot(x_pair[rows], grad_member[later], NT) * weight
            grad_x_ref[0, rows, at] = grad_x
    grad_scores = total_ref[...].astype(jnp.bfloat16)
    grad_b_ref[0] = dot(grad_scores, c_state)
    grad_c_ref[0] = dot(grad_scores, b_state, TN)


def share_kernel(widths, chosen_ref, left_ref, right_ref, *refs):
    outs = refs[-len(widths) :]
    start = 0
    for out_ref, width in zip(outs, widths):
        out_ref[0] = dot(left_ref[...], right_ref[:, start : start + width], TN)
        start += width


def share_of_product(left, right, chosen, widths, held=None):
    dp_count = lax.axis_size("dp")
    left = left.reshape(-1, left.shape[2])
    right = right.reshape(-1, right.shape[2])
    tokens, rows = left.shape[0], left.shape[1] // dp_count
    held = [] if held is None else [held]
    results = pl.pallas_call(
        functools.partial(share_kernel, widths),
        grid_spec=pltpu.PrefetchScalarGridSpec(
            num_scalar_prefetch=1,
            grid=(dp_count // 2,),
            in_specs=[
                pl.BlockSpec((tokens, rows), lambda y, chosen: (0, 2 * y + chosen[0])),
                pl.BlockSpec(right.shape, lambda y, chosen: (0, 0)),
            ]
            + [untouched()] * len(held),
            out_specs=[untouched()] * len(held)
            + [pl.BlockSpec((1, rows, width), lambda y, chosen: (y, 0, 0)) for width in widths],
        ),
        out_shape=[shape_of(item.shape, item.dtype) for item in held]
        + [shape_of((dp_count // 2, rows, width), jnp.float32) for width in widths],
        input_output_aliases={3: 0} if held else {},
        compiler_params=pltpu.CompilerParams(vmem_limit_bytes=VMEM_BYTES),
    )(chosen.reshape(1), left, right, *held)
    return results[len(held) :], results[0] if held else None


def share_parts(left, right, widths, held=None):
    mine = lax.axis_index("dp") & 1
    away, _ = share_of_product(left, right, 1 - mine, widths)
    away = [swap(piece, "dp", 0) for piece in away]
    kept, held = share_of_product(left, right, mine, widths, held)
    return list(zip(kept, away)), held


class HalvedSum:
    def __init__(self, parts, y_first):
        dp_bits, ctx_bits = bit_count("dp"), bit_count("ctx")
        x_bits = dp_bits - 1
        self.names = [("dp", bit) for bit in reversed(range(1, dp_bits))]
        self.names += [("ctx", bit) for bit in reversed(range(ctx_bits))]
        split = (2,) * len(self.names)
        self.kept, self.arrived = (part.reshape(split + (-1, part.shape[2])) for part in parts)
        y_part = [("dp", bit) for bit in reversed(range(1, dp_bits))]
        x_part = [("ctx", bit) for bit in reversed(range(x_bits))]
        z_part = [("ctx", bit) for bit in range(x_bits, ctx_bits)]
        self.order = (y_part + x_part if y_first else x_part + y_part) + z_part

    def step(self):
        if not self.order:
            return
        axis, bit = self.order.pop(0)
        dim = self.names.index((axis, bit))
        self.names.remove((axis, bit))
        mine = (lax.axis_index(axis) >> bit) & 1

        def half(member):
            first, second = (
                lax.dynamic_index_in_dim(part, member, dim, keepdims=False)
                for part in (self.kept, self.arrived)
            )
            return first + second

        away = swap(half(1 - mine), axis, bit)
        self.kept, self.arrived = half(mine), away

    def finish(self):
        while self.order:
            self.step()
        return self.kept + self.arrived


def exit_kernel(held_count, *refs):
    ins, rest = refs[:17], refs[17:]
    outs, scratch = rest[-8 - held_count : -3 - held_count], rest[-3:]
    (
        act_ref,
        wide_ref,
        grad_ssd_ref,
        inner_x_ref,
        inner_b_ref,
        inner_c_ref,
        outer_c_ref,
        leaving_ref,
        row_term_ref,
        raw_ref,
        step_ref,
        decay_ref,
        marks_ref,
        conv_ref,
        heads_ref,
        skip_ref,
        spread_ref,
    ) = ins
    grad_mixer_ref, tail_ref, rim_ref, grad_conv_ref, grad_heads_ref = outs
    grad_act_ref, shift_ref, taken_ref = scratch
    row = pl.program_id(0)
    length, channels = act_ref.shape[1], act_ref.shape[2]
    inner = spread_ref.shape[1]
    state = (channels - inner) // 2
    spread = spread_ref[...]
    step, decay = step_ref[0], decay_ref[0]
    b_state = act_ref[0, :, inner : inner + state]
    leaving = join_groups(leaving_ref, slice(0, state))
    x_part = act_ref[0, :, :inner].astype(jnp.float32)
    last = decay[length - 1 : length]
    end_weight = spread_heads(jnp.exp(last - decay) * marks_ref[0, :, 4:5] * step, spread)
    scaled = (end_weight * x_part).astype(jnp.bfloat16)
    end_part = end_weight * dot(b_state, leaving)
    grad_x = inner_x_ref[0] + end_part
    grad_act_ref[:, :inner] = grad_x + skip_ref[0:1] * grad_ssd_ref[0].astype(jnp.float32)
    grad_act_ref[:, inner : inner + state] = inner_b_ref[0] + dot(scaled, leaving, NT)
    grad_act_ref[:, inner + state :] = inner_c_ref[0] + outer_c_ref[0]
    column_term = sum_heads(x_part * grad_x, spread)
    passed = join_groups(leaving_ref, slice(state, state + 16)).astype(jnp.float32)
    passed = jnp.sum(passed, axis=0, keepdims=True)
    ended = jnp.sum(x_part * end_part, axis=0, keepdims=True)
    ends = sum_heads(jnp.concatenate([passed, ended, jnp.zeros((6, inner), jnp.float32)], 0), spread)
    passing = jnp.exp(last) * marks_ref[0, length - 1 : length, 3:4]
    final = ends[1:2] + ends[0:1] * passing
    at_row, at_column = causal(length, length)
    token = lax.broadcasted_iota(jnp.int32, step.shape, 0)
    grad_decay = row_term_ref[0] - column_term + jnp.where(token == length - 1, final, 0.0)
    upper = jnp.where(at_row <= at_column, 1.0, 0.0)
    grad_later = dot(upper, grad_decay, precision=lax.Precision.HIGHEST)
    rate = heads_ref[1:2]
    grad_step = jnp.where(step > 0.0, column_term / jnp.where(step > 0.0, step, 1.0), 0.0)
    grad_step = grad_step + rate * grad_later
    grad_raw = grad_step * jax.nn.sigmoid(raw_ref[0] + heads_ref[0:1])
    grad_raw = jnp.where(step > 0.0, grad_raw, 0.0)
    grad_mixer_ref[0, :, channels:] = grad_raw.astype(jnp.bfloat16)

    @pl.when(row == 0)
    def _():
        grad_conv_ref[...] = jnp.zeros_like(grad_conv_ref)
        grad_heads_ref[...] = jnp.zeros_like(grad_heads_ref)

    grad_heads_ref[0:1] += jnp.sum(grad_later * step, axis=0, keepdims=True) * rate
    grad_heads_ref[1:2] += jnp.sum(grad_raw, axis=0, keepdims=True)

    same = [
        jnp.broadcast_to(marks_ref[0, :, tap : tap + 1], (length, LANES)) for tap in range(3)
    ]
    shift_ref[0:8] = jnp.zeros((8, LANES), jnp.float32)
    shift_ref[length + 8 :] = jnp.zeros((8, LANES), jnp.float32)

    def convolve(tile, carry):
        at = pl.ds(pl.multiple_of(tile * LANES, LANES), LANES)
        taken_ref[...] = wide_ref[0, :, at].astype(jnp.float32)
        pre = jnp.broadcast_to(conv_ref[4:5, at], (length, LANES))
        for tap in range(3):
            taken = taken_ref[13 + tap : 13 + tap + length]
            pre = pre + conv_ref[tap : tap + 1, at] * taken * same[tap]
        pre = pre + conv_ref[3:4, at] * taken_ref[16:]
        sigmoid = jax.nn.sigmoid(pre)
        grad_pre = grad_act_ref[:, at] * (sigmoid * (1.0 + pre * (1.0 - sigmoid)))
        grad_conv_ref[4:5, at] += jnp.sum(grad_pre, axis=0, keepdims=True)
        grad_conv_ref[3:4, at] += jnp.sum(grad_pre * taken_ref[16:], axis=0, keepdims=True)
        grad_in = grad_pre * conv_ref[3:4, at]
        rim = jnp.zeros((8, LANES), jnp.float32)
        for tap in range(3):
            masked = grad_pre * same[tap]
            taken = taken_ref[13 + tap : 13 + tap + length]
            grad_conv_ref[tap : tap + 1, at] += jnp.sum(masked * taken, axis=0, keepdims=True)
            shift_ref[8 : length + 8] = masked * conv_ref[tap : tap + 1, at]
            grad_in = grad_in + shift_ref[11 - tap : 11 - tap + length]
            rim = rim + shift_ref[8 - tap : 16 - tap]
        grad_mixer_ref[0, :, at] = grad_in.astype(jnp.bfloat16)
        tail_ref[0, :, at] = grad_in[length - 8 :]
        rim_ref[0, :, at] = rim
        return carry

    lax.fori_loop(0, channels // LANES, convolve, 0)


def adamw(weight, gradient, first_moment, second_moment, step_rate):
    first_new = BETA_ONE * first_moment + (1.0 - BETA_ONE) * gradient
    second_new = BETA_TWO * second_moment + (1.0 - BETA_TWO) * gradient * gradient
    corrected = first_new / (1.0 - BETA_ONE**STEP)
    spread = jnp.sqrt(second_new / (1.0 - BETA_TWO**STEP))
    weight_new = weight - step_rate * (corrected / (spread + ADAM_EPS) + DECAY_RATE * weight)
    return (first_new, second_new, weight_new)


def local(
    tokens,
    cotangent,
    segments,
    w_in,
    w_out,
    conv,
    gains,
    heads,
    in_first,
    in_second,
    out_first,
    out_second,
    conv_first,
    conv_second,
    gain_first,
    gain_second,
    head_first,
    head_second,
):
    devices = lax.axis_size(("dp", "ctx"))
    ctx_count = lax.axis_size("ctx")
    inner_width = w_out.shape[0] * devices
    own_rows, projected_width = w_in.shape
    seq_count, length, model_width = tokens.shape
    channels, taps = conv.shape[0] * devices, conv.shape[1] - 1
    state_dim = (channels - inner_width) // 2
    heads_count = heads.shape[1]
    head_dim = inner_width // heads_count
    mixer_width = projected_width - inner_width
    spare = -mixer_width % LANES
    wide_width = mixer_width + spare
    groups = ctx_count // seq_count
    lanes = inner_width // groups
    f32, bf16 = jnp.float32, jnp.bfloat16

    small = jnp.concatenate([conv.reshape(-1), gains])
    small = jnp.pad(small, (0, own_rows * spare - small.shape[0])).reshape(own_rows, spare)
    first_send = jnp.concatenate([w_in[:, inner_width:], small], axis=1).astype(bf16)
    mixer_weight = lax.all_gather(first_send, ("dp", "ctx"), axis=0, tiled=True)
    second_send = jnp.concatenate([w_in[:, :inner_width], w_out.reshape(own_rows, -1)], axis=1)
    mixer_weight, second_send = lax.optimization_barrier(
        (mixer_weight, second_send.astype(bf16))
    )
    second_weights = lax.all_gather(second_send, ("dp", "ctx"), axis=0, tiled=True)
    gate_weight = second_weights[:, :inner_width]
    output_weight = second_weights[:, inner_width:].reshape(inner_width, model_width)
    small = mixer_weight[:, mixer_width:].reshape(devices, own_rows * spare)
    conv_rows = small[:, : conv.size].reshape(channels, taps + 1).astype(f32).T
    conv_rows = jnp.pad(conv_rows, ((0, 7 - taps), (0, 0)))
    gain_vector = small[:, conv.size : conv.size + gains.size].reshape(-1).astype(f32)
    gain_in, gain_out = gain_vector[:model_width], gain_vector[model_width:]

    rim_x, rim_segment = shifted((tokens[:, length - 16 :], segments[:, length - 16 :]), "ctx", 1)
    rim_segment = jnp.where(lax.axis_index("ctx") == 0, -1, rim_segment)
    wide_segment = jnp.concatenate([rim_segment, segments], axis=1)
    marks = [wide_segment[:, 13 + tap : 13 + tap + length] == segments for tap in range(3)]
    marks.append(segments == rim_segment[:, 15:])
    marks.append(segments == segments[:, length - 1 :])
    marks = [mark.astype(f32) for mark in marks] + [segments.astype(f32)]
    marks = jnp.stack(marks + [jnp.zeros_like(marks[0])] * 2, axis=2)
    segment_rows = jnp.broadcast_to(segments.astype(f32)[:, None], (seq_count, 8, length))
    head_rows = jnp.stack([heads[2], -jnp.exp(heads[0])])
    head_rows = jnp.pad(head_rows, ((0, 6), (0, LANES - heads_count)))
    skip_row = jnp.broadcast_to(jnp.repeat(heads[1], head_dim), (8, inner_width))
    lane_head = lax.broadcasted_iota(jnp.int32, (LANES, inner_width), 1) // head_dim
    spread = lane_head == lax.broadcasted_iota(jnp.int32, (LANES, inner_width), 0)
    spread = spread.astype(bf16)
    gain_rows = jnp.broadcast_to(gain_in, (8, model_width))
    gate_rows = jnp.broadcast_to(gain_out, (8, inner_width))

    normed, wide_in, activated, step_raw, step_size, decay_sum, sent = kernel_call(
        functools.partial(entry_kernel, heads_count),
        (seq_count,),
        [
            per_row(length, model_width),
            per_row(16, model_width),
            per_row(length, 8),
            whole(model_width, wide_width),
            whole(8, model_width),
            whole(8, channels),
            whole(8, LANES),
            whole(LANES, inner_width),
        ],
        [
            per_row(length, model_width),
            per_row(length + 16, channels),
            per_row(length, channels),
            per_row(length, LANES),
            per_row(length, LANES),
            per_row(length, LANES),
            per_row(groups, state_dim + 8, lanes),
        ],
        [
            shape_of((seq_count, length, model_width), bf16),
            shape_of((seq_count, length + 16, channels), bf16),
            shape_of((seq_count, length, channels), bf16),
            shape_of((seq_count, length, LANES), f32),
            shape_of((seq_count, length, LANES), f32),
            shape_of((seq_count, length, LANES), f32),
            shape_of((seq_count, groups, state_dim + 8, lanes), f32),
        ],
        [pltpu.VMEM((length + 8, channels), f32)],
    )(tokens, rim_x, marks, mixer_weight, gain_rows, conv_rows, head_rows, spread)

    received = lax.all_to_all(
        sent.reshape(ctx_count, state_dim + 8, lanes), "ctx", 0, 0, tiled=True
    )
    within = kernel_call(
        functools.partial(inner_forward_kernel, heads_count),
        (seq_count,),
        [
            per_row(length, channels),
            per_row(length, LANES),
            per_row(length, LANES),
            per_row(length, 8),
            per_row(8, length),
        ],
        per_row(length, inner_width),
        shape_of((seq_count, length, inner_width), f32),
    )(activated, step_size, decay_sum, marks, segment_rows)
    tile = min(lanes, 2 * LANES)
    by_lane = lambda rows: pl.BlockSpec((ctx_count, rows, tile), lambda place: (0, 0, place))
    incoming_low, incoming, within = kernel_call(
        carry_forward_kernel,
        (lanes // tile,),
        [by_lane(state_dim + 8), untouched()],
        [by_lane(state_dim), by_lane(state_dim), untouched()],
        [
            shape_of((ctx_count, state_dim, lanes), bf16),
            shape_of((ctx_count, state_dim, lanes), f32),
            shape_of(within.shape, f32),
        ],
        aliases={1: 2},
    )(received, within)
    incoming_low = lax.all_to_all(incoming_low, "ctx", 0, 0, tiled=True)
    incoming_low = incoming_low.reshape(seq_count, groups, state_dim, lanes)

    half = min(length, 128)
    by_piece = lambda columns: pl.BlockSpec((1, half, columns), lambda row, piece: (row, piece, 0))
    mixed, grad_gate, grad_ssd, sent, outer_c, row_term, grad_gain_out, grad_skip = kernel_call(
        functools.partial(middle_kernel, groups),
        (seq_count, length // half),
        [
            by_piece(model_width),
            by_piece(model_width),
            whole(model_width, inner_width),
            whole(inner_width, model_width),
            whole(8, inner_width),
            whole(8, inner_width),
            by_piece(channels),
            by_piece(inner_width),
            per_row(groups, state_dim, lanes),
            by_piece(LANES),
            by_piece(8),
            whole(LANES, inner_width),
        ],
        [
            by_piece(inner_width),
            by_piece(inner_width),
            by_piece(inner_width),
            per_row(groups, state_dim, lanes),
            by_piece(state_dim),
            by_piece(LANES),
            whole(8, inner_width),
            whole(8, inner_width),
        ],
        [
            shape_of((seq_count, length, inner_width), bf16),
            shape_of((seq_count, length, inner_width), bf16),
            shape_of((seq_count, length, inner_width), bf16),
            shape_of((seq_count, groups, state_dim, lanes), bf16),
            shape_of((seq_count, length, state_dim), f32),
            shape_of((seq_count, length, LANES), f32),
            shape_of((8, inner_width), f32),
            shape_of((8, inner_width), f32),
        ],
        [pltpu.VMEM((state_dim, inner_width), f32)],
    )(
        cotangent,
        normed,
        gate_weight,
        output_weight,
        gate_rows,
        skip_row,
        activated,
        within,
        incoming_low,
        decay_sum,
        marks,
        spread,
    )
    grad_received = lax.all_to_all(
        sent.reshape(ctx_count, state_dim, lanes), "ctx", 0, 0, tiled=True
    )
    inner_x, inner_b, inner_c = kernel_call(
        functools.partial(inner_backward_kernel, heads_count),
        (seq_count,),
        [
            per_row(length, channels),
            per_row(length, inner_width),
            per_row(length, LANES),
            per_row(length, LANES),
            per_row(length, 8),
            per_row(8, length),
        ],
        [per_row(length, inner_width), per_row(length, state_dim), per_row(length, state_dim)],
        [
            shape_of((seq_count, length, inner_width), f32),
            shape_of((seq_count, length, state_dim), f32),
            shape_of((seq_count, length, state_dim), f32),
        ],
        [pltpu.VMEM((length, length), f32)],
    )(activated, grad_ssd, step_size, decay_sum, marks, segment_rows)
    sent, inner_x, mixed, grad_gate = kernel_call(
        carry_backward_kernel,
        (lanes // tile,),
        [
            by_lane(state_dim),
            pl.BlockSpec((ctx_count, 8, tile), lambda place: (0, state_dim // 8, place)),
            by_lane(state_dim),
            untouched(),
            untouched(),
            untouched(),
        ],
        [by_lane(state_dim + 16), untouched(), untouched(), untouched()],
        [
            shape_of((ctx_count, state_dim + 16, lanes), bf16),
            shape_of(inner_x.shape, f32),
            shape_of(mixed.shape, bf16),
            shape_of(grad_gate.shape, bf16),
        ],
        aliases={3: 1, 4: 2, 5: 3},
    )(grad_received, received, incoming, inner_x, mixed, grad_gate)
    leaving = lax.all_to_all(sent, "ctx", 0, 0, tiled=True)
    leaving = leaving.reshape(seq_count, groups, state_dim + 16, lanes)

    input_float = tokens.astype(f32)
    output = (
        input_float
        + jnp.einsum("exp,pk->exk", mixed, output_weight, preferred_element_type=f32)
    ).astype(bf16)
    gate_normed = jnp.einsum("hou,qu->hoq", grad_gate, gate_weight, preferred_element_type=f32)
    gate_parts, _ = share_parts(normed, grad_gate, [inner_width])
    out_parts, _ = share_parts(mixed, cotangent, [model_width])
    first_sums = [HalvedSum(gate_parts[0], True), HalvedSum(out_parts[0], False)]
    for item in first_sums:
        item.step()

    def exit_rows(first, count, held, previous):
        at_row = functools.partial(per_row, first=first)
        shapes = [
            shape_of((seq_count, length, wide_width), bf16),
            shape_of((seq_count, 8, channels), f32),
            shape_of((seq_count, 8, channels), f32),
            shape_of((8, channels), f32),
            shape_of((8, LANES), f32),
        ]
        aliases = {17 + place: place for place in range(len(previous))}
        aliases.update(
            {17 + len(previous) + place: 5 + place for place in range(len(held))}
        )
        return kernel_call(
            functools.partial(exit_kernel, len(held)),
            (count,),
            [
                at_row(length, channels),
                at_row(length + 16, channels),
                at_row(length, inner_width),
                at_row(length, inner_width),
                at_row(length, state_dim),
                at_row(length, state_dim),
                at_row(length, state_dim),
                at_row(groups, state_dim + 16, lanes),
                at_row(length, LANES),
                at_row(length, LANES),
                at_row(length, LANES),
                at_row(length, LANES),
                at_row(length, 8),
                whole(8, channels),
                whole(8, LANES),
                whole(8, inner_width),
                whole(LANES, inner_width),
            ]
            + [untouched()] * (len(previous) + len(held)),
            [
                at_row(length, wide_width),
                at_row(8, channels),
                at_row(8, channels),
                whole(8, channels),
                whole(8, LANES),
            ]
            + [untouched()] * len(held),
            shapes + [shape_of(item.shape, item.dtype) for item in held],
            [
                pltpu.VMEM((length, channels), f32),
                pltpu.VMEM((length + 16, LANES), f32),
                pltpu.VMEM((length + 16, LANES), f32),
            ],
            aliases=aliases,
        )(
            activated,
            wide_in,
            grad_ssd,
            inner_x,
            inner_b,
            inner_c,
            outer_c,
            leaving,
            row_term,
            step_raw,
            step_size,
            decay_sum,
            marks,
            conv_rows,
            head_rows,
            skip_row,
            spread,
            *previous,
            *held,
        )

    held = [item.kept for item in first_sums] + [gate_normed, output]
    *previous, first_conv, first_heads, kept_gate, kept_out, gate_normed, output = exit_rows(
        0, seq_count // 2, held, []
    )
    for item, kept in zip(first_sums, (kept_gate, kept_out)):
        item.kept = kept
        item.step()
    grad_mixer, tail, rim, grad_conv, grad_heads, kept_gate, kept_out = exit_rows(
        seq_count // 2, seq_count - seq_count // 2, [item.kept for item in first_sums], previous
    )
    for item, kept in zip(first_sums, (kept_gate, kept_out)):
        item.kept = kept
        item.step()
    grad_conv, grad_heads = grad_conv + first_conv, grad_heads + first_heads
    rim_back = shifted(rim[:, : taps - 1].astype(bf16), "ctx", -1).astype(f32)
    tail = tail.at[:, 9 - taps :].add(rim_back).astype(bf16)
    grad_mixer = grad_mixer.at[:, length - 8 :, :channels].set(tail)
    middle = wide_width // 256 * 128
    (left_parts, right_parts), gate_normed = share_parts(
        normed, grad_mixer, [middle, wide_width - middle], gate_normed
    )
    left_sum, right_sum = HalvedSum(left_parts, True), HalvedSum(right_parts, False)
    gate_sum, out_sum, left_sum, right_sum = (
        item.finish() for item in (*first_sums, left_sum, right_sum)
    )
    grad_normed = gate_normed + jnp.einsum(
        "hou,qu->hoq", grad_mixer, mixer_weight, preferred_element_type=f32
    )
    scale_in = inverse_rms(input_float)
    unit_in = input_float * scale_in
    grad_gain_in = jnp.sum(grad_normed * unit_in, axis=(0, 1))
    grad_unit_in = grad_normed * gain_in
    grad_tokens = cotangent.astype(f32) + scale_in * (
        grad_unit_in - unit_in * jnp.mean(grad_unit_in * unit_in, axis=-1, keepdims=True)
    )
    grad_conv = grad_conv[: taps + 1].T
    grad_gains = jnp.concatenate([grad_gain_in, grad_gain_out[0]])
    grad_skip = jnp.sum(grad_skip[0].reshape(heads_count, head_dim), axis=1)
    grad_heads = jnp.concatenate(
        [grad_heads[0, :heads_count], grad_skip, grad_heads[1, :heads_count]]
    )
    small_sum, head_grad = sum_small(
        jnp.concatenate(
            [grad_conv.reshape(devices, -1), grad_gains.reshape(devices, -1)], axis=1
        ),
        grad_heads,
    )
    owned_grads = (
        jnp.concatenate([gate_sum, left_sum, right_sum], axis=1)[:, :projected_width],
        out_sum.reshape(w_out.shape),
        small_sum[: conv.size].reshape(conv.shape),
        small_sum[conv.size :],
    )
    head_grad = head_grad.reshape(heads.shape)
    in_new = adamw(w_in, owned_grads[0], in_first, in_second, RATE_IN)
    out_new = adamw(w_out, owned_grads[1], out_first, out_second, RATE_OUT)
    conv_new = adamw(conv, owned_grads[2], conv_first, conv_second, RATE_CONV)
    gain_new = adamw(gains, owned_grads[3], gain_first, gain_second, RATE_GAIN)
    head_new = adamw(heads, head_grad, head_first, head_second, RATE_HEAD)
    return (
        output,
        grad_tokens,
        in_new[0],
        in_new[1],
        in_new[2],
        out_new[0],
        out_new[1],
        out_new[2],
        conv_new[0],
        conv_new[1],
        conv_new[2],
        gain_new[0],
        gain_new[1],
        gain_new[2],
        head_new[0],
        head_new[1],
        head_new[2],
    )


def solution(mesh):
    placed = (
        P("dp", "ctx", None),
        P("dp", "ctx", None),
        P("dp", "ctx"),
        P(("dp", "ctx"), None),
        P(("dp", "ctx"), None),
        P(("dp", "ctx"), None),
        P(("dp", "ctx")),
        P(),
        P(("dp", "ctx"), None),
        P(("dp", "ctx"), None),
        P(("dp", "ctx"), None),
        P(("dp", "ctx"), None),
        P(("dp", "ctx"), None),
        P(("dp", "ctx"), None),
        P(("dp", "ctx")),
        P(("dp", "ctx")),
        P(),
        P(),
    )
    return jax.shard_map(
        local,
        mesh=mesh,
        in_specs=placed,
        out_specs=(
            P("dp", "ctx", None),
            P("dp", "ctx", None),
            P(("dp", "ctx"), None),
            P(("dp", "ctx"), None),
            P(("dp", "ctx"), None),
            P(("dp", "ctx"), None),
            P(("dp", "ctx"), None),
            P(("dp", "ctx"), None),
            P(("dp", "ctx"), None),
            P(("dp", "ctx"), None),
            P(("dp", "ctx"), None),
            P(("dp", "ctx")),
            P(("dp", "ctx")),
            P(("dp", "ctx")),
            P(),
            P(),
            P(),
        ),
        check_vma=False,
    )
```

```python
import functools

import jax
import jax.numpy as jnp
from jax import lax
from jax.experimental import pallas as pl
from jax.experimental.pallas import tpu as pltpu
from jax.sharding import PartitionSpec as P

STEP = 10


EPSILON = 1e-05
BETA_ONE = 0.9
BETA_TWO = 0.95
ADAM_EPS = 1e-08
DECAY_RATE = 0.1
RATE_IN = 0.03
RATE_OUT = 0.02
RATE_CONV = 0.3
RATE_GAIN = 0.2
RATE_HEAD = 0.5
LOG2E = 1.4426950408889634
BELOW = -1e30
LANES = 128
VMEM_BYTES = 58 << 20
NT = (((1,), (1,)), ((), ()))
TN = (((0,), (0,)), ((), ()))


def shifted(value, axis, steps):
    count = lax.axis_size(axis)
    first, last = (max(0, -steps), min(count, count - steps))
    return lax.ppermute(value, axis, [(source, source + steps) for source in range(first, last)])


def bit_count(axis):
    return lax.axis_size(axis).bit_length() - 1


def swap(values, axis, bit):
    count = lax.axis_size(axis)
    return lax.ppermute(values, axis, [(place, place ^ (1 << bit)) for place in range(count)])


def sum_small(values, shared):
    dp_bits, ctx_bits = bit_count("dp"), bit_count("ctx")
    names = [("dp", bit) for bit in reversed(range(dp_bits))]
    names += [("ctx", bit) for bit in reversed(range(ctx_bits))]
    values = values.reshape((2,) * len(names) + (values.shape[1],))
    for axis, bit in list(names):
        dim = names.index((axis, bit))
        mine = (lax.axis_index(axis) >> bit) & 1
        kept = lax.dynamic_index_in_dim(values, mine, dim, keepdims=False)
        away = lax.dynamic_index_in_dim(values, 1 - mine, dim, keepdims=False)
        count = lax.axis_size(axis)
        away = lax.ppermute(
            jnp.concatenate([away.reshape(-1), shared]),
            axis,
            [(place, place ^ (1 << bit)) for place in range(count)],
        )
        values = kept + away[: kept.size].reshape(kept.shape)
        shared = shared + away[kept.size :]
        names.remove((axis, bit))
    return values, shared


def inverse_rms(values):
    return lax.rsqrt(jnp.mean(values * values, axis=-1, keepdims=True) + EPSILON)


def dot(left, right, dims=(((1,), (0,)), ((), ())), precision=None):
    return lax.dot_general(
        left, right, dims, precision=precision, preferred_element_type=jnp.float32
    )


def split_parts(values):
    high = values.astype(jnp.bfloat16)
    rest = values - high.astype(jnp.float32)
    middle = rest.astype(jnp.bfloat16)
    low = (rest - middle.astype(jnp.float32)).astype(jnp.bfloat16)
    return high, middle, low


def spread_heads(values, spread):
    high, middle, low = split_parts(values)
    return dot(high, spread) + dot(middle, spread) + dot(low, spread)


def sum_heads(values, spread):
    high, middle, low = split_parts(values)
    return dot(high, spread, NT) + dot(middle, spread, NT) + dot(low, spread, NT)


def causal(rows, columns):
    at_row = lax.broadcasted_iota(jnp.int32, (rows, columns), 0)
    at_column = lax.broadcasted_iota(jnp.int32, (rows, columns), 1)
    return at_row, at_column


def kernel_call(body, grid, in_specs, out_specs, out_shape, scratch=(), aliases=None):
    return pl.pallas_call(
        body,
        grid=grid,
        in_specs=in_specs,
        out_specs=out_specs,
        out_shape=out_shape,
        scratch_shapes=list(scratch),
        input_output_aliases=aliases or {},
        compiler_params=pltpu.CompilerParams(
            dimension_semantics=("arbitrary",) * len(grid), vmem_limit_bytes=VMEM_BYTES
        ),
    )


def per_row(*shape, first=0):
    return pl.BlockSpec((1,) + shape, lambda row, *_: (row + first,) + (0,) * len(shape))


def whole(*shape):
    return pl.BlockSpec(shape, lambda *_: (0,) * len(shape))


def untouched():
    return pl.BlockSpec(memory_space=pl.ANY)


def shape_of(shape, dtype):
    return jax.ShapeDtypeStruct(shape, dtype)


def entry_kernel(
    heads_count,
    x_ref,
    rim_ref,
    marks_ref,
    weight_ref,
    gain_ref,
    conv_ref,
    heads_ref,
    spread_ref,
    normed_ref,
    marks_out_ref,
    wide_out_ref,
    act_ref,
    raw_ref,
    step_ref,
    decay_ref,
    send_ref,
    wide_ref,
):
    length = x_ref.shape[1]
    inner, channels = spread_ref.shape[1], act_ref.shape[2]
    state = (channels - inner) // 2
    gain = gain_ref[0:1]
    marks = marks_ref[0].T
    marks_out_ref[0] = marks

    def normalize(values):
        values = values.astype(jnp.float32)
        scale = lax.rsqrt(jnp.mean(values * values, axis=-1, keepdims=True) + EPSILON)
        return (values * scale * gain).astype(jnp.bfloat16)

    normed = normalize(x_ref[0])
    normed_ref[0] = normed
    normed = jnp.concatenate([normalize(rim_ref[0]), normed], axis=0)
    part = 768 if channels % 768 == 0 else LANES
    for start in range(0, channels, part):
        piece = dot(normed, weight_ref[:, start : start + part]).astype(jnp.bfloat16)
        wide_ref[:, start : start + part] = piece[8:].astype(jnp.float32)
    raw = dot(normed, weight_ref[:, channels:])[16:]
    raw_ref[0] = raw

    same = [
        jnp.broadcast_to(marks[:, tap : tap + 1], (length, LANES)) for tap in range(3)
    ]

    def convolve(tile, carry):
        at = pl.ds(pl.multiple_of(tile * LANES, LANES), LANES)
        pre = jnp.broadcast_to(conv_ref[4:5, at], (length, LANES))
        for tap in range(3):
            taken = wide_ref[5 + tap : 5 + tap + length, at]
            pre = pre + conv_ref[tap : tap + 1, at] * taken * same[tap]
        pre = pre + conv_ref[3:4, at] * wide_ref[8:, at]
        act_ref[0, :, at] = (pre * jax.nn.sigmoid(pre)).astype(jnp.bfloat16)
        wide_out_ref[0, :, at] = jnp.concatenate(
            [jnp.zeros((8, LANES), jnp.float32), wide_ref[:, at]], axis=0
        ).astype(jnp.bfloat16)
        return carry

    lax.fori_loop(0, channels // LANES, convolve, 0)

    biased = raw + heads_ref[0:1]
    step = jnp.maximum(biased, 0.0) + jnp.log1p(jnp.exp(-jnp.abs(biased)))
    lane = lax.broadcasted_iota(jnp.int32, step.shape, 1)
    step = jnp.where(lane < heads_count, step, 0.0)
    step_ref[0] = step
    at_row, at_column = causal(length, length)
    lower = jnp.where(at_row >= at_column, 1.0, 0.0)
    decay = dot(lower, step * heads_ref[1:2], precision=lax.Precision.HIGHEST)
    decay_ref[0] = decay
    last = decay[length - 1 : length]
    end_weight = jnp.exp(last - decay) * marks[:, 4:5] * step
    spread = spread_ref[...]
    scaled = (spread_heads(end_weight, spread) * act_ref[0, :, :inner].astype(jnp.float32)).astype(
        jnp.bfloat16
    )
    states = dot(act_ref[0, :, inner : inner + state], scaled, TN)
    passing = jnp.exp(last) * marks[length - 1 : length, 3:4]
    passing = spread_heads(jnp.broadcast_to(passing, (8, LANES)), spread)
    groups, lanes = send_ref.shape[1], send_ref.shape[3]
    for group in range(groups):
        at = slice(group * lanes, (group + 1) * lanes)
        send_ref[0, group, :state] = states[:, at]
        send_ref[0, group, state:] = passing[:, at]


def pair_masks(pair_lanes, head_dim, rows):
    lane = lax.broadcasted_iota(jnp.int32, (rows, pair_lanes), 1)
    return [
        (lane >= member * head_dim) & (lane < (member + 1) * head_dim)
        for member in range(pair_lanes // head_dim)
    ]


def inner_forward_kernel(
    heads_count, act_ref, step_ref, decay_ref, marks_ref, segment_ref, y_ref
):
    length = act_ref.shape[1]
    inner = y_ref.shape[2]
    state = (act_ref.shape[2] - inner) // 2
    head_dim = inner // heads_count
    b_state = act_ref[0, :, inner : inner + state]
    c_state = act_ref[0, :, inner + state :]
    decay = decay_ref[0] * LOG2E
    lifted = (decay - jnp.log2(step_ref[0])).T
    at_row, at_column = causal(length, length)
    joined = (at_row >= at_column) & (marks_ref[0, :, 5:6] == segment_ref[0, 0:1])
    masked = jnp.where(joined, 0.0, BELOW)
    scores = dot(c_state, b_state, NT)
    chunk = max(length // 2, 16)
    masks = pair_masks(LANES, head_dim, length)
    for pair in range(inner // LANES):
        at = slice(pair * LANES, (pair + 1) * LANES)
        x_pair = act_ref[0, :, at]
        members = [jnp.where(mask, x_pair, jnp.zeros_like(x_pair)) for mask in masks]
        for start in range(0, length, chunk):
            rows, seen = slice(start, start + chunk), start + chunk
            total = jnp.zeros((chunk, LANES), jnp.float32)
            for member, x_member in enumerate(members):
                head = pair * len(masks) + member
                span = decay[rows, head : head + 1] - lifted[head : head + 1, :seen]
                mixing = scores[rows, :seen] * jnp.exp2(span + masked[rows, :seen])
                total = total + dot(mixing.astype(jnp.bfloat16), x_member[:seen])
            y_ref[0, rows, at] = total


def carry_forward_kernel(received_ref, held_ref, low_ref, incoming_ref, kept_ref):
    blocks, state = low_ref.shape[0], low_ref.shape[1]
    carried = jnp.zeros(low_ref.shape[1:], jnp.float32)
    for block in range(blocks):
        incoming_ref[block] = carried
        low_ref[block] = carried.astype(jnp.bfloat16)
        passing = received_ref[block, state : state + 1]
        carried = passing * carried + received_ref[block, :state]


def carry_backward_kernel(
    received_ref, passing_ref, incoming_ref, inner_ref, choice_ref, send_ref, *kept_refs
):
    blocks, state = received_ref.shape[0], received_ref.shape[1]
    carried = jnp.zeros(received_ref.shape[1:], jnp.float32)
    for block in reversed(range(blocks)):
        send_ref[block, :state] = carried.astype(jnp.bfloat16)
        total = jnp.sum(carried * incoming_ref[block], axis=0, keepdims=True)
        parts = [part.astype(jnp.float32) for part in split_parts(total)]
        parts.append(jnp.zeros((13,) + total.shape[1:], jnp.float32))
        send_ref[block, state:] = jnp.concatenate(parts, axis=0).astype(jnp.bfloat16)
        carried = passing_ref[block, 0:1] * carried + received_ref[block].astype(jnp.float32)


def join_groups(ref, rows):
    return jnp.concatenate([ref[0, group, rows] for group in range(ref.shape[1])], axis=1)


def middle_kernel(
    groups,
    cotangent_ref,
    normed_ref,
    gate_weight_ref,
    out_weight_ref,
    gain_ref,
    skip_ref,
    act_ref,
    y_ref,
    incoming_ref,
    decay_ref,
    marks_ref,
    spread_ref,
    mixed_ref,
    grad_gate_ref,
    grad_ssd_ref,
    send_ref,
    grad_c_ref,
    row_term_ref,
    grad_gain_ref,
    grad_skip_ref,
    total_ref,
):
    row, piece = pl.program_id(0), pl.program_id(1)
    inner = spread_ref.shape[1]
    state = total_ref.shape[0]
    spread = spread_ref[...]
    gain, skip = gain_ref[0:1], skip_ref[0:1]
    x_part = act_ref[0, :, :inner].astype(jnp.float32)
    c_state = act_ref[0, :, inner + state :]
    incoming = join_groups(incoming_ref, slice(None))
    entry = spread_heads(jnp.exp(decay_ref[0]) * marks_ref[0, :, 3:4], spread)
    inner_part = y_ref[0] + entry * dot(c_state, incoming)
    ssd = inner_part + skip * x_part
    gate = dot(normed_ref[0], gate_weight_ref[...])
    sigmoid = jax.nn.sigmoid(gate)
    silu = gate * sigmoid
    gated = ssd * silu
    scale = lax.rsqrt(jnp.mean(gated * gated, axis=-1, keepdims=True) + EPSILON)
    unit = gated * scale
    mixed_ref[0] = (unit * gain).astype(jnp.bfloat16)
    grad_mixed = dot(cotangent_ref[0], out_weight_ref[...], NT)
    grad_unit = grad_mixed * gain
    mean = jnp.mean(grad_unit * unit, axis=-1, keepdims=True)
    grad_gated = scale * (grad_unit - unit * mean)
    slope = sigmoid * (1.0 + gate * (1.0 - sigmoid))
    grad_gate_ref[0] = (grad_gated * ssd * slope).astype(jnp.bfloat16)
    grad_ssd = (grad_gated * silu).astype(jnp.bfloat16)
    grad_ssd_ref[0] = grad_ssd
    grad_ssd = grad_ssd.astype(jnp.float32)
    row_term_ref[0] = sum_heads(grad_ssd * inner_part, spread)
    grad_before = (grad_ssd * entry).astype(jnp.bfloat16)
    grad_c_ref[0] = dot(grad_before, incoming, NT)
    grad_states = dot(c_state, grad_before, TN)
    gain_sum = jnp.sum(grad_mixed * unit, axis=0, keepdims=True)
    skip_sum = jnp.sum(grad_ssd * x_part, axis=0, keepdims=True)

    @pl.when(piece == 0)
    def _():
        total_ref[...] = grad_states

    @pl.when(piece > 0)
    def _():
        total_ref[...] += grad_states

    @pl.when((piece == 0) & (row == 0))
    def _():
        grad_gain_ref[...] = jnp.zeros_like(grad_gain_ref)
        grad_skip_ref[...] = jnp.zeros_like(grad_skip_ref)

    grad_gain_ref[0:1] += gain_sum
    grad_skip_ref[0:1] += skip_sum
    lanes = inner // groups

    @pl.when(piece == pl.num_programs(1) - 1)
    def _():
        for group in range(groups):
            at = slice(group * lanes, (group + 1) * lanes)
            send_ref[0, group] = total_ref[:, at].astype(jnp.bfloat16)


def inner_backward_kernel(
    heads_count,
    act_ref,
    grad_ssd_ref,
    step_ref,
    decay_ref,
    marks_ref,
    segment_ref,
    grad_x_ref,
    grad_b_ref,
    grad_c_ref,
    total_ref,
):
    length = act_ref.shape[1]
    inner = grad_ssd_ref.shape[2]
    state = (act_ref.shape[2] - inner) // 2
    head_dim = inner // heads_count
    b_state = act_ref[0, :, inner : inner + state]
    c_state = act_ref[0, :, inner + state :]
    decay = decay_ref[0] * LOG2E
    lowered = jnp.log2(step_ref[0]) - decay
    decay = decay.T
    at_row, at_column = causal(length, length)
    joined = (at_row <= at_column) & (marks_ref[0, :, 5:6] == segment_ref[0, 0:1])
    masked = jnp.where(joined, 0.0, BELOW)
    scores = dot(b_state, c_state, NT)
    chunk = max(length // 2, 16)
    masks = pair_masks(LANES, head_dim, length)
    total_ref[...] = jnp.zeros_like(total_ref)
    for pair in range(inner // LANES):
        at = slice(pair * LANES, (pair + 1) * LANES)
        x_pair = act_ref[0, :, at]
        grad_pair = grad_ssd_ref[0, :, at]
        members = [jnp.where(mask, grad_pair, jnp.zeros_like(grad_pair)) for mask in masks]
        for start in range(0, length, chunk):
            rows, later = slice(start, start + chunk), slice(start, length)
            grad_x = jnp.zeros((chunk, LANES), jnp.float32)
            for member, grad_member in enumerate(members):
                head = pair * len(masks) + member
                span = decay[head : head + 1, later] + lowered[rows, head : head + 1]
                weight = jnp.exp2(span + masked[rows, later])
                mixing = (scores[rows, later] * weight).astype(jnp.bfloat16)
                grad_x = grad_x + dot(mixing, grad_member[later])
                total_ref[rows, later] += dot(x_pair[rows], grad_member[later], NT) * weight
            grad_x_ref[0, rows, at] = grad_x
    grad_scores = total_ref[...].astype(jnp.bfloat16)
    grad_b_ref[0] = dot(grad_scores, c_state)
    grad_c_ref[0] = dot(grad_scores, b_state, TN)


def share_kernel(widths, chosen_ref, left_ref, right_ref, *refs):
    outs = refs[-len(widths) :]
    start = 0
    for out_ref, width in zip(outs, widths):
        out_ref[0] = dot(left_ref[...], right_ref[:, start : start + width], TN)
        start += width


def share_of_product(left, right, chosen, widths, held=None):
    dp_count = lax.axis_size("dp")
    left = left.reshape(-1, left.shape[2])
    right = right.reshape(-1, right.shape[2])
    tokens, rows = left.shape[0], left.shape[1] // dp_count
    held = [] if held is None else [held]
    results = pl.pallas_call(
        functools.partial(share_kernel, widths),
        grid_spec=pltpu.PrefetchScalarGridSpec(
            num_scalar_prefetch=1,
            grid=(dp_count // 2,),
            in_specs=[
                pl.BlockSpec((tokens, rows), lambda y, chosen: (0, 2 * y + chosen[0])),
                pl.BlockSpec(right.shape, lambda y, chosen: (0, 0)),
            ]
            + [untouched()] * len(held),
            out_specs=[untouched()] * len(held)
            + [pl.BlockSpec((1, rows, width), lambda y, chosen: (y, 0, 0)) for width in widths],
        ),
        out_shape=[shape_of(item.shape, item.dtype) for item in held]
        + [shape_of((dp_count // 2, rows, width), jnp.float32) for width in widths],
        input_output_aliases={3: 0} if held else {},
        compiler_params=pltpu.CompilerParams(vmem_limit_bytes=VMEM_BYTES),
    )(chosen, left, right, *held)
    return results[len(held) :], results[0] if held else None


def share_parts(left, right, widths, choice, held=None):
    away, _ = share_of_product(left, right, choice[1:], widths)
    away = [swap(piece, "dp", 0) for piece in away]
    kept, held = share_of_product(left, right, choice[:1], widths, held)
    return list(zip(kept, away)), held


class HalvedSum:
    def __init__(self, parts, y_first):
        dp_bits, ctx_bits = bit_count("dp"), bit_count("ctx")
        x_bits = dp_bits - 1
        self.names = [("dp", bit) for bit in reversed(range(1, dp_bits))]
        self.names += [("ctx", bit) for bit in reversed(range(ctx_bits))]
        split = (2,) * len(self.names)
        self.kept, self.arrived = (part.reshape(split + (-1, part.shape[2])) for part in parts)
        y_part = [("dp", bit) for bit in reversed(range(1, dp_bits))]
        x_part = [("ctx", bit) for bit in reversed(range(x_bits))]
        z_part = [("ctx", bit) for bit in range(x_bits, ctx_bits)]
        self.order = (y_part + x_part if y_first else x_part + y_part) + z_part

    def step(self):
        if not self.order:
            return
        axis, bit = self.order.pop(0)
        dim = self.names.index((axis, bit))
        self.names.remove((axis, bit))
        mine = (lax.axis_index(axis) >> bit) & 1

        def half(member):
            first, second = (
                lax.dynamic_index_in_dim(part, member, dim, keepdims=False)
                for part in (self.kept, self.arrived)
            )
            return first + second

        away = swap(half(1 - mine), axis, bit)
        self.kept, self.arrived = half(mine), away

    def finish(self):
        while self.order:
            self.step()
        return self.kept + self.arrived


def exit_kernel(held_count, *refs):
    ins, rest = refs[:17], refs[17:]
    outs, scratch = rest[-8 - held_count : -3 - held_count], rest[-3:]
    (
        act_ref,
        wide_ref,
        grad_ssd_ref,
        inner_x_ref,
        inner_b_ref,
        inner_c_ref,
        outer_c_ref,
        leaving_ref,
        row_term_ref,
        raw_ref,
        step_ref,
        decay_ref,
        marks_ref,
        conv_ref,
        heads_ref,
        skip_ref,
        spread_ref,
    ) = ins
    grad_mixer_ref, tail_ref, rim_ref, grad_conv_ref, grad_heads_ref = outs
    grad_act_ref, shift_ref, taken_ref = scratch
    row = pl.program_id(0)
    length, channels = act_ref.shape[1], act_ref.shape[2]
    inner = spread_ref.shape[1]
    state = (channels - inner) // 2
    spread = spread_ref[...]
    step, decay = step_ref[0], decay_ref[0]
    b_state = act_ref[0, :, inner : inner + state]
    leaving = join_groups(leaving_ref, slice(0, state))
    x_part = act_ref[0, :, :inner].astype(jnp.float32)
    last = decay[length - 1 : length]
    end_weight = spread_heads(jnp.exp(last - decay) * marks_ref[0, :, 4:5] * step, spread)
    scaled = (end_weight * x_part).astype(jnp.bfloat16)
    end_part = end_weight * dot(b_state, leaving)
    grad_x = inner_x_ref[0] + end_part
    grad_act_ref[:, :inner] = grad_x + skip_ref[0:1] * grad_ssd_ref[0].astype(jnp.float32)
    grad_act_ref[:, inner : inner + state] = inner_b_ref[0] + dot(scaled, leaving, NT)
    grad_act_ref[:, inner + state :] = inner_c_ref[0] + outer_c_ref[0]
    column_term = sum_heads(x_part * grad_x, spread)
    passed = join_groups(leaving_ref, slice(state, state + 16)).astype(jnp.float32)
    passed = jnp.sum(passed, axis=0, keepdims=True)
    ended = jnp.sum(x_part * end_part, axis=0, keepdims=True)
    ends = sum_heads(jnp.concatenate([passed, ended, jnp.zeros((6, inner), jnp.float32)], 0), spread)
    passing = jnp.exp(last) * marks_ref[0, length - 1 : length, 3:4]
    final = ends[1:2] + ends[0:1] * passing
    at_row, at_column = causal(length, length)
    token = lax.broadcasted_iota(jnp.int32, step.shape, 0)
    grad_decay = row_term_ref[0] - column_term + jnp.where(token == length - 1, final, 0.0)
    upper = jnp.where(at_row <= at_column, 1.0, 0.0)
    grad_later = dot(upper, grad_decay, precision=lax.Precision.HIGHEST)
    rate = heads_ref[1:2]
    grad_step = jnp.where(step > 0.0, column_term / jnp.where(step > 0.0, step, 1.0), 0.0)
    grad_step = grad_step + rate * grad_later
    grad_raw = grad_step * jax.nn.sigmoid(raw_ref[0] + heads_ref[0:1])
    grad_raw = jnp.where(step > 0.0, grad_raw, 0.0)
    grad_mixer_ref[0, :, channels:] = grad_raw.astype(jnp.bfloat16)

    @pl.when(row == 0)
    def _():
        grad_conv_ref[...] = jnp.zeros_like(grad_conv_ref)
        grad_heads_ref[...] = jnp.zeros_like(grad_heads_ref)

    grad_heads_ref[0:1] += jnp.sum(grad_later * step, axis=0, keepdims=True) * rate
    grad_heads_ref[1:2] += jnp.sum(grad_raw, axis=0, keepdims=True)

    same = [
        jnp.broadcast_to(marks_ref[0, :, tap : tap + 1], (length, LANES)) for tap in range(3)
    ]
    shift_ref[0:8] = jnp.zeros((8, LANES), jnp.float32)
    shift_ref[length + 8 :] = jnp.zeros((8, LANES), jnp.float32)

    def convolve(tile, carry):
        at = pl.ds(pl.multiple_of(tile * LANES, LANES), LANES)
        taken_ref[...] = wide_ref[0, :, at].astype(jnp.float32)
        pre = jnp.broadcast_to(conv_ref[4:5, at], (length, LANES))
        for tap in range(3):
            taken = taken_ref[13 + tap : 13 + tap + length]
            pre = pre + conv_ref[tap : tap + 1, at] * taken * same[tap]
        pre = pre + conv_ref[3:4, at] * taken_ref[16:]
        sigmoid = jax.nn.sigmoid(pre)
        grad_pre = grad_act_ref[:, at] * (sigmoid * (1.0 + pre * (1.0 - sigmoid)))
        grad_conv_ref[4:5, at] += jnp.sum(grad_pre, axis=0, keepdims=True)
        grad_conv_ref[3:4, at] += jnp.sum(grad_pre * taken_ref[16:], axis=0, keepdims=True)
        grad_in = grad_pre * conv_ref[3:4, at]
        rim = jnp.zeros((8, LANES), jnp.float32)
        for tap in range(3):
            masked = grad_pre * same[tap]
            taken = taken_ref[13 + tap : 13 + tap + length]
            grad_conv_ref[tap : tap + 1, at] += jnp.sum(masked * taken, axis=0, keepdims=True)
            shift_ref[8 : length + 8] = masked * conv_ref[tap : tap + 1, at]
            grad_in = grad_in + shift_ref[11 - tap : 11 - tap + length]
            rim = rim + shift_ref[8 - tap : 16 - tap]
        grad_mixer_ref[0, :, at] = grad_in.astype(jnp.bfloat16)
        tail_ref[0, :, at] = grad_in[length - 8 :]
        rim_ref[0, :, at] = rim
        return carry

    lax.fori_loop(0, channels // LANES, convolve, 0)


def adamw(weight, gradient, first_moment, second_moment, step_rate):
    first_new = BETA_ONE * first_moment + (1.0 - BETA_ONE) * gradient
    second_new = BETA_TWO * second_moment + (1.0 - BETA_TWO) * gradient * gradient
    corrected = first_new / (1.0 - BETA_ONE**STEP)
    spread = jnp.sqrt(second_new / (1.0 - BETA_TWO**STEP))
    weight_new = weight - step_rate * (corrected / (spread + ADAM_EPS) + DECAY_RATE * weight)
    return (first_new, second_new, weight_new)


def local(
    tokens,
    cotangent,
    segments,
    w_in,
    w_out,
    conv,
    gains,
    heads,
    in_first,
    in_second,
    out_first,
    out_second,
    conv_first,
    conv_second,
    gain_first,
    gain_second,
    head_first,
    head_second,
):
    devices = lax.axis_size(("dp", "ctx"))
    ctx_count = lax.axis_size("ctx")
    inner_width = w_out.shape[0] * devices
    own_rows, projected_width = w_in.shape
    seq_count, length, model_width = tokens.shape
    channels, taps = conv.shape[0] * devices, conv.shape[1] - 1
    state_dim = (channels - inner_width) // 2
    heads_count = heads.shape[1]
    head_dim = inner_width // heads_count
    mixer_width = projected_width - inner_width
    spare = -mixer_width % LANES
    wide_width = mixer_width + spare
    groups = ctx_count // seq_count
    lanes = inner_width // groups
    f32, bf16 = jnp.float32, jnp.bfloat16

    small = jnp.concatenate([conv.reshape(-1), gains])
    small = jnp.pad(small, (0, own_rows * spare - small.shape[0])).reshape(own_rows, spare)
    first_send = jnp.concatenate([w_in[:, inner_width:], small], axis=1).astype(bf16)
    mixer_weight = lax.all_gather(first_send, ("dp", "ctx"), axis=0, tiled=True)
    second_send = jnp.concatenate([w_in[:, :inner_width], w_out.reshape(own_rows, -1)], axis=1)
    mixer_weight, second_send = lax.optimization_barrier(
        (mixer_weight, second_send.astype(bf16))
    )
    second_weights = lax.all_gather(second_send, ("dp", "ctx"), axis=0, tiled=True)
    gate_weight = second_weights[:, :inner_width]
    output_weight = second_weights[:, inner_width:].reshape(inner_width, model_width)
    small = mixer_weight[:, mixer_width:].reshape(devices, own_rows * spare)
    conv_rows = small[:, : conv.size].reshape(channels, taps + 1).astype(f32).T
    conv_rows = jnp.pad(conv_rows, ((0, 7 - taps), (0, 0)))
    gain_vector = small[:, conv.size : conv.size + gains.size].reshape(-1).astype(f32)
    gain_in, gain_out = gain_vector[:model_width], gain_vector[model_width:]

    rim_send = tokens[:, length - 16 :]
    tail_segments = segments[:, None, length - 16 :].astype(bf16)
    rim_send = rim_send.at[:, :1, :16].set(tail_segments)
    rim_x = shifted(rim_send, "ctx", 1)
    rim_segment = rim_x[:, 0, :16].astype(jnp.int32)
    rim_segment = jnp.where(lax.axis_index("ctx") == 0, -1, rim_segment)
    wide_segment = jnp.concatenate([rim_segment, segments], axis=1)
    marks = [wide_segment[:, 13 + tap : 13 + tap + length] == segments for tap in range(3)]
    marks.append(segments == rim_segment[:, 15:])
    marks.append(segments == segments[:, length - 1 :])
    marks = [mark.astype(f32) for mark in marks] + [segments.astype(f32)]
    marks = jnp.stack(marks + [jnp.zeros_like(marks[0])] * 2, axis=1)
    segment_rows = jnp.broadcast_to(segments.astype(f32)[:, None], (seq_count, 8, length))
    head_rows = jnp.stack([heads[2], -jnp.exp(heads[0])])
    head_rows = jnp.pad(head_rows, ((0, 6), (0, LANES - heads_count)))
    skip_row = jnp.broadcast_to(jnp.repeat(heads[1], head_dim), (8, inner_width))
    lane_head = lax.broadcasted_iota(jnp.int32, (LANES, inner_width), 1) // head_dim
    spread = lane_head == lax.broadcasted_iota(jnp.int32, (LANES, inner_width), 0)
    spread = spread.astype(bf16)
    gain_rows = jnp.broadcast_to(gain_in, (8, model_width))
    gate_rows = jnp.broadcast_to(gain_out, (8, inner_width))

    normed, marks, wide_in, activated, step_raw, step_size, decay_sum, sent = kernel_call(
        functools.partial(entry_kernel, heads_count),
        (seq_count,),
        [
            per_row(length, model_width),
            per_row(16, model_width),
            per_row(8, length),
            whole(model_width, wide_width),
            whole(8, model_width),
            whole(8, channels),
            whole(8, LANES),
            whole(LANES, inner_width),
        ],
        [
            per_row(length, model_width),
            per_row(length, 8),
            per_row(length + 16, channels),
            per_row(length, channels),
            per_row(length, LANES),
            per_row(length, LANES),
            per_row(length, LANES),
            per_row(groups, state_dim + 8, lanes),
        ],
        [
            shape_of((seq_count, length, model_width), bf16),
            shape_of((seq_count, length, 8), f32),
            shape_of((seq_count, length + 16, channels), bf16),
            shape_of((seq_count, length, channels), bf16),
            shape_of((seq_count, length, LANES), f32),
            shape_of((seq_count, length, LANES), f32),
            shape_of((seq_count, length, LANES), f32),
            shape_of((seq_count, groups, state_dim + 8, lanes), f32),
        ],
        [pltpu.VMEM((length + 8, channels), f32)],
    )(tokens, rim_x, marks, mixer_weight, gain_rows, conv_rows, head_rows, spread)

    received = lax.all_to_all(
        sent.reshape(ctx_count, state_dim + 8, lanes), "ctx", 0, 0, tiled=True
    )
    within = kernel_call(
        functools.partial(inner_forward_kernel, heads_count),
        (seq_count,),
        [
            per_row(length, channels),
            per_row(length, LANES),
            per_row(length, LANES),
            per_row(length, 8),
            per_row(8, length),
        ],
        per_row(length, inner_width),
        shape_of((seq_count, length, inner_width), f32),
    )(activated, step_size, decay_sum, marks, segment_rows)
    tile = min(lanes, 2 * LANES)
    by_lane = lambda rows: pl.BlockSpec((ctx_count, rows, tile), lambda place: (0, 0, place))
    incoming_low, incoming, within = kernel_call(
        carry_forward_kernel,
        (lanes // tile,),
        [by_lane(state_dim + 8), untouched()],
        [by_lane(state_dim), by_lane(state_dim), untouched()],
        [
            shape_of((ctx_count, state_dim, lanes), bf16),
            shape_of((ctx_count, state_dim, lanes), f32),
            shape_of(within.shape, f32),
        ],
        aliases={1: 2},
    )(received, within)
    incoming_low = lax.all_to_all(incoming_low, "ctx", 0, 0, tiled=True)
    incoming_low = incoming_low.reshape(seq_count, groups, state_dim, lanes)

    half = min(length, 128)
    by_piece = lambda columns: pl.BlockSpec((1, half, columns), lambda row, piece: (row, piece, 0))
    mixed, grad_gate, grad_ssd, sent, outer_c, row_term, grad_gain_out, grad_skip = kernel_call(
        functools.partial(middle_kernel, groups),
        (seq_count, length // half),
        [
            by_piece(model_width),
            by_piece(model_width),
            whole(model_width, inner_width),
            whole(inner_width, model_width),
            whole(8, inner_width),
            whole(8, inner_width),
            by_piece(channels),
            by_piece(inner_width),
            per_row(groups, state_dim, lanes),
            by_piece(LANES),
            by_piece(8),
            whole(LANES, inner_width),
        ],
        [
            by_piece(inner_width),
            by_piece(inner_width),
            by_piece(inner_width),
            per_row(groups, state_dim, lanes),
            by_piece(state_dim),
            by_piece(LANES),
            whole(8, inner_width),
            whole(8, inner_width),
        ],
        [
            shape_of((seq_count, length, inner_width), bf16),
            shape_of((seq_count, length, inner_width), bf16),
            shape_of((seq_count, length, inner_width), bf16),
            shape_of((seq_count, groups, state_dim, lanes), bf16),
            shape_of((seq_count, length, state_dim), f32),
            shape_of((seq_count, length, LANES), f32),
            shape_of((8, inner_width), f32),
            shape_of((8, inner_width), f32),
        ],
        [pltpu.VMEM((state_dim, inner_width), f32)],
    )(
        cotangent,
        normed,
        gate_weight,
        output_weight,
        gate_rows,
        skip_row,
        activated,
        within,
        incoming_low,
        decay_sum,
        marks,
        spread,
    )
    grad_received = lax.all_to_all(
        sent.reshape(ctx_count, state_dim, lanes), "ctx", 0, 0, tiled=True
    )
    inner_x, inner_b, inner_c = kernel_call(
        functools.partial(inner_backward_kernel, heads_count),
        (seq_count,),
        [
            per_row(length, channels),
            per_row(length, inner_width),
            per_row(length, LANES),
            per_row(length, LANES),
            per_row(length, 8),
            per_row(8, length),
        ],
        [per_row(length, inner_width), per_row(length, state_dim), per_row(length, state_dim)],
        [
            shape_of((seq_count, length, inner_width), f32),
            shape_of((seq_count, length, state_dim), f32),
            shape_of((seq_count, length, state_dim), f32),
        ],
        [pltpu.VMEM((length, length), f32)],
    )(activated, grad_ssd, step_size, decay_sum, marks, segment_rows)
    mine = lax.axis_index("dp") & 1
    choice = jnp.stack([mine, 1 - mine]).astype(jnp.int32)
    sent, inner_x, choice = kernel_call(
        carry_backward_kernel,
        (lanes // tile,),
        [
            by_lane(state_dim),
            pl.BlockSpec((ctx_count, 8, tile), lambda place: (0, state_dim // 8, place)),
            by_lane(state_dim),
            untouched(),
            untouched(),
        ],
        [by_lane(state_dim + 16), untouched(), untouched()],
        [
            shape_of((ctx_count, state_dim + 16, lanes), bf16),
            shape_of(inner_x.shape, f32),
            shape_of(choice.shape, jnp.int32),
        ],
        aliases={3: 1, 4: 2},
    )(grad_received, received, incoming, inner_x, choice)
    leaving = lax.all_to_all(sent, "ctx", 0, 0, tiled=True)
    leaving = leaving.reshape(seq_count, groups, state_dim + 16, lanes)

    input_float = tokens.astype(f32)
    output = (
        input_float
        + jnp.einsum("exp,pk->exk", mixed, output_weight, preferred_element_type=f32)
    ).astype(bf16)
    gate_normed = jnp.einsum("hou,qu->hoq", grad_gate, gate_weight, preferred_element_type=f32)
    gate_parts, _ = share_parts(normed, grad_gate, [inner_width], choice)
    out_parts, _ = share_parts(mixed, cotangent, [model_width], choice)
    first_sums = [HalvedSum(gate_parts[0], True), HalvedSum(out_parts[0], False)]
    for item in first_sums:
        item.step()

    def exit_rows(first, count, held, previous):
        at_row = functools.partial(per_row, first=first)
        shapes = [
            shape_of((seq_count, length, wide_width), bf16),
            shape_of((seq_count, 8, channels), f32),
            shape_of((seq_count, 8, channels), f32),
            shape_of((8, channels), f32),
            shape_of((8, LANES), f32),
        ]
        aliases = {17 + place: place for place in range(len(previous))}
        aliases.update(
            {17 + len(previous) + place: 5 + place for place in range(len(held))}
        )
        return kernel_call(
            functools.partial(exit_kernel, len(held)),
            (count,),
            [
                at_row(length, channels),
                at_row(length + 16, channels),
                at_row(length, inner_width),
                at_row(length, inner_width),
                at_row(length, state_dim),
                at_row(length, state_dim),
                at_row(length, state_dim),
                at_row(groups, state_dim + 16, lanes),
                at_row(length, LANES),
                at_row(length, LANES),
                at_row(length, LANES),
                at_row(length, LANES),
                at_row(length, 8),
                whole(8, channels),
                whole(8, LANES),
                whole(8, inner_width),
                whole(LANES, inner_width),
            ]
            + [untouched()] * (len(previous) + len(held)),
            [
                at_row(length, wide_width),
                at_row(8, channels),
                at_row(8, channels),
                whole(8, channels),
                whole(8, LANES),
            ]
            + [untouched()] * len(held),
            shapes + [shape_of(item.shape, item.dtype) for item in held],
            [
                pltpu.VMEM((length, channels), f32),
                pltpu.VMEM((length + 16, LANES), f32),
                pltpu.VMEM((length + 16, LANES), f32),
            ],
            aliases=aliases,
        )(
            activated,
            wide_in,
            grad_ssd,
            inner_x,
            inner_b,
            inner_c,
            outer_c,
            leaving,
            row_term,
            step_raw,
            step_size,
            decay_sum,
            marks,
            conv_rows,
            head_rows,
            skip_row,
            spread,
            *previous,
            *held,
        )

    held = [item.kept for item in first_sums] + [gate_normed, output]
    *previous, first_conv, first_heads, kept_gate, kept_out, gate_normed, output = exit_rows(
        0, seq_count // 2, held, []
    )
    for item, kept in zip(first_sums, (kept_gate, kept_out)):
        item.kept = kept
        item.step()
    grad_mixer, tail, rim, grad_conv, grad_heads, kept_gate, kept_out = exit_rows(
        seq_count // 2, seq_count - seq_count // 2, [item.kept for item in first_sums], previous
    )
    for item, kept in zip(first_sums, (kept_gate, kept_out)):
        item.kept = kept
        item.step()
    grad_conv, grad_heads = grad_conv + first_conv, grad_heads + first_heads
    rim_back = shifted(rim[:, : taps - 1].astype(bf16), "ctx", -1).astype(f32)
    tail = tail.at[:, 9 - taps :].add(rim_back).astype(bf16)
    grad_mixer = grad_mixer.at[:, length - 8 :, :channels].set(tail)
    middle = wide_width // 256 * 128
    (left_parts, right_parts), mixer_weight = share_parts(
        normed, grad_mixer, [middle, wide_width - middle], choice, mixer_weight
    )
    left_sum, right_sum = HalvedSum(left_parts, True), HalvedSum(right_parts, False)
    gate_sum, out_sum, left_sum, right_sum = (
        item.finish() for item in (*first_sums, left_sum, right_sum)
    )
    grad_normed = gate_normed + jnp.einsum(
        "hou,qu->hoq", grad_mixer, mixer_weight, preferred_element_type=f32
    )
    scale_in = inverse_rms(input_float)
    unit_in = input_float * scale_in
    grad_gain_in = jnp.sum(grad_normed * unit_in, axis=(0, 1))
    grad_unit_in = grad_normed * gain_in
    grad_tokens = cotangent.astype(f32) + scale_in * (
        grad_unit_in - unit_in * jnp.mean(grad_unit_in * unit_in, axis=-1, keepdims=True)
    )
    grad_conv = grad_conv[: taps + 1].T
    grad_gains = jnp.concatenate([grad_gain_in, grad_gain_out[0]])
    grad_skip = jnp.sum(grad_skip[0].reshape(heads_count, head_dim), axis=1)
    grad_heads = jnp.concatenate(
        [grad_heads[0, :heads_count], grad_skip, grad_heads[1, :heads_count]]
    )
    small_sum, head_grad = sum_small(
        jnp.concatenate(
            [grad_conv.reshape(devices, -1), grad_gains.reshape(devices, -1)], axis=1
        ),
        grad_heads,
    )
    owned_grads = (
        jnp.concatenate([gate_sum, left_sum, right_sum], axis=1)[:, :projected_width],
        out_sum.reshape(w_out.shape),
        small_sum[: conv.size].reshape(conv.shape),
        small_sum[conv.size :],
    )
    head_grad = head_grad.reshape(heads.shape)
    in_new = adamw(w_in, owned_grads[0], in_first, in_second, RATE_IN)
    out_new = adamw(w_out, owned_grads[1], out_first, out_second, RATE_OUT)
    conv_new = adamw(conv, owned_grads[2], conv_first, conv_second, RATE_CONV)
    gain_new = adamw(gains, owned_grads[3], gain_first, gain_second, RATE_GAIN)
    head_new = adamw(heads, head_grad, head_first, head_second, RATE_HEAD)
    return (
        output,
        grad_tokens,
        in_new[0],
        in_new[1],
        in_new[2],
        out_new[0],
        out_new[1],
        out_new[2],
        conv_new[0],
        conv_new[1],
        conv_new[2],
        gain_new[0],
        gain_new[1],
        gain_new[2],
        head_new[0],
        head_new[1],
        head_new[2],
    )


def solution(mesh):
    placed = (
        P("dp", "ctx", None),
        P("dp", "ctx", None),
        P("dp", "ctx"),
        P(("dp", "ctx"), None),
        P(("dp", "ctx"), None),
        P(("dp", "ctx"), None),
        P(("dp", "ctx")),
        P(),
        P(("dp", "ctx"), None),
        P(("dp", "ctx"), None),
        P(("dp", "ctx"), None),
        P(("dp", "ctx"), None),
        P(("dp", "ctx"), None),
        P(("dp", "ctx"), None),
        P(("dp", "ctx")),
        P(("dp", "ctx")),
        P(),
        P(),
    )
    return jax.shard_map(
        local,
        mesh=mesh,
        in_specs=placed,
        out_specs=(
            P("dp", "ctx", None),
            P("dp", "ctx", None),
            P(("dp", "ctx"), None),
            P(("dp", "ctx"), None),
            P(("dp", "ctx"), None),
            P(("dp", "ctx"), None),
            P(("dp", "ctx"), None),
            P(("dp", "ctx"), None),
            P(("dp", "ctx"), None),
            P(("dp", "ctx"), None),
            P(("dp", "ctx"), None),
            P(("dp", "ctx")),
            P(("dp", "ctx")),
            P(("dp", "ctx")),
            P(),
            P(),
            P(),
        ),
        check_vma=False,
    )
```

```python
import functools

import jax
import jax.numpy as jnp
from jax import lax
from jax.experimental import pallas as pl
from jax.experimental.pallas import tpu as pltpu
from jax.sharding import PartitionSpec as P

STEP = 10


EPSILON = 1e-05
BETA_ONE = 0.9
BETA_TWO = 0.95
ADAM_EPS = 1e-08
DECAY_RATE = 0.1
RATE_IN = 0.03
RATE_OUT = 0.02
RATE_CONV = 0.3
RATE_GAIN = 0.2
RATE_HEAD = 0.5
LOG2E = 1.4426950408889634
BELOW = -1e30
LANES = 128
VMEM_BYTES = 58 << 20
NT = (((1,), (1,)), ((), ()))
TN = (((0,), (0,)), ((), ()))


def shifted(value, axis, steps):
    count = lax.axis_size(axis)
    first, last = (max(0, -steps), min(count, count - steps))
    return lax.ppermute(value, axis, [(source, source + steps) for source in range(first, last)])


def bit_count(axis):
    return lax.axis_size(axis).bit_length() - 1


def swap(values, axis, bit):
    count = lax.axis_size(axis)
    return lax.ppermute(values, axis, [(place, place ^ (1 << bit)) for place in range(count)])


def sum_small(values, shared):
    dp_bits, ctx_bits = bit_count("dp"), bit_count("ctx")
    names = [("dp", bit) for bit in reversed(range(dp_bits))]
    names += [("ctx", bit) for bit in reversed(range(ctx_bits))]
    values = values.reshape((2,) * len(names) + (values.shape[1],))
    for axis, bit in list(names):
        dim = names.index((axis, bit))
        mine = (lax.axis_index(axis) >> bit) & 1
        kept = lax.dynamic_index_in_dim(values, mine, dim, keepdims=False)
        away = lax.dynamic_index_in_dim(values, 1 - mine, dim, keepdims=False)
        count = lax.axis_size(axis)
        away = lax.ppermute(
            jnp.concatenate([away.reshape(-1), shared]),
            axis,
            [(place, place ^ (1 << bit)) for place in range(count)],
        )
        values = kept + away[: kept.size].reshape(kept.shape)
        shared = shared + away[kept.size :]
        names.remove((axis, bit))
    return values, shared


def inverse_rms(values):
    return lax.rsqrt(jnp.mean(values * values, axis=-1, keepdims=True) + EPSILON)


def dot(left, right, dims=(((1,), (0,)), ((), ())), precision=None):
    return lax.dot_general(
        left, right, dims, precision=precision, preferred_element_type=jnp.float32
    )


def split_parts(values):
    high = values.astype(jnp.bfloat16)
    rest = values - high.astype(jnp.float32)
    middle = rest.astype(jnp.bfloat16)
    low = (rest - middle.astype(jnp.float32)).astype(jnp.bfloat16)
    return high, middle, low


def spread_heads(values, spread):
    high, middle, low = split_parts(values)
    return dot(high, spread) + dot(middle, spread) + dot(low, spread)


def sum_heads(values, spread):
    high, middle, low = split_parts(values)
    return dot(high, spread, NT) + dot(middle, spread, NT) + dot(low, spread, NT)


def causal(rows, columns):
    at_row = lax.broadcasted_iota(jnp.int32, (rows, columns), 0)
    at_column = lax.broadcasted_iota(jnp.int32, (rows, columns), 1)
    return at_row, at_column


def kernel_call(body, grid, in_specs, out_specs, out_shape, scratch=(), aliases=None):
    return pl.pallas_call(
        body,
        grid=grid,
        in_specs=in_specs,
        out_specs=out_specs,
        out_shape=out_shape,
        scratch_shapes=list(scratch),
        input_output_aliases=aliases or {},
        compiler_params=pltpu.CompilerParams(
            dimension_semantics=("arbitrary",) * len(grid), vmem_limit_bytes=VMEM_BYTES
        ),
    )


def per_row(*shape, first=0):
    return pl.BlockSpec((1,) + shape, lambda row, *_: (row + first,) + (0,) * len(shape))


def whole(*shape):
    return pl.BlockSpec(shape, lambda *_: (0,) * len(shape))


def untouched():
    return pl.BlockSpec(memory_space=pl.ANY)


def shape_of(shape, dtype):
    return jax.ShapeDtypeStruct(shape, dtype)


def entry_kernel(
    heads_count,
    x_ref,
    rim_ref,
    marks_ref,
    weight_ref,
    gain_ref,
    conv_ref,
    heads_ref,
    spread_ref,
    normed_ref,
    marks_out_ref,
    wide_out_ref,
    act_ref,
    raw_ref,
    step_ref,
    decay_ref,
    send_ref,
    wide_ref,
):
    length = x_ref.shape[1]
    inner, channels = spread_ref.shape[1], act_ref.shape[2]
    state = (channels - inner) // 2
    gain = gain_ref[0:1]
    marks = marks_ref[0].T
    marks_out_ref[0] = marks

    def normalize(values):
        values = values.astype(jnp.float32)
        scale = lax.rsqrt(jnp.mean(values * values, axis=-1, keepdims=True) + EPSILON)
        return (values * scale * gain).astype(jnp.bfloat16)

    normed = normalize(x_ref[0])
    normed_ref[0] = normed
    normed = jnp.concatenate([normalize(rim_ref[0]), normed], axis=0)
    part = 768 if channels % 768 == 0 else LANES
    for start in range(0, channels, part):
        piece = dot(normed, weight_ref[:, start : start + part]).astype(jnp.bfloat16)
        wide_ref[:, start : start + part] = piece[8:].astype(jnp.float32)
    raw = dot(normed, weight_ref[:, channels:])[16:]
    raw_ref[0] = raw

    same = [
        jnp.broadcast_to(marks[:, tap : tap + 1], (length, LANES)) for tap in range(3)
    ]

    def convolve(tile, carry):
        at = pl.ds(pl.multiple_of(tile * LANES, LANES), LANES)
        pre = jnp.broadcast_to(conv_ref[4:5, at], (length, LANES))
        for tap in range(3):
            taken = wide_ref[5 + tap : 5 + tap + length, at]
            pre = pre + conv_ref[tap : tap + 1, at] * taken * same[tap]
        pre = pre + conv_ref[3:4, at] * wide_ref[8:, at]
        act_ref[0, :, at] = (pre * jax.nn.sigmoid(pre)).astype(jnp.bfloat16)
        wide_out_ref[0, :, at] = jnp.concatenate(
            [jnp.zeros((8, LANES), jnp.float32), wide_ref[:, at]], axis=0
        ).astype(jnp.bfloat16)
        return carry

    lax.fori_loop(0, channels // LANES, convolve, 0)

    biased = raw + heads_ref[0:1]
    step = jnp.maximum(biased, 0.0) + jnp.log1p(jnp.exp(-jnp.abs(biased)))
    lane = lax.broadcasted_iota(jnp.int32, step.shape, 1)
    step = jnp.where(lane < heads_count, step, 0.0)
    step_ref[0] = step
    at_row, at_column = causal(length, length)
    lower = jnp.where(at_row >= at_column, 1.0, 0.0)
    decay = dot(lower, step * heads_ref[1:2], precision=lax.Precision.HIGHEST)
    decay_ref[0] = decay
    last = decay[length - 1 : length]
    end_weight = jnp.exp(last - decay) * marks[:, 4:5] * step
    spread = spread_ref[...]
    scaled = (spread_heads(end_weight, spread) * act_ref[0, :, :inner].astype(jnp.float32)).astype(
        jnp.bfloat16
    )
    states = dot(act_ref[0, :, inner : inner + state], scaled, TN)
    passing = jnp.exp(last) * marks[length - 1 : length, 3:4]
    passing = spread_heads(jnp.broadcast_to(passing, (8, LANES)), spread)
    groups, lanes = send_ref.shape[1], send_ref.shape[3]
    for group in range(groups):
        at = slice(group * lanes, (group + 1) * lanes)
        send_ref[0, group, :state] = states[:, at]
        send_ref[0, group, state:] = passing[:, at]


def pair_masks(pair_lanes, head_dim, rows):
    lane = lax.broadcasted_iota(jnp.int32, (rows, pair_lanes), 1)
    return [
        (lane >= member * head_dim) & (lane < (member + 1) * head_dim)
        for member in range(pair_lanes // head_dim)
    ]


def inner_forward_kernel(
    heads_count, act_ref, step_ref, decay_ref, marks_ref, segment_ref, y_ref
):
    length = act_ref.shape[1]
    inner = y_ref.shape[2]
    state = (act_ref.shape[2] - inner) // 2
    head_dim = inner // heads_count
    b_state = act_ref[0, :, inner : inner + state]
    c_state = act_ref[0, :, inner + state :]
    decay = decay_ref[0] * LOG2E
    lifted = (decay - jnp.log2(step_ref[0])).T
    at_row, at_column = causal(length, length)
    joined = (at_row >= at_column) & (marks_ref[0, :, 5:6] == segment_ref[0, 0:1])
    masked = jnp.where(joined, 0.0, BELOW)
    scores = dot(c_state, b_state, NT)
    chunk = max(length // 2, 16)
    masks = pair_masks(LANES, head_dim, length)
    for pair in range(inner // LANES):
        at = slice(pair * LANES, (pair + 1) * LANES)
        x_pair = act_ref[0, :, at]
        members = [jnp.where(mask, x_pair, jnp.zeros_like(x_pair)) for mask in masks]
        for start in range(0, length, chunk):
            rows, seen = slice(start, start + chunk), start + chunk
            total = jnp.zeros((chunk, LANES), jnp.float32)
            for member, x_member in enumerate(members):
                head = pair * len(masks) + member
                span = decay[rows, head : head + 1] - lifted[head : head + 1, :seen]
                mixing = scores[rows, :seen] * jnp.exp2(span + masked[rows, :seen])
                total = total + dot(mixing.astype(jnp.bfloat16), x_member[:seen])
            y_ref[0, rows, at] = total


def carry_forward_kernel(received_ref, held_ref, low_ref, incoming_ref, kept_ref):
    blocks, state = low_ref.shape[0], low_ref.shape[1]
    carried = jnp.zeros(low_ref.shape[1:], jnp.float32)
    for block in range(blocks):
        incoming_ref[block] = carried
        low_ref[block] = carried.astype(jnp.bfloat16)
        passing = received_ref[block, state : state + 1]
        carried = passing * carried + received_ref[block, :state]


def carry_backward_kernel(
    received_ref, passing_ref, incoming_ref, inner_ref, choice_ref, gate_ref, send_ref, *kept_refs
):
    blocks, state = received_ref.shape[0], received_ref.shape[1]
    carried = jnp.zeros(received_ref.shape[1:], jnp.float32)
    for block in reversed(range(blocks)):
        send_ref[block, :state] = carried.astype(jnp.bfloat16)
        total = jnp.sum(carried * incoming_ref[block], axis=0, keepdims=True)
        parts = [part.astype(jnp.float32) for part in split_parts(total)]
        parts.append(jnp.zeros((13,) + total.shape[1:], jnp.float32))
        send_ref[block, state:] = jnp.concatenate(parts, axis=0).astype(jnp.bfloat16)
        carried = passing_ref[block, 0:1] * carried + received_ref[block].astype(jnp.float32)


def join_groups(ref, rows):
    return jnp.concatenate([ref[0, group, rows] for group in range(ref.shape[1])], axis=1)


def middle_kernel(
    groups,
    cotangent_ref,
    normed_ref,
    gate_weight_ref,
    out_weight_ref,
    gain_ref,
    skip_ref,
    act_ref,
    y_ref,
    incoming_ref,
    decay_ref,
    marks_ref,
    spread_ref,
    mixed_ref,
    grad_gate_ref,
    grad_ssd_ref,
    send_ref,
    grad_c_ref,
    row_term_ref,
    grad_gain_ref,
    grad_skip_ref,
    total_ref,
):
    row, piece = pl.program_id(0), pl.program_id(1)
    inner = spread_ref.shape[1]
    state = total_ref.shape[0]
    spread = spread_ref[...]
    gain, skip = gain_ref[0:1], skip_ref[0:1]
    x_part = act_ref[0, :, :inner].astype(jnp.float32)
    c_state = act_ref[0, :, inner + state :]
    incoming = join_groups(incoming_ref, slice(None))
    entry = spread_heads(jnp.exp(decay_ref[0]) * marks_ref[0, :, 3:4], spread)
    inner_part = y_ref[0] + entry * dot(c_state, incoming)
    ssd = inner_part + skip * x_part
    gate = dot(normed_ref[0], gate_weight_ref[...])
    sigmoid = jax.nn.sigmoid(gate)
    silu = gate * sigmoid
    gated = ssd * silu
    scale = lax.rsqrt(jnp.mean(gated * gated, axis=-1, keepdims=True) + EPSILON)
    unit = gated * scale
    mixed_ref[0] = (unit * gain).astype(jnp.bfloat16)
    grad_mixed = dot(cotangent_ref[0], out_weight_ref[...], NT)
    grad_unit = grad_mixed * gain
    mean = jnp.mean(grad_unit * unit, axis=-1, keepdims=True)
    grad_gated = scale * (grad_unit - unit * mean)
    slope = sigmoid * (1.0 + gate * (1.0 - sigmoid))
    grad_gate_ref[0] = (grad_gated * ssd * slope).astype(jnp.bfloat16)
    grad_ssd = (grad_gated * silu).astype(jnp.bfloat16)
    grad_ssd_ref[0] = grad_ssd
    grad_ssd = grad_ssd.astype(jnp.float32)
    row_term_ref[0] = sum_heads(grad_ssd * inner_part, spread)
    grad_before = (grad_ssd * entry).astype(jnp.bfloat16)
    grad_c_ref[0] = dot(grad_before, incoming, NT)
    grad_states = dot(c_state, grad_before, TN)
    gain_sum = jnp.sum(grad_mixed * unit, axis=0, keepdims=True)
    skip_sum = jnp.sum(grad_ssd * x_part, axis=0, keepdims=True)

    @pl.when(piece == 0)
    def _():
        total_ref[...] = grad_states

    @pl.when(piece > 0)
    def _():
        total_ref[...] += grad_states

    @pl.when((piece == 0) & (row == 0))
    def _():
        grad_gain_ref[...] = jnp.zeros_like(grad_gain_ref)
        grad_skip_ref[...] = jnp.zeros_like(grad_skip_ref)

    grad_gain_ref[0:1] += gain_sum
    grad_skip_ref[0:1] += skip_sum
    lanes = inner // groups

    @pl.when(piece == pl.num_programs(1) - 1)
    def _():
        for group in range(groups):
            at = slice(group * lanes, (group + 1) * lanes)
            send_ref[0, group] = total_ref[:, at].astype(jnp.bfloat16)


def inner_backward_kernel(
    heads_count,
    act_ref,
    grad_ssd_ref,
    step_ref,
    decay_ref,
    marks_ref,
    segment_ref,
    grad_x_ref,
    grad_b_ref,
    grad_c_ref,
    total_ref,
):
    length = act_ref.shape[1]
    inner = grad_ssd_ref.shape[2]
    state = (act_ref.shape[2] - inner) // 2
    head_dim = inner // heads_count
    b_state = act_ref[0, :, inner : inner + state]
    c_state = act_ref[0, :, inner + state :]
    decay = decay_ref[0] * LOG2E
    lowered = jnp.log2(step_ref[0]) - decay
    decay = decay.T
    at_row, at_column = causal(length, length)
    joined = (at_row <= at_column) & (marks_ref[0, :, 5:6] == segment_ref[0, 0:1])
    masked = jnp.where(joined, 0.0, BELOW)
    scores = dot(b_state, c_state, NT)
    chunk = max(length // 2, 16)
    masks = pair_masks(LANES, head_dim, length)
    total_ref[...] = jnp.zeros_like(total_ref)
    for pair in range(inner // LANES):
        at = slice(pair * LANES, (pair + 1) * LANES)
        x_pair = act_ref[0, :, at]
        grad_pair = grad_ssd_ref[0, :, at]
        members = [jnp.where(mask, grad_pair, jnp.zeros_like(grad_pair)) for mask in masks]
        for start in range(0, length, chunk):
            rows, later = slice(start, start + chunk), slice(start, length)
            grad_x = jnp.zeros((chunk, LANES), jnp.float32)
            for member, grad_member in enumerate(members):
                head = pair * len(masks) + member
                span = decay[head : head + 1, later] + lowered[rows, head : head + 1]
                weight = jnp.exp2(span + masked[rows, later])
                mixing = (scores[rows, later] * weight).astype(jnp.bfloat16)
                grad_x = grad_x + dot(mixing, grad_member[later])
                total_ref[rows, later] += dot(x_pair[rows], grad_member[later], NT) * weight
            grad_x_ref[0, rows, at] = grad_x
    grad_scores = total_ref[...].astype(jnp.bfloat16)
    grad_b_ref[0] = dot(grad_scores, c_state)
    grad_c_ref[0] = dot(grad_scores, b_state, TN)


def share_kernel(widths, chosen_ref, left_ref, right_ref, *refs):
    outs = refs[-len(widths) :]
    start = 0
    for out_ref, width in zip(outs, widths):
        out_ref[0] = dot(left_ref[...], right_ref[:, start : start + width], TN)
        start += width


def share_of_product(left, right, chosen, widths, held=None):
    dp_count = lax.axis_size("dp")
    left = left.reshape(-1, left.shape[2])
    right = right.reshape(-1, right.shape[2])
    tokens, rows = left.shape[0], left.shape[1] // dp_count
    held = [] if held is None else [held]
    results = pl.pallas_call(
        functools.partial(share_kernel, widths),
        grid_spec=pltpu.PrefetchScalarGridSpec(
            num_scalar_prefetch=1,
            grid=(dp_count // 2,),
            in_specs=[
                pl.BlockSpec((tokens, rows), lambda y, chosen: (0, 2 * y + chosen[0])),
                pl.BlockSpec(right.shape, lambda y, chosen: (0, 0)),
            ]
            + [untouched()] * len(held),
            out_specs=[untouched()] * len(held)
            + [pl.BlockSpec((1, rows, width), lambda y, chosen: (y, 0, 0)) for width in widths],
        ),
        out_shape=[shape_of(item.shape, item.dtype) for item in held]
        + [shape_of((dp_count // 2, rows, width), jnp.float32) for width in widths],
        input_output_aliases={3: 0} if held else {},
        compiler_params=pltpu.CompilerParams(vmem_limit_bytes=VMEM_BYTES),
    )(chosen, left, right, *held)
    return results[len(held) :], results[0] if held else None


def share_parts(left, right, widths, choice, held=None):
    away, choice = share_of_product(left, right, choice[1:], widths, choice)
    away = [swap(piece, "dp", 0) for piece in away]
    kept, held = share_of_product(left, right, choice[:1], widths, held)
    return list(zip(kept, away)), held


class HalvedSum:
    def __init__(self, parts, y_first):
        dp_bits, ctx_bits = bit_count("dp"), bit_count("ctx")
        x_bits = dp_bits - 1
        self.names = [("dp", bit) for bit in reversed(range(1, dp_bits))]
        self.names += [("ctx", bit) for bit in reversed(range(ctx_bits))]
        split = (2,) * len(self.names)
        self.kept, self.arrived = (part.reshape(split + (-1, part.shape[2])) for part in parts)
        y_part = [("dp", bit) for bit in reversed(range(1, dp_bits))]
        x_part = [("ctx", bit) for bit in reversed(range(x_bits))]
        z_part = [("ctx", bit) for bit in range(x_bits, ctx_bits)]
        self.order = (y_part + x_part if y_first else x_part + y_part) + z_part

    def step(self):
        if not self.order:
            return
        axis, bit = self.order.pop(0)
        dim = self.names.index((axis, bit))
        self.names.remove((axis, bit))
        mine = (lax.axis_index(axis) >> bit) & 1

        def half(member):
            first, second = (
                lax.dynamic_index_in_dim(part, member, dim, keepdims=False)
                for part in (self.kept, self.arrived)
            )
            return first + second

        away = swap(half(1 - mine), axis, bit)
        self.kept, self.arrived = half(mine), away

    def finish(self):
        while self.order:
            self.step()
        return self.kept + self.arrived


def exit_kernel(held_count, *refs):
    ins, rest = refs[:17], refs[17:]
    outs, scratch = rest[-8 - held_count : -3 - held_count], rest[-3:]
    (
        act_ref,
        wide_ref,
        grad_ssd_ref,
        inner_x_ref,
        inner_b_ref,
        inner_c_ref,
        outer_c_ref,
        leaving_ref,
        row_term_ref,
        raw_ref,
        step_ref,
        decay_ref,
        marks_ref,
        conv_ref,
        heads_ref,
        skip_ref,
        spread_ref,
    ) = ins
    grad_mixer_ref, tail_ref, rim_ref, grad_conv_ref, grad_heads_ref = outs
    grad_act_ref, shift_ref, taken_ref = scratch
    row = pl.program_id(0)
    length, channels = act_ref.shape[1], act_ref.shape[2]
    inner = spread_ref.shape[1]
    state = (channels - inner) // 2
    spread = spread_ref[...]
    step, decay = step_ref[0], decay_ref[0]
    b_state = act_ref[0, :, inner : inner + state]
    leaving = join_groups(leaving_ref, slice(0, state))
    x_part = act_ref[0, :, :inner].astype(jnp.float32)
    last = decay[length - 1 : length]
    end_weight = spread_heads(jnp.exp(last - decay) * marks_ref[0, :, 4:5] * step, spread)
    scaled = (end_weight * x_part).astype(jnp.bfloat16)
    end_part = end_weight * dot(b_state, leaving)
    grad_x = inner_x_ref[0] + end_part
    grad_act_ref[:, :inner] = grad_x + skip_ref[0:1] * grad_ssd_ref[0].astype(jnp.float32)
    grad_act_ref[:, inner : inner + state] = inner_b_ref[0] + dot(scaled, leaving, NT)
    grad_act_ref[:, inner + state :] = inner_c_ref[0] + outer_c_ref[0]
    column_term = sum_heads(x_part * grad_x, spread)
    passed = join_groups(leaving_ref, slice(state, state + 16)).astype(jnp.float32)
    passed = jnp.sum(passed, axis=0, keepdims=True)
    ended = jnp.sum(x_part * end_part, axis=0, keepdims=True)
    ends = sum_heads(jnp.concatenate([passed, ended, jnp.zeros((6, inner), jnp.float32)], 0), spread)
    passing = jnp.exp(last) * marks_ref[0, length - 1 : length, 3:4]
    final = ends[1:2] + ends[0:1] * passing
    at_row, at_column = causal(length, length)
    token = lax.broadcasted_iota(jnp.int32, step.shape, 0)
    grad_decay = row_term_ref[0] - column_term + jnp.where(token == length - 1, final, 0.0)
    upper = jnp.where(at_row <= at_column, 1.0, 0.0)
    grad_later = dot(upper, grad_decay, precision=lax.Precision.HIGHEST)
    rate = heads_ref[1:2]
    grad_step = jnp.where(step > 0.0, column_term / jnp.where(step > 0.0, step, 1.0), 0.0)
    grad_step = grad_step + rate * grad_later
    grad_raw = grad_step * jax.nn.sigmoid(raw_ref[0] + heads_ref[0:1])
    grad_raw = jnp.where(step > 0.0, grad_raw, 0.0)
    grad_mixer_ref[0, :, channels:] = grad_raw.astype(jnp.bfloat16)

    @pl.when(row == 0)
    def _():
        grad_conv_ref[...] = jnp.zeros_like(grad_conv_ref)
        grad_heads_ref[...] = jnp.zeros_like(grad_heads_ref)

    grad_heads_ref[0:1] += jnp.sum(grad_later * step, axis=0, keepdims=True) * rate
    grad_heads_ref[1:2] += jnp.sum(grad_raw, axis=0, keepdims=True)

    same = [
        jnp.broadcast_to(marks_ref[0, :, tap : tap + 1], (length, LANES)) for tap in range(3)
    ]
    shift_ref[0:8] = jnp.zeros((8, LANES), jnp.float32)
    shift_ref[length + 8 :] = jnp.zeros((8, LANES), jnp.float32)

    def convolve(tile, carry):
        at = pl.ds(pl.multiple_of(tile * LANES, LANES), LANES)
        taken_ref[...] = wide_ref[0, :, at].astype(jnp.float32)
        pre = jnp.broadcast_to(conv_ref[4:5, at], (length, LANES))
        for tap in range(3):
            taken = taken_ref[13 + tap : 13 + tap + length]
            pre = pre + conv_ref[tap : tap + 1, at] * taken * same[tap]
        pre = pre + conv_ref[3:4, at] * taken_ref[16:]
        sigmoid = jax.nn.sigmoid(pre)
        grad_pre = grad_act_ref[:, at] * (sigmoid * (1.0 + pre * (1.0 - sigmoid)))
        grad_conv_ref[4:5, at] += jnp.sum(grad_pre, axis=0, keepdims=True)
        grad_conv_ref[3:4, at] += jnp.sum(grad_pre * taken_ref[16:], axis=0, keepdims=True)
        grad_in = grad_pre * conv_ref[3:4, at]
        rim = jnp.zeros((8, LANES), jnp.float32)
        for tap in range(3):
            masked = grad_pre * same[tap]
            taken = taken_ref[13 + tap : 13 + tap + length]
            grad_conv_ref[tap : tap + 1, at] += jnp.sum(masked * taken, axis=0, keepdims=True)
            shift_ref[8 : length + 8] = masked * conv_ref[tap : tap + 1, at]
            grad_in = grad_in + shift_ref[11 - tap : 11 - tap + length]
            rim = rim + shift_ref[8 - tap : 16 - tap]
        grad_mixer_ref[0, :, at] = grad_in.astype(jnp.bfloat16)
        tail_ref[0, :, at] = grad_in[length - 8 :]
        rim_ref[0, :, at] = rim
        return carry

    lax.fori_loop(0, channels // LANES, convolve, 0)


def adamw(weight, gradient, first_moment, second_moment, step_rate):
    first_new = BETA_ONE * first_moment + (1.0 - BETA_ONE) * gradient
    second_new = BETA_TWO * second_moment + (1.0 - BETA_TWO) * gradient * gradient
    corrected = first_new / (1.0 - BETA_ONE**STEP)
    spread = jnp.sqrt(second_new / (1.0 - BETA_TWO**STEP))
    weight_new = weight - step_rate * (corrected / (spread + ADAM_EPS) + DECAY_RATE * weight)
    return (first_new, second_new, weight_new)


def local(
    tokens,
    cotangent,
    segments,
    w_in,
    w_out,
    conv,
    gains,
    heads,
    in_first,
    in_second,
    out_first,
    out_second,
    conv_first,
    conv_second,
    gain_first,
    gain_second,
    head_first,
    head_second,
):
    devices = lax.axis_size(("dp", "ctx"))
    ctx_count = lax.axis_size("ctx")
    inner_width = w_out.shape[0] * devices
    own_rows, projected_width = w_in.shape
    seq_count, length, model_width = tokens.shape
    channels, taps = conv.shape[0] * devices, conv.shape[1] - 1
    state_dim = (channels - inner_width) // 2
    heads_count = heads.shape[1]
    head_dim = inner_width // heads_count
    mixer_width = projected_width - inner_width
    spare = -mixer_width % LANES
    wide_width = mixer_width + spare
    groups = ctx_count // seq_count
    lanes = inner_width // groups
    f32, bf16 = jnp.float32, jnp.bfloat16

    small = jnp.concatenate([conv.reshape(-1), gains])
    small = jnp.pad(small, (0, own_rows * spare - small.shape[0])).reshape(own_rows, spare)
    first_send = jnp.concatenate([w_in[:, inner_width:], small], axis=1).astype(bf16)
    mixer_weight = lax.all_gather(first_send, ("dp", "ctx"), axis=0, tiled=True)
    second_send = jnp.concatenate([w_in[:, :inner_width], w_out.reshape(own_rows, -1)], axis=1)
    mixer_weight, second_send = lax.optimization_barrier(
        (mixer_weight, second_send.astype(bf16))
    )
    second_weights = lax.all_gather(second_send, ("dp", "ctx"), axis=0, tiled=True)
    gate_weight = second_weights[:, :inner_width]
    output_weight = second_weights[:, inner_width:].reshape(inner_width, model_width)
    small = mixer_weight[:, mixer_width:].reshape(devices, own_rows * spare)
    conv_rows = small[:, : conv.size].reshape(channels, taps + 1).astype(f32).T
    conv_rows = jnp.pad(conv_rows, ((0, 7 - taps), (0, 0)))
    gain_vector = small[:, conv.size : conv.size + gains.size].reshape(-1).astype(f32)
    gain_in, gain_out = gain_vector[:model_width], gain_vector[model_width:]

    rim_send = tokens[:, length - 16 :]
    tail_segments = segments[:, None, length - 16 :].astype(bf16)
    rim_send = rim_send.at[:, :1, :16].set(tail_segments)
    rim_x = shifted(rim_send, "ctx", 1)
    rim_segment = rim_x[:, 0, :16].astype(jnp.int32)
    rim_segment = jnp.where(lax.axis_index("ctx") == 0, -1, rim_segment)
    wide_segment = jnp.concatenate([rim_segment, segments], axis=1)
    marks = [wide_segment[:, 13 + tap : 13 + tap + length] == segments for tap in range(3)]
    marks.append(segments == rim_segment[:, 15:])
    marks.append(segments == segments[:, length - 1 :])
    marks = [mark.astype(f32) for mark in marks] + [segments.astype(f32)]
    marks = jnp.stack(marks + [jnp.zeros_like(marks[0])] * 2, axis=1)
    segment_rows = jnp.broadcast_to(segments.astype(f32)[:, None], (seq_count, 8, length))
    head_rows = jnp.stack([heads[2], -jnp.exp(heads[0])])
    head_rows = jnp.pad(head_rows, ((0, 6), (0, LANES - heads_count)))
    skip_row = jnp.broadcast_to(jnp.repeat(heads[1], head_dim), (8, inner_width))
    lane_head = lax.broadcasted_iota(jnp.int32, (LANES, inner_width), 1) // head_dim
    spread = lane_head == lax.broadcasted_iota(jnp.int32, (LANES, inner_width), 0)
    spread = spread.astype(bf16)
    gain_rows = jnp.broadcast_to(gain_in, (8, model_width))
    gate_rows = jnp.broadcast_to(gain_out, (8, inner_width))

    normed, marks, wide_in, activated, step_raw, step_size, decay_sum, sent = kernel_call(
        functools.partial(entry_kernel, heads_count),
        (seq_count,),
        [
            per_row(length, model_width),
            per_row(16, model_width),
            per_row(8, length),
            whole(model_width, wide_width),
            whole(8, model_width),
            whole(8, channels),
            whole(8, LANES),
            whole(LANES, inner_width),
        ],
        [
            per_row(length, model_width),
            per_row(length, 8),
            per_row(length + 16, channels),
            per_row(length, channels),
            per_row(length, LANES),
            per_row(length, LANES),
            per_row(length, LANES),
            per_row(groups, state_dim + 8, lanes),
        ],
        [
            shape_of((seq_count, length, model_width), bf16),
            shape_of((seq_count, length, 8), f32),
            shape_of((seq_count, length + 16, channels), bf16),
            shape_of((seq_count, length, channels), bf16),
            shape_of((seq_count, length, LANES), f32),
            shape_of((seq_count, length, LANES), f32),
            shape_of((seq_count, length, LANES), f32),
            shape_of((seq_count, groups, state_dim + 8, lanes), f32),
        ],
        [pltpu.VMEM((length + 8, channels), f32)],
    )(tokens, rim_x, marks, mixer_weight, gain_rows, conv_rows, head_rows, spread)

    received = lax.all_to_all(
        sent.reshape(ctx_count, state_dim + 8, lanes), "ctx", 0, 0, tiled=True
    )
    within = kernel_call(
        functools.partial(inner_forward_kernel, heads_count),
        (seq_count,),
        [
            per_row(length, channels),
            per_row(length, LANES),
            per_row(length, LANES),
            per_row(length, 8),
            per_row(8, length),
        ],
        per_row(length, inner_width),
        shape_of((seq_count, length, inner_width), f32),
    )(activated, step_size, decay_sum, marks, segment_rows)
    tile = min(lanes, 2 * LANES)
    by_lane = lambda rows: pl.BlockSpec((ctx_count, rows, tile), lambda place: (0, 0, place))
    incoming_low, incoming, within = kernel_call(
        carry_forward_kernel,
        (lanes // tile,),
        [by_lane(state_dim + 8), untouched()],
        [by_lane(state_dim), by_lane(state_dim), untouched()],
        [
            shape_of((ctx_count, state_dim, lanes), bf16),
            shape_of((ctx_count, state_dim, lanes), f32),
            shape_of(within.shape, f32),
        ],
        aliases={1: 2},
    )(received, within)
    incoming_low = lax.all_to_all(incoming_low, "ctx", 0, 0, tiled=True)
    incoming_low = incoming_low.reshape(seq_count, groups, state_dim, lanes)

    half = min(length, 128)
    by_piece = lambda columns: pl.BlockSpec((1, half, columns), lambda row, piece: (row, piece, 0))
    mixed, grad_gate, grad_ssd, sent, outer_c, row_term, grad_gain_out, grad_skip = kernel_call(
        functools.partial(middle_kernel, groups),
        (seq_count, length // half),
        [
            by_piece(model_width),
            by_piece(model_width),
            whole(model_width, inner_width),
            whole(inner_width, model_width),
            whole(8, inner_width),
            whole(8, inner_width),
            by_piece(channels),
            by_piece(inner_width),
            per_row(groups, state_dim, lanes),
            by_piece(LANES),
            by_piece(8),
            whole(LANES, inner_width),
        ],
        [
            by_piece(inner_width),
            by_piece(inner_width),
            by_piece(inner_width),
            per_row(groups, state_dim, lanes),
            by_piece(state_dim),
            by_piece(LANES),
            whole(8, inner_width),
            whole(8, inner_width),
        ],
        [
            shape_of((seq_count, length, inner_width), bf16),
            shape_of((seq_count, length, inner_width), bf16),
            shape_of((seq_count, length, inner_width), bf16),
            shape_of((seq_count, groups, state_dim, lanes), bf16),
            shape_of((seq_count, length, state_dim), f32),
            shape_of((seq_count, length, LANES), f32),
            shape_of((8, inner_width), f32),
            shape_of((8, inner_width), f32),
        ],
        [pltpu.VMEM((state_dim, inner_width), f32)],
    )(
        cotangent,
        normed,
        gate_weight,
        output_weight,
        gate_rows,
        skip_row,
        activated,
        within,
        incoming_low,
        decay_sum,
        marks,
        spread,
    )
    grad_received = lax.all_to_all(
        sent.reshape(ctx_count, state_dim, lanes), "ctx", 0, 0, tiled=True
    )
    inner_x, inner_b, inner_c = kernel_call(
        functools.partial(inner_backward_kernel, heads_count),
        (seq_count,),
        [
            per_row(length, channels),
            per_row(length, inner_width),
            per_row(length, LANES),
            per_row(length, LANES),
            per_row(length, 8),
            per_row(8, length),
        ],
        [per_row(length, inner_width), per_row(length, state_dim), per_row(length, state_dim)],
        [
            shape_of((seq_count, length, inner_width), f32),
            shape_of((seq_count, length, state_dim), f32),
            shape_of((seq_count, length, state_dim), f32),
        ],
        [pltpu.VMEM((length, length), f32)],
    )(activated, grad_ssd, step_size, decay_sum, marks, segment_rows)
    gate_normed = jnp.einsum("hou,qu->hoq", grad_gate, gate_weight, preferred_element_type=f32)
    mine = lax.axis_index("dp") & 1
    choice = jnp.stack([mine, 1 - mine]).astype(jnp.int32)
    sent, inner_x, choice, gate_normed = kernel_call(
        carry_backward_kernel,
        (lanes // tile,),
        [
            by_lane(state_dim),
            pl.BlockSpec((ctx_count, 8, tile), lambda place: (0, state_dim // 8, place)),
            by_lane(state_dim),
            untouched(),
            untouched(),
            untouched(),
        ],
        [by_lane(state_dim + 16), untouched(), untouched(), untouched()],
        [
            shape_of((ctx_count, state_dim + 16, lanes), bf16),
            shape_of(inner_x.shape, f32),
            shape_of(choice.shape, jnp.int32),
            shape_of(gate_normed.shape, f32),
        ],
        aliases={3: 1, 4: 2, 5: 3},
    )(grad_received, received, incoming, inner_x, choice, gate_normed)
    leaving = lax.all_to_all(sent, "ctx", 0, 0, tiled=True)
    leaving = leaving.reshape(seq_count, groups, state_dim + 16, lanes)

    input_float = tokens.astype(f32)
    output = (
        input_float
        + jnp.dot(
            mixed.reshape(-1, inner_width), output_weight, preferred_element_type=f32
        ).reshape(tokens.shape)
    ).astype(bf16)
    gate_parts, _ = share_parts(normed, grad_gate, [inner_width], choice)
    out_parts, _ = share_parts(mixed, cotangent, [model_width], choice)
    first_sums = [HalvedSum(gate_parts[0], True), HalvedSum(out_parts[0], False)]
    for item in first_sums:
        item.step()

    def exit_rows(first, count, held, previous):
        at_row = functools.partial(per_row, first=first)
        shapes = [
            shape_of((seq_count, length, wide_width), bf16),
            shape_of((seq_count, 8, channels), f32),
            shape_of((seq_count, 8, channels), f32),
            shape_of((8, channels), f32),
            shape_of((8, LANES), f32),
        ]
        aliases = {17 + place: place for place in range(len(previous))}
        aliases.update(
            {17 + len(previous) + place: 5 + place for place in range(len(held))}
        )
        return kernel_call(
            functools.partial(exit_kernel, len(held)),
            (count,),
            [
                at_row(length, channels),
                at_row(length + 16, channels),
                at_row(length, inner_width),
                at_row(length, inner_width),
                at_row(length, state_dim),
                at_row(length, state_dim),
                at_row(length, state_dim),
                at_row(groups, state_dim + 16, lanes),
                at_row(length, LANES),
                at_row(length, LANES),
                at_row(length, LANES),
                at_row(length, LANES),
                at_row(length, 8),
                whole(8, channels),
                whole(8, LANES),
                whole(8, inner_width),
                whole(LANES, inner_width),
            ]
            + [untouched()] * (len(previous) + len(held)),
            [
                at_row(length, wide_width),
                at_row(8, channels),
                at_row(8, channels),
                whole(8, channels),
                whole(8, LANES),
            ]
            + [untouched()] * len(held),
            shapes + [shape_of(item.shape, item.dtype) for item in held],
            [
                pltpu.VMEM((length, channels), f32),
                pltpu.VMEM((length + 16, LANES), f32),
                pltpu.VMEM((length + 16, LANES), f32),
            ],
            aliases=aliases,
        )(
            activated,
            wide_in,
            grad_ssd,
            inner_x,
            inner_b,
            inner_c,
            outer_c,
            leaving,
            row_term,
            step_raw,
            step_size,
            decay_sum,
            marks,
            conv_rows,
            head_rows,
            skip_row,
            spread,
            *previous,
            *held,
        )

    held = [item.kept for item in first_sums] + [gate_normed, output]
    *previous, first_conv, first_heads, kept_gate, kept_out, gate_normed, output = exit_rows(
        0, seq_count // 2, held, []
    )
    for item, kept in zip(first_sums, (kept_gate, kept_out)):
        item.kept = kept
        item.step()
    grad_mixer, tail, rim, grad_conv, grad_heads, kept_gate, kept_out = exit_rows(
        seq_count // 2, seq_count - seq_count // 2, [item.kept for item in first_sums], previous
    )
    for item, kept in zip(first_sums, (kept_gate, kept_out)):
        item.kept = kept
        item.step()
    grad_conv, grad_heads = grad_conv + first_conv, grad_heads + first_heads
    rim_back = shifted(rim[:, : taps - 1].astype(bf16), "ctx", -1).astype(f32)
    tail = tail.at[:, 9 - taps :].add(rim_back).astype(bf16)
    grad_mixer = grad_mixer.at[:, length - 8 :, :channels].set(tail)
    middle = wide_width // 256 * 128
    (left_parts, right_parts), mixer_weight = share_parts(
        normed, grad_mixer, [middle, wide_width - middle], choice, mixer_weight
    )
    left_sum, right_sum = HalvedSum(left_parts, True), HalvedSum(right_parts, False)
    gate_sum, out_sum, left_sum, right_sum = (
        item.finish() for item in (*first_sums, left_sum, right_sum)
    )
    grad_normed = gate_normed + jnp.einsum(
        "hou,qu->hoq", grad_mixer, mixer_weight, preferred_element_type=f32
    )
    scale_in = inverse_rms(input_float)
    unit_in = input_float * scale_in
    grad_gain_in = jnp.sum(grad_normed * unit_in, axis=(0, 1))
    grad_unit_in = grad_normed * gain_in
    grad_tokens = cotangent.astype(f32) + scale_in * (
        grad_unit_in - unit_in * jnp.mean(grad_unit_in * unit_in, axis=-1, keepdims=True)
    )
    grad_conv = grad_conv[: taps + 1].T
    grad_gains = jnp.concatenate([grad_gain_in, grad_gain_out[0]])
    grad_skip = jnp.sum(grad_skip[0].reshape(heads_count, head_dim), axis=1)
    grad_heads = jnp.concatenate(
        [grad_heads[0, :heads_count], grad_skip, grad_heads[1, :heads_count]]
    )
    small_sum, head_grad = sum_small(
        jnp.concatenate(
            [grad_conv.reshape(devices, -1), grad_gains.reshape(devices, -1)], axis=1
        ),
        grad_heads,
    )
    owned_grads = (
        jnp.concatenate([gate_sum, left_sum, right_sum], axis=1)[:, :projected_width],
        out_sum.reshape(w_out.shape),
        small_sum[: conv.size].reshape(conv.shape),
        small_sum[conv.size :],
    )
    head_grad = head_grad.reshape(heads.shape)
    in_new = adamw(w_in, owned_grads[0], in_first, in_second, RATE_IN)
    out_new = adamw(w_out, owned_grads[1], out_first, out_second, RATE_OUT)
    conv_new = adamw(conv, owned_grads[2], conv_first, conv_second, RATE_CONV)
    gain_new = adamw(gains, owned_grads[3], gain_first, gain_second, RATE_GAIN)
    head_new = adamw(heads, head_grad, head_first, head_second, RATE_HEAD)
    return (
        output,
        grad_tokens,
        in_new[0],
        in_new[1],
        in_new[2],
        out_new[0],
        out_new[1],
        out_new[2],
        conv_new[0],
        conv_new[1],
        conv_new[2],
        gain_new[0],
        gain_new[1],
        gain_new[2],
        head_new[0],
        head_new[1],
        head_new[2],
    )


def solution(mesh):
    placed = (
        P("dp", "ctx", None),
        P("dp", "ctx", None),
        P("dp", "ctx"),
        P(("dp", "ctx"), None),
        P(("dp", "ctx"), None),
        P(("dp", "ctx"), None),
        P(("dp", "ctx")),
        P(),
        P(("dp", "ctx"), None),
        P(("dp", "ctx"), None),
        P(("dp", "ctx"), None),
        P(("dp", "ctx"), None),
        P(("dp", "ctx"), None),
        P(("dp", "ctx"), None),
        P(("dp", "ctx")),
        P(("dp", "ctx")),
        P(),
        P(),
    )
    return jax.shard_map(
        local,
        mesh=mesh,
        in_specs=placed,
        out_specs=(
            P("dp", "ctx", None),
            P("dp", "ctx", None),
            P(("dp", "ctx"), None),
            P(("dp", "ctx"), None),
            P(("dp", "ctx"), None),
            P(("dp", "ctx"), None),
            P(("dp", "ctx"), None),
            P(("dp", "ctx"), None),
            P(("dp", "ctx"), None),
            P(("dp", "ctx"), None),
            P(("dp", "ctx"), None),
            P(("dp", "ctx")),
            P(("dp", "ctx")),
            P(("dp", "ctx")),
            P(),
            P(),
            P(),
        ),
        check_vma=False,
    )
```
